32 devices in a mesh: batch: 4 (over y, x), ch: 8 (over z, core).
Axes of the slice: x: 2, y: 2, z: 4, core: 2. Of those that a mesh axis runs over, the one named last changes fastest.
Arguments:
- earlier: bfloat16 [4, 3840, 512], P('batch', 'ch'), may hold values from -6 to 6
- lengths: int32 [4], P('batch'), may hold values from 128 to 512, as said below
- lower_entry: bfloat16 [25, 768, 640], P(None, 'ch'), may hold values from -0.046875 to 0.046875
- lower_convs: bfloat16 [1, 25, 768, 768], P(None, None, 'ch'), may hold values from -0.046875 to 0.046875
- upper_convs: bfloat16 [2, 25, 768, 768], P(None, None, 'ch'), may hold values from -0.046875 to 0.046875
- lower_dense: bfloat16 [768, 3840], P('ch'), may hold values from -0.09375 to 0.09375
- upper_dense: bfloat16 [768, 4608], P('ch'), may hold values from -0.09375 to 0.09375
- lower_gain: float32 [11, 768], P(None, 'ch'), may hold values from 0.25 to 1.75
- lower_shift: float32 [11, 768], P(None, 'ch'), may hold values from -2 to 2
- upper_gain: float32 [12, 768], P(None, 'ch'), may hold values from 0.25 to 1.75
- upper_shift: float32 [12, 768], P(None, 'ch'), may hold values from -2 to 2
- cotangent: bfloat16 [4, 768, 512], P('batch', 'ch'), may hold values from -6 to 6
Outputs:
- final: bfloat16 [4, 768, 512], P('batch', 'ch')
- earlier_grad: float32 [4, 3840, 512], P('batch', 'ch')
- lower_entry_grad: float32 [25, 768, 640], P(None, 'ch', 'batch')
- lower_convs_grad: float32 [1, 25, 768, 768], P(None, None, 'ch', 'batch')
- upper_convs_grad: float32 [2, 25, 768, 768], P(None, None, 'ch', 'batch')
- lower_dense_grad: float32 [768, 3840], P('ch', 'batch')
- upper_dense_grad: float32 [768, 4608], P('ch', 'batch')
- lower_gain_grad: float32 [11, 768], P(None, 'ch')
- lower_shift_grad: float32 [11, 768], P(None, 'ch')
- upper_gain_grad: float32 [12, 768], P(None, 'ch')
- upper_shift_grad: float32 [12, 768], P(None, 'ch')
The draws below stay inside these ranges and needn't reach their ends.
Inputs may be any that keep to these rules, and one draw needn't show every extreme that they name: `lengths`: one utterance has exactly 512 frames; the others have at least 128.
All inputs are finite; a program needn't handle non-finite values.
Results may differ from the reference program's by a relative error of at most 0.025.
Values may be sent and summed in bfloat16 or wider, within the bound.
A program may use at most 192 MiB of HBM per device.

```python
import jax
import jax.numpy as jnp
from jax import lax

BASE = 128
KERNEL = 25
SUBS = 2
SOURCES = 9
FRAMES = 512
WIDE = 768
PRE = 640
EARLIER = 3840
UTTS = 4


def draw_lengths(key, part):
    key = jax.random.fold_in(key, 11)
    first_key, second_key = jax.random.split(key)
    drawn = jax.random.randint(first_key, (UTTS,), FRAMES // 4, FRAMES + 1)
    chosen = jax.random.randint(second_key, (), 0, UTTS)
    return jnp.where(jnp.arange(UTTS) == chosen, FRAMES, drawn).astype(jnp.int32)


def block_levels(own_key, extent, pieces, least, top_value):
    factor_of = 1.0
    for axis_at, parts in pieces:
        heights = jax.random.uniform(jax.random.fold_in(jax.random.fold_in(own_key, 6), axis_at), (parts,), jnp.float32, least / len(pieces), top_value / len(pieces))
        factor_of = factor_of * jnp.repeat(jnp.exp(heights), extent[axis_at] // parts).reshape((-1,) + (1,) * (len(extent) - 1 - axis_at))
    return factor_of


def gaussian(own_key, extent, deviation, most, cuts=(), kind=jnp.bfloat16):
    values = jax.random.normal(own_key, extent, jnp.float32) * deviation
    if len(cuts) > 0:
        values = block_levels(own_key, extent, cuts, -0.22, 0.18) * values
    return jnp.clip(values, min=-most, max=most).astype(kind)


def setup_inputs(seed: int = 0) -> dict:
    splits = jax.random.split(jax.random.key(seed), 13)
    return {
        "earlier": gaussian(splits[0], (UTTS, EARLIER, FRAMES), 1.0, 6.0, ((0, 4), (1, 8))),
        "lengths": draw_lengths(jax.random.fold_in(splits[12], 71), 0),
        "lower_entry": gaussian(splits[2], (KERNEL, WIDE, PRE), (KERNEL * PRE) ** -0.5, 0.046875, ((1, 8),)),
        "lower_convs": gaussian(splits[3], (SUBS - 1, KERNEL, WIDE, WIDE), (KERNEL * WIDE) ** -0.5, 0.046875, ((2, 8),)),
        "upper_convs": gaussian(splits[4], (SUBS, KERNEL, WIDE, WIDE), (KERNEL * WIDE) ** -0.5, 0.046875, ((2, 8),)),
        "lower_dense": gaussian(splits[5], (WIDE, EARLIER), EARLIER ** -0.5, 0.09375, ((0, 8),)),
        "upper_dense": gaussian(splits[6], (WIDE, EARLIER + WIDE), (EARLIER + WIDE) ** -0.5, 0.09375, ((0, 8),)),
        "lower_gain": jnp.clip(1.0 + 0.15 * jax.random.normal(splits[7], (SUBS + SOURCES, WIDE), jnp.float32), 0.25, 1.75),
        "lower_shift": gaussian(splits[8], (SUBS + SOURCES, WIDE), 0.5, 2.0, ((1, 8),), jnp.float32),
        "upper_gain": jnp.clip(1.0 + 0.15 * jax.random.normal(splits[9], (SUBS + SOURCES + 1, WIDE), jnp.float32), 0.25, 1.75),
        "upper_shift": gaussian(splits[10], (SUBS + SOURCES + 1, WIDE), 0.5, 2.0, ((1, 8),), jnp.float32),
        "cotangent": gaussian(splits[11], (UTTS, WIDE, FRAMES), 1.0, 6.0, ((0, 4), (1, 8))),
    }


epsilon = 0.001
unit_widths = (2, 2, 2, 3, 3, 4, 4, 5, 5)

@jax.custom_vjp
def low(v):
    return lax.optimization_barrier(v.astype(jnp.bfloat16)).astype(jnp.float32)

@jax.custom_vjp
def low_back(v):
    return v

def low_keep(v):
    return (low(v), None)

def low_pass(kept, grad):
    return (grad,)

def back_keep(v):
    return (v, None)

def back_low(kept, grad):
    return (low(grad),)
low.defvjp(low_keep, low_pass)
low_back.defvjp(back_keep, back_low)

def conv_apply(weight, inputs):
    kernel_taps = weight.shape[0]
    before = (kernel_taps - 1) // 2
    return lax.conv_general_dilated(inputs, weight, (1,), [(before, kernel_taps - 1 - before)], dimension_numbers=('NCH', 'HOI', 'NCH'), precision=lax.Precision.HIGHEST)

def normalize(values, validity, frame_count, gain_row, shift_row):
    average = lax.optimization_barrier(jnp.sum(values * validity, axis=(0, 2))) / frame_count
    second = lax.optimization_barrier(jnp.sum(values * values * validity, axis=(0, 2))) / frame_count
    scaling = lax.rsqrt(second - average * average + epsilon)
    return (values - average[:, None]) * scaling[:, None] * gain_row[:, None] + shift_row[:, None]

def run_block(entry_input, conv_list, dense_weight, source_pieces, gain_rows, shift_rows, validity, frame_count):
    subs = len(conv_list)
    current = entry_input
    for sub_index in range(subs):
        if sub_index > 0:
            current = low(jax.nn.silu(current) * validity)
        current = normalize(low_back(conv_apply(conv_list[sub_index], current)), validity, frame_count, gain_rows[sub_index], shift_rows[sub_index])
    offset = 0
    for source_index, source_piece in enumerate(source_pieces):
        channels = source_piece.shape[1]
        branch = jnp.einsum('oi,uit->uot', dense_weight[:, offset:offset + channels], source_piece, precision=lax.Precision.HIGHEST)
        current = current + normalize(low_back(branch), validity, frame_count, gain_rows[subs + source_index], shift_rows[subs + source_index])
        offset = offset + channels
    return jax.nn.silu(current) * validity

def reference(earlier, lengths, lower_entry, lower_convs, upper_convs, lower_dense, upper_dense, lower_gain, lower_shift, upper_gain, upper_shift, cotangent):
    validity = (jnp.arange(FRAMES).astype(jnp.int32)[None, :] < lengths[:, None]).astype(jnp.float32)[:, None, :]
    frame_count = jnp.sum(lengths).astype(jnp.float32)
    widths = [factor * BASE for factor in unit_widths]

    def forward(earlier_f, entry_f, lower_f, upper_f, lower_dense_f, upper_dense_f, lower_gain_f, lower_shift_f, upper_gain_f, upper_shift_f):
        sources = low(earlier_f * validity)
        source_pieces = []
        offset = 0
        for channels in widths:
            source_pieces.append(sources[:, offset:offset + channels])
            offset = offset + channels
        lower_list = [entry_f] + [lower_f[sub_index] for sub_index in range(SUBS - 1)]
        middle = low(run_block(source_pieces[-1], lower_list, lower_dense_f, source_pieces, lower_gain_f, lower_shift_f, validity, frame_count))
        upper_list = [upper_f[sub_index] for sub_index in range(SUBS)]
        return run_block(middle, upper_list, upper_dense_f, source_pieces + [middle], upper_gain_f, upper_shift_f, validity, frame_count)
    result, pullback = jax.vjp(forward, earlier.astype(jnp.float32), lower_entry.astype(jnp.float32), lower_convs.astype(jnp.float32), upper_convs.astype(jnp.float32), lower_dense.astype(jnp.float32), upper_dense.astype(jnp.float32), lower_gain.astype(jnp.float32), lower_shift.astype(jnp.float32), upper_gain.astype(jnp.float32), upper_shift.astype(jnp.float32))
    gradients = pullback(cotangent.astype(jnp.float32))
    return (result.astype(jnp.bfloat16), gradients[0], gradients[1], gradients[2], gradients[3], gradients[4], gradients[5], gradients[6], gradients[7], gradients[8], gradients[9])
```

```python
import functools
import math

import jax
import jax.numpy as jnp
from jax import lax
from jax.experimental import pallas as pl
from jax.experimental.pallas import tpu as pltpu
from jax.sharding import PartitionSpec as P

EPS = 0.001
WIDTHS = (2, 2, 2, 3, 3, 4, 4, 5, 5)
MESH = pl.DeviceIdType.MESH
F32 = jnp.float32
BF16 = jnp.bfloat16
RB = 16
LANES = 128


def shifted(x, by):
    if by == 0:
        return x
    frames = x.shape[1]
    lane = lax.broadcasted_iota(jnp.int32, x.shape, 1)
    rolled = pltpu.roll(x, (-by) % frames, 1)
    keep = (lane < frames - by) if by > 0 else (lane >= -by)
    return jnp.where(keep, rolled, jnp.zeros_like(rolled))


def squash(v):
    return 0.5 * jnp.tanh(0.5 * v) + 0.5


def dot(a, b):
    return jnp.dot(a, b, preferred_element_type=F32)


def dot_first(a, b):
    return lax.dot_general(a, b, (((0,), (0,)), ((), ())), preferred_element_type=F32)


def dot_last(a, b):
    return lax.dot_general(a, b, (((1,), (1,)), ((), ())), preferred_element_type=F32)


class Plan:
    def __init__(self, nb, nc, own, frames, taps, cw, pre):
        self.nb, self.nc, self.nz = nb, nc, nc // 2
        self.own, self.frames, self.taps, self.cw, self.pre = own, frames, taps, cw, pre
        self.wide = cw * nc
        self.all = own * nc
        unit = self.all // 30
        self.pieces = []
        at = 0
        for w in WIDTHS:
            self.pieces.append((at, w * unit))
            at += w * unit
        self.head = self.all - pre
        self.full = self.head // own
        self.part = self.head % own
        step = math.gcd(own, self.head)
        self.step = step // 2 if step % 32 == 0 else step
        self.late = []
        for row in range(self.head, self.all, self.step):
            c = row // own
            self.late.append((c // 2, c % 2, row))
        self.iw0 = pre // nb
        self.iw = self.wide // nb
        self.group = 5
        self.sems = 0
        nz = self.nz
        self.s_entry = self.take(2 * len(self.late))
        self.s_rest = self.take(2 * nz)
        self.s_x = [self.take(2 * nz) for _ in range(3)]
        self.s_sum = [self.take(nb) for _ in range(8)]
        self.s_xs = [self.take(nb) for _ in range(4)]
        self.s_dy = [self.take(nb) for _ in range(4)]
        self.s_rs = [self.take(2 * nz) for _ in range(3)]
        self.s_dp = self.take(2 * nz)
        self.s_tail = self.take(3 * len(self.late))
        self.s_dr = [self.take(nb) for _ in range(2)]

    def take(self, count):
        base = self.sems
        self.sems += count
        return base


def up16(n):
    return (n + 15) // 16 * 16


SUM_ROWS = (8, 40, 8, 8, 16, 8, 16, 8)


def kernel(
    pn,
    length_ref,
    earlier_hbm,
    w0_hbm,
    w1_hbm,
    w23_hbm,
    rl_hbm,
    ru_hbm,
    lg_ref,
    lsh_ref,
    ug_ref,
    ush_ref,
    cot_ref,
    final_ref,
    egrad_hbm,
    g0_hbm,
    g1_hbm,
    g23_hbm,
    rlg_ref,
    rug_ref,
    lgg_ref,
    lsg_ref,
    ugg_ref,
    usg_ref,
    w0,
    w1,
    w2,
    w3,
    rcat,
    src,
    x1,
    x2,
    x3,
    big,
    resid,
    rmid,
    ys,
    dbuf,
    dgrp,
    drcat,
    dpart,
    dpsib,
    dprecv,
    dxpart,
    dxsib,
    dxrecv,
    tailsib,
    tailrecv,
    dyg,
    xs0,
    xs,
    xst,
    drs,
    drr,
    sums,
    colbuf,
    rowbuf,
    kcol,
    prm,
    hold,
    gout,
    gst,
    lsem,
    osem,
    ss,
    rs,
):
    nb, nc, nz = pn.nb, pn.nc, pn.nz
    T, K, C, E = pn.frames, pn.taps, pn.cw, pn.own
    WIDE, PRE, HEAD = pn.wide, pn.pre, pn.head
    b = lax.axis_index("batch")
    c = lax.axis_index("ch")
    z = c // 2
    q = lax.rem(c, 2)
    sib = z * 2 + 1 - q
    other = 1 - q

    def mult(v, m=16):
        return pl.multiple_of(v, m)

    def rcopy(source, target, i_send, i_recv, device):
        return pltpu.make_async_remote_copy(
            src_ref=source,
            dst_ref=target,
            send_sem=ss.at[i_send],
            recv_sem=rs.at[i_recv],
            device_id=device,
            device_id_type=MESH,
        )

    def chip(zz, qq):
        return {"ch": zz * 2 + qq}

    local_loads = []

    def load(source, target):
        cp = pltpu.make_async_copy(source, target, lsem.at[len(local_loads)])
        local_loads.append(cp)
        cp.start()
        return cp

    raw = dpart
    ld_raw = load(earlier_hbm, raw.at[0:E])
    ld_w0 = load(w0_hbm, w0.at[0 : K * C])
    ld_w0l = load(rl_hbm.at[:, HEAD : HEAD + PRE], w0.at[K * C : (K + 1) * C])
    ld_w0u = load(ru_hbm.at[:, HEAD : HEAD + PRE], w0.at[(K + 1) * C : (K + 2) * C])
    ld_w1 = load(w1_hbm, w1)
    ld_rl = load(rl_hbm.at[:, 0:HEAD], rcat.at[0:C])
    ld_ru = load(ru_hbm.at[:, 0:HEAD], rcat.at[C : 2 * C])
    ld_w2 = load(w23_hbm.at[0 : K * C], w2.at[0 : K * C])
    ld_w2m = load(ru_hbm.at[:, HEAD + PRE : HEAD + PRE + WIDE], w2.at[K * C : (K + 1) * C])
    ld_w3 = load(w23_hbm.at[K * C : 2 * K * C], w3)

    bar = pltpu.get_barrier_semaphore()
    pl.semaphore_signal(bar, inc=1, device_id={"ch": sib}, device_id_type=MESH)
    for d in range(1, nz):
        pl.semaphore_signal(bar, inc=1, device_id=chip(lax.rem(z + d, nz), q), device_id_type=MESH)
    for d in range(1, nb):
        pl.semaphore_signal(bar, inc=1, device_id={"batch": lax.rem(b + d, nb)}, device_id_type=MESH)

    colbuf[...] = jnp.zeros_like(colbuf)
    rowbuf[...] = jnp.zeros_like(rowbuf)
    prm[...] = jnp.zeros_like(prm)
    prm[0, 0:11, 0:C] = lg_ref[...]
    prm[1, 0:11, 0:C] = lsh_ref[...]
    prm[2, 0:12, 0:C] = ug_ref[...]
    prm[3, 0:12, 0:C] = ush_ref[...]
    length = length_ref[0]
    lane_row = lax.broadcasted_iota(jnp.int32, (1, T), 1)
    valid = jnp.where(lane_row < length, 1.0, 0.0).astype(F32)
    valid_rb = jnp.broadcast_to(valid, (RB, T))

    ld_raw.wait()
    valid_b = valid.astype(BF16)

    def mask_rows(i, _):
        src[pl.ds(mult(c * E + i * RB), RB), :] = raw[pl.ds(mult(i * RB), RB), :] * jnp.broadcast_to(
            valid_b, (RB, T)
        )
        return 0

    lax.fori_loop(0, E // RB, mask_rows, 0, unroll=2)
    pl.semaphore_wait(bar, 1 + (nz - 1) + (nb - 1))

    def entry_rows(n):
        return src.at[pn.late[n][2] : pn.late[n][2] + pn.step]

    def entry_hop(n, device):
        v = entry_rows(n)
        return rcopy(v, v, pn.s_entry + n, pn.s_entry + n, device)

    def entry_sib(n):
        i = pn.s_entry + len(pn.late) + n
        return rcopy(entry_rows(n), entry_rows(n), i, i, {"ch": sib})

    order = [n for n in range(len(pn.late))]
    below = chip(jnp.maximum(z - 1, 0), q)
    above = chip(jnp.minimum(z + 1, nz - 1), q)

    for n in order:
        zc, qc, _ = pn.late[n]

        @pl.when((q == qc) & (z == zc))
        def _():
            if zc > 0:
                entry_hop(n, below).start()
            if zc < nz - 1:
                v = entry_rows(n)
                rcopy(v, v, pn.s_tail + n, pn.s_entry + n, above).start()
            entry_sib(n).start()

    for n in order:
        zc, qc, _ = pn.late[n]

        @pl.when((q == qc) & (z < zc))
        def _():
            entry_hop(n, below).wait_recv()

            @pl.when(z > 0)
            def _():
                entry_hop(n, below).start()

            entry_sib(n).start()

        if zc < nz - 1:

            @pl.when((q == qc) & (z > zc))
            def _():
                entry_hop(n, above).wait_recv()

                @pl.when(z < nz - 1)
                def _():
                    entry_hop(n, above).start()

                entry_sib(n).start()

        @pl.when(q != qc)
        def _():
            entry_sib(n).wait_recv()

    def entry_drain():
        for n in order:
            zc, qc, _ = pn.late[n]

            @pl.when(q == qc)
            def _():
                entry_sib(n).wait_send()

            @pl.when((q == qc) & (z <= zc) & (z > 0))
            def _():
                entry_hop(n, below).wait_send()

            if zc < nz - 1:

                @pl.when((q == qc) & (z == zc))
                def _():
                    v = entry_rows(n)
                    rcopy(v, v, pn.s_tail + n, pn.s_entry + n, above).wait_send()

                @pl.when((q == qc) & (z > zc) & (z < nz - 1))
                def _():
                    entry_hop(n, above).wait_send()

    def sized(cc, body):
        @pl.when(cc < pn.full)
        def _():
            body(E)

        if pn.part:

            @pl.when(cc == pn.full)
            def _():
                body(pn.part)

    class Gather:
        def __init__(self, base, buf, rows, cut=False):
            self.base, self.buf, self.rows, self.cut = base, buf, rows, cut

        def each(self, zz, qq, body):
            cc = zz * 2 + qq
            if self.cut:
                sized(cc, lambda n: body(self.buf.at[pl.ds(mult(cc * self.rows), n)]))
            else:
                body(self.buf.at[pl.ds(mult(cc * self.rows), self.rows)])

        def start(self):
            def go(v):
                for d in range(1, nz):
                    zz = lax.rem(z + d, nz)
                    rcopy(v, v, self.base + zz, self.base + z, chip(zz, q)).start()
                rcopy(v, v, self.base + nz + z, self.base + nz + z, {"ch": sib}).start()

            self.each(z, q, go)

        def step(self, d):
            zz = lax.rem(z + d, nz)

            def go(v):
                rcopy(v, v, self.base + zz, self.base + zz, {"ch": sib}).wait_recv()
                rcopy(v, v, self.base + nz + zz, self.base + nz + zz, {"ch": sib}).start()

            self.each(zz, q, go)

        def end(self):
            for d in range(nz):
                zz = lax.rem(z + d, nz)
                i = self.base + nz + zz
                self.each(zz, other, lambda v: rcopy(v, v, i, i, {"ch": sib}).wait_recv())

        def drain(self):
            def go(v):
                for d in range(1, nz):
                    zz = lax.rem(z + d, nz)
                    rcopy(v, v, self.base + zz, self.base + z, chip(zz, q)).wait_send()

            self.each(z, q, go)
            for d in range(nz):
                zz = lax.rem(z + d, nz)
                i = self.base + nz + zz
                self.each(zz, q, lambda v: rcopy(v, v, i, i, {"ch": sib}).wait_send())

    def sum_copies(p):
        rows = SUM_ROWS[p]
        for d in range(1, nb):
            bb = lax.rem(b + d, nb)
            v = sums.at[p, b, 0:rows]
            yield bb, rcopy(v, v, pn.s_sum[p] + bb, pn.s_sum[p] + b, {"batch": bb})

    def sum_start(p):
        rows = SUM_ROWS[p]
        sums[p, b, 0:rows, :] = colbuf[...].T[0:rows, :]
        for _, cp in sum_copies(p):
            cp.start()

    def sum_finish(p):
        rows = SUM_ROWS[p]
        for bb, _ in sum_copies(p):
            v = sums.at[p, bb, 0:rows]
            rcopy(v, v, pn.s_sum[p] + bb, pn.s_sum[p] + bb, {"batch": bb}).wait_recv()
        total = sums[p, 0, 0:rows, :]
        for bb in range(1, nb):
            total = total + sums[p, bb, 0:rows, :]
        return total

    def columns(p, parts):
        at = 0
        for part in parts:
            rowbuf[at : at + part.shape[0], :] = part
            at += part.shape[0]
        kcol[p] = rowbuf[...].T

    def norm_rows(first, second, count, gain, shift):
        average = first / count
        scaling = lax.rsqrt(second / count - average * average + EPS)
        scale = scaling * gain
        return average, scaling, scale, shift - average * scale

    def blocks(body):
        def step(i, carry):
            body(pl.ds(mult(i * RB), RB))
            return carry

        lax.fori_loop(0, C // RB, step, 0)

    def at_row(base, r):
        return pl.ds(mult(base + r.start), RB)

    def lane_sum(v):
        return jnp.sum(v, axis=1, keepdims=True)

    def conv(w, x, y_index, extra):
        rows = (K * C) // 5

        def part(g, carry):
            r = pl.ds(mult(g * rows), rows)
            big[r, :] = dot(w[r, :], x)
            return carry

        lax.fori_loop(0, 5, part, 0)
        if extra:
            big[K * C : (K + extra) * C, :] = dot(w[K * C : (K + extra) * C, :], x)

        def add(i, carry):
            total = None
            for k in range(K):
                v = shifted(big[pl.ds(mult(k * C + i * RB), RB), :], k - K // 2)
                total = v if total is None else total + v
            ys[y_index, pl.ds(mult(i * RB), RB), :] = total
            return carry

        lax.fori_loop(0, C // RB, add, 0)

    def conv_sums(y_index, col):
        def body(r):
            y = ys[y_index, r, :] * valid_rb
            colbuf[r, col : col + 1] = lane_sum(y)
            colbuf[r, col + 1 : col + 2] = lane_sum(y * y)

        blocks(body)

    def slices(j):
        if j == 0:
            return src, HEAD, pn.iw0, xs0
        return (None, x1, x2, x3)[j], 0, pn.iw, xs.at[j - 1]

    def slice_copies(j):
        x, base, iw, target = slices(j)
        rows = up16(iw)
        for d in range(1, nb):
            bb = lax.rem(b + d, nb)
            if rows == iw:
                source = x.at[pl.ds(mult(base + bb * iw), iw)]
            else:
                source = xst.at[j, bb, 0:rows]
            there = target.at[:, pl.ds(mult(b * T, LANES), T)]
            yield bb, rcopy(source, there, pn.s_xs[j] + bb, pn.s_xs[j] + b, {"batch": bb})

    def slice_start(j):
        x, base, iw, target = slices(j)
        rows = up16(iw)
        here = pl.ds(mult(b * T, LANES), T)
        if rows == iw:
            target[:, here] = x[pl.ds(mult(base + b * iw), iw), :]
        else:
            for bb in range(nb):
                xst[j, bb, 0:rows, :] = jnp.zeros((rows, T), BF16)
                xst[j, bb, 0:iw, :] = x[base + bb * iw : base + (bb + 1) * iw, :]
            target[:, here] = xst[j, b, 0:rows, :]
        for _, cp in slice_copies(j):
            cp.start()

    def slice_finish(j):
        target = slices(j)[3]
        for bb, _ in slice_copies(j):
            v = target.at[:, pl.ds(mult(bb * T, LANES), T)]
            rcopy(v, v, pn.s_xs[j] + bb, pn.s_xs[j] + bb, {"batch": bb}).wait_recv()

    def dy_copies(j):
        v = dyg.at[j, :, pl.ds(mult(b * T, LANES), T)]
        for d in range(1, nb):
            bb = lax.rem(b + d, nb)
            yield bb, rcopy(v, v, pn.s_dy[j] + bb, pn.s_dy[j] + b, {"batch": bb})

    def dy_start(j):
        for _, cp in dy_copies(j):
            cp.start()

    def dy_finish(j):
        for bb, _ in dy_copies(j):
            v = dyg.at[j, :, pl.ds(mult(bb * T, LANES), T)]
            rcopy(v, v, pn.s_dy[j] + bb, pn.s_dy[j] + bb, {"batch": bb}).wait_recv()

    out_copies = []

    def weight_grad(j, out, first):
        _, _, iw, target = slices(j)
        slice_finish(j)
        dy_finish(j)
        rows = pn.group * C
        for g in range(K // pn.group):

            def build(u, carry):
                here = pl.ds(mult(u * T, LANES), T)
                dy = dyg[j, :, here]
                for i in range(pn.group):
                    k = g * pn.group + i
                    dgrp[i * C : (i + 1) * C, here] = shifted(dy, K // 2 - k)
                return carry

            lax.fori_loop(0, nb, build, 0)
            slot = len(out_copies) % 2
            if len(out_copies) >= 2 and not (j == 0 and g > 1):
                out_copies[-2].wait()
            grad = dot_last(dgrp[...], target[...])
            stage = gst if j == 0 else gout.at[slot]
            if j == 0 and g > 0:
                out_copies[-1].wait()
            stage[...] = grad[:, 0:iw]
            source = stage
            cp = pltpu.make_async_copy(
                source, out.at[first + g * rows : first + (g + 1) * rows], osem.at[slot]
            )
            cp.start()
            out_copies.append(cp)

    half = WIDE // 2
    hz = nz // 2
    upper_half = z // hz

    def shift_all(j):
        dy = dyg[j, :, pl.ds(mult(b * T, LANES), T)]
        for k in range(K):
            dbuf[k * C : (k + 1) * C, :] = shifted(dy, K // 2 - k)

    def back_rows(w, extra, lanes, to):
        rows = (K * C) // 5
        if extra:
            r = slice(K * C, (K + extra) * C)
            big[to, :] = dot_first(w[r, lanes], dbuf[r, :])
        else:
            r = pl.ds(0, rows)
            big[to, :] = dot_first(w[r, lanes], dbuf[r, :])

        def part(g, carry):
            r = pl.ds(mult(g * rows), rows)
            big[to, :] += dot_first(w[r, lanes], dbuf[r, :])
            return carry

        lax.fori_loop(0 if extra else 1, 5, part, 0)

    class Scatter:
        def __init__(self, n):
            self.base, self.part, self.sibs, self.recv = pn.s_rs[n], dxpart, dxsib.at[n], dxrecv.at[n]

        def rows(self, zz, qq):
            return pl.ds(mult((zz * 2 + qq) * C), C)

        def to_sib(self, zz):
            return rcopy(
                self.part.at[self.rows(zz, other)],
                self.sibs.at[zz],
                self.base + zz,
                self.base + zz,
                {"ch": sib},
            )

        def to_chip(self, zz):
            return rcopy(
                self.part.at[self.rows(zz, q)],
                self.recv.at[z],
                self.base + nz + zz,
                self.base + nz + z,
                chip(zz, q),
            )

        def compute(self, w, extra):
            for far in (1, 0):
                m = upper_half + far - 2 * upper_half * far
                at = pl.ds(mult(m * half, LANES), half)
                back_rows(w, extra, at, at)
                for i in range(hz):
                    zz = m * hz + i
                    r = self.rows(zz, other)
                    self.part[r, :] = big[r, :].astype(BF16)
                    self.to_sib(zz).start()

        def fold(self, zz):
            self.to_sib(zz).wait_recv()
            return big[self.rows(zz, q), :] + self.sibs[zz].astype(F32)

        def send(self):
            for i in range(hz):
                zz = (1 - upper_half) * hz + i
                self.part[self.rows(zz, q), :] = self.fold(zz).astype(BF16)
                self.to_chip(zz).start()
            for i in range(1, hz):
                zz = upper_half * hz + lax.rem(z - upper_half * hz + i, hz)
                self.part[self.rows(zz, q), :] = self.fold(zz).astype(BF16)
                self.to_chip(zz).start()
            hold[0] = self.fold(z)

        def end(self):
            total = hold[0]
            for d in range(1, nz):
                zz = lax.rem(z + d, nz)
                v = self.recv.at[zz]
                rcopy(v, v, self.base + nz + zz, self.base + nz + zz, {"ch": sib}).wait_recv()
                total = total + self.recv[zz].astype(F32)
            hold[0] = total
            self.drain()

        def drain(self):
            for d in range(nz):
                self.to_sib(lax.rem(z + d, nz)).wait_send()
            for d in range(1, nz):
                self.to_chip(lax.rem(z + d, nz)).wait_send()

    rest = Gather(pn.s_rest, src, E, cut=True)
    rest.start()
    ld_w0.wait()
    ld_w0l.wait()
    ld_w0u.wait()
    conv(w0, src[HEAD : HEAD + PRE, :], 0, 2)
    resid[8] = big[K * C : (K + 2) * C, :]
    conv_sums(0, 0)
    colbuf[0:C, 2:3] = jnp.broadcast_to(length.astype(F32), (C, 1))
    sum_start(0)
    total = sum_finish(0)
    count = jnp.broadcast_to(total[2:3, 0:1], (1, LANES))
    av, rsd, sc, off = norm_rows(total[0:1], total[1:2], count, prm[0, 0:1], prm[1, 0:1])
    columns(0, [sc, off, av, rsd])

    def activate(p, y_index, out):
        def body(r):
            v = ys[y_index, r, :] * kcol[p, r, 0:1] + kcol[p, r, 1:2]
            out[at_row(c * C, r), :] = (v * squash(v) * valid_rb).astype(BF16)

        blocks(body)

    activate(0, 0, x1)
    gx1 = Gather(pn.s_x[0], x1, C)
    gx1.start()
    slice_start(0)
    for d in range(1, nz):
        gx1.step(d)
    gx1.end()
    ld_w1.wait()
    conv(w1, x1[...], 1, 0)
    for d in range(1, nz):
        rest.step(d)
    rest.end()
    ld_rl.wait()
    ld_ru.wait()
    for s in range(8):
        at, width = pn.pieces[s]
        resid[s] = dot(rcat[:, at : at + width], src[at : at + width, :])

    def first_sums(r):
        y = ys[1, r, :] * valid_rb
        colbuf[r, 0:1] = lane_sum(y)
        colbuf[r, 10:11] = lane_sum(y * y)
        for s in range(9):
            v = resid[s, r, :]
            colbuf[r, 1 + s : 2 + s] = lane_sum(v)
            colbuf[r, 11 + s : 12 + s] = lane_sum(v * v)
            v = resid[s, at_row(C, r), :]
            colbuf[r, 20 + s : 21 + s] = lane_sum(v)
            colbuf[r, 29 + s : 30 + s] = lane_sum(v * v)

    blocks(first_sums)
    sum_start(1)
    total = sum_finish(1)
    lo = norm_rows(total[0:10], total[10:20], count, prm[0, 1:11], prm[1, 1:11])
    lo_scale_rows, lo_rsd_rows = lo[2], lo[1]
    off_sum = jnp.sum(lo[3], axis=0, keepdims=True)
    columns(1, [lo[2], lo[0], lo[1], off_sum])
    up_av, up_rsd, up_sc, up_off = norm_rows(total[20:29], total[29:38], count, prm[2, 2:11], prm[3, 2:11])
    up_off_sum = jnp.sum(up_off, axis=0, keepdims=True)

    def lower_value(r):
        v = ys[1, r, :] * kcol[1, r, 0:1] + kcol[1, r, 30:31]
        for s in range(9):
            v = v + resid[s, r, :] * kcol[1, r, 1 + s : 2 + s]
        return v

    def lower_out(r):
        v = lower_value(r)
        hold[1, r, :] = v
        x2[at_row(c * C, r), :] = (v * squash(v) * valid_rb).astype(BF16)

    blocks(lower_out)
    gx2 = Gather(pn.s_x[1], x2, C)
    gx2.start()
    slice_start(1)
    for d in range(1, nz):
        gx2.step(d)
    gx2.end()
    ld_w2.wait()
    ld_w2m.wait()
    conv(w2, x2[...], 2, 1)
    rmid[...] = big[K * C : (K + 1) * C, :]
    conv_sums(2, 0)

    def mid_sums(r):
        v = rmid[r, :]
        colbuf[r, 2:3] = lane_sum(v)
        colbuf[r, 3:4] = lane_sum(v * v)

    blocks(mid_sums)
    sum_start(2)
    total = sum_finish(2)
    u2 = norm_rows(total[0:1], total[1:2], count, prm[2, 0:1], prm[3, 0:1])
    mid = norm_rows(total[2:3], total[3:4], count, prm[2, 11:12], prm[3, 11:12])
    columns(2, [u2[2], u2[3], u2[0], u2[1]])
    activate(2, 2, x3)
    gx3 = Gather(pn.s_x[2], x3, C)
    gx3.start()
    slice_start(2)
    for d in range(1, nz):
        gx3.step(d)
    gx3.end()
    ld_w3.wait()
    conv(w3, x3[...], 3, 0)
    conv_sums(3, 0)
    sum_start(3)
    total = sum_finish(3)
    u3 = norm_rows(total[0:1], total[1:2], count, prm[2, 1:2], prm[3, 1:2])
    up_scale_rows = [u3[2], up_sc, mid[2]]
    columns(
        3,
        [
            u3[2], up_sc, mid[2],
            u3[0], up_av, mid[0],
            u3[1], up_rsd, mid[1],
            u3[3] + up_off_sum + mid[3],
        ],
    )

    def value_back(v, gradient):
        s = squash(v)
        return gradient * valid_rb * s * (1.0 + v * (1.0 - s))

    def upper_out(r):
        v = ys[3, r, :] * kcol[3, r, 0:1] + kcol[3, r, 33:34]
        for s in range(9):
            v = v + resid[s, at_row(C, r), :] * kcol[3, r, 1 + s : 2 + s]
        v = v + rmid[r, :] * kcol[3, r, 10:11]
        final_ref[r, :] = (v * squash(v) * valid_rb).astype(BF16)
        dv = value_back(v, cot_ref[r, :].astype(F32))
        hold[2, r, :] = dv
        colbuf[r, 0:1] = lane_sum(dv)
        colbuf[r, 1:2] = lane_sum(dv * (ys[3, r, :] - kcol[3, r, 11:12])) * kcol[3, r, 22:23]
        for s in range(9):
            centred = resid[s, at_row(C, r), :] - kcol[3, r, 12 + s : 13 + s]
            colbuf[r, 2 + s : 3 + s] = lane_sum(dv * centred) * kcol[3, r, 23 + s : 24 + s]
        centred = rmid[r, :] - kcol[3, r, 21:22]
        colbuf[r, 11:12] = lane_sum(dv * centred) * kcol[3, r, 32:33]

    blocks(upper_out)
    sum_start(4)
    total = sum_finish(4)
    slice_start(3)
    upper_q = total[0:1]
    upper_g = total[1:12]
    usg_ref[1:12, :] = jnp.broadcast_to(upper_q[:, 0:C], (11, C))
    ugg_ref[1:12, :] = upper_g[:, 0:C]
    sc_rows = jnp.concatenate(up_scale_rows, axis=0)
    rsd_rows = jnp.concatenate([u3[1], up_rsd, mid[1]], axis=0)
    columns(4, [sc_rows * upper_q / count, sc_rows * rsd_rows * upper_g / count])

    def grad_rows(gradient, values, sc_col, av_col, a_col, b_col):
        return ((sc_col * gradient - (a_col + b_col * (values - av_col))) * valid_rb).astype(BF16)

    own_lanes = pl.ds(mult(b * T, LANES), T)

    def upper_dy(r):
        dyg[3, r, own_lanes] = grad_rows(
            hold[2, r, :], ys[3, r, :], kcol[3, r, 0:1], kcol[3, r, 11:12], kcol[4, r, 0:1], kcol[4, r, 11:12]
        )

    blocks(upper_dy)
    shift_all(3)
    sc0 = Scatter(0)
    sc0.compute(w3, 0)
    sc0.send()
    dy_start(3)

    def upper_dr(r):
        dv = hold[2, r, :]
        for s in range(9):
            drcat[s, at_row(C, r), :] = grad_rows(
                dv,
                resid[s, at_row(C, r), :],
                kcol[3, r, 1 + s : 2 + s],
                kcol[3, r, 12 + s : 13 + s],
                kcol[4, r, 1 + s : 2 + s],
                kcol[4, r, 12 + s : 13 + s],
            )
        dbuf[at_row(K * C, r), :] = grad_rows(
            dv, rmid[r, :], kcol[3, r, 10:11], kcol[3, r, 21:22], kcol[4, r, 10:11], kcol[4, r, 21:22]
        )

    blocks(upper_dr)

    def dense_stage(n, first_col, value):
        share = (pn.all + (WIDE if n else 0)) // nb
        end = first_col + value.shape[1]
        for bb in range(nb):
            lo_c, hi_c = max(first_col, bb * share), min(end, (bb + 1) * share)
            if lo_c < hi_c:
                drs[n, bb, :, lo_c - bb * share : hi_c - bb * share] = value[
                    :, lo_c - first_col : hi_c - first_col
                ].astype(BF16)

    def dense_copies(n):
        for d in range(1, nb):
            bb = lax.rem(b + d, nb)
            yield bb, rcopy(drs.at[n, bb], drr.at[n, b], pn.s_dr[n] + bb, pn.s_dr[n] + b, {"batch": bb})

    def dense_start(n):
        for _, cp in dense_copies(n):
            cp.start()

    def dense_finish(n, out):
        share = (pn.all + (WIDE if n else 0)) // nb
        total = drs[n, b, :, 0:share].astype(F32)
        for bb, _ in dense_copies(n):
            v = drr.at[n, bb]
            rcopy(v, v, pn.s_dr[n] + bb, pn.s_dr[n] + bb, {"batch": bb}).wait_recv()
            total = total + drr[n, bb, :, 0:share].astype(F32)
        out[...] = total

    for s in range(9):
        at, width = pn.pieces[s]
        dense_stage(1, at, dot_last(drcat[s, C : 2 * C, :], src[at : at + width, :]))
    dense_stage(1, HEAD + PRE, dot_last(dbuf[K * C : (K + 1) * C, :], x2[...]))
    sc0.end()

    def inner_back(p, y_index):
        def body(r):
            y = ys[y_index, r, :]
            dz = value_back(y * kcol[p, r, 0:1] + kcol[p, r, 1:2], hold[0, r, :])
            hold[3, r, :] = dz
            colbuf[r, 0:1] = lane_sum(dz)
            colbuf[r, 1:2] = lane_sum(dz * (y - kcol[p, r, 2:3])) * kcol[p, r, 3:4]

        blocks(body)

    def inner_dy(p, kept, y_index):
        def body(r):
            dyg[y_index, r, own_lanes] = grad_rows(
                hold[3, r, :], ys[y_index, r, :], kcol[kept, r, 0:1], kcol[kept, r, 2:3], kcol[p, r, 0:1], kcol[p, r, 1:2]
            )

        blocks(body)

    inner_back(2, 2)
    sum_start(5)
    total = sum_finish(5)
    dense_start(1)
    usg_ref[0:1, :] = total[0:1, 0:C]
    ugg_ref[0:1, :] = total[1:2, 0:C]
    columns(5, [u2[2] * total[0:1] / count, u2[2] * u2[1] * total[1:2] / count])
    inner_dy(5, 2, 2)
    shift_all(2)
    sc1 = Scatter(1)
    sc1.compute(w2, 1)
    sc1.send()
    dy_start(2)
    weight_grad(3, g23_hbm, K * C)
    sc1.end()

    def lower_back(r):
        v = hold[1, r, :]
        dv = value_back(v, hold[0, r, :])
        hold[2, r, :] = dv
        colbuf[r, 0:1] = lane_sum(dv)
        colbuf[r, 1:2] = lane_sum(dv * (ys[1, r, :] - kcol[1, r, 10:11])) * kcol[1, r, 20:21]
        for s in range(9):
            centred = resid[s, r, :] - kcol[1, r, 11 + s : 12 + s]
            colbuf[r, 2 + s : 3 + s] = lane_sum(dv * centred) * kcol[1, r, 21 + s : 22 + s]

    blocks(lower_back)
    sum_start(6)
    total = sum_finish(6)
    lower_q = total[0:1]
    lower_g = total[1:11]
    lsg_ref[1:11, :] = jnp.broadcast_to(lower_q[:, 0:C], (10, C))
    lgg_ref[1:11, :] = lower_g[:, 0:C]
    columns(6, [lo_scale_rows * lower_q / count, lo_scale_rows * lo_rsd_rows * lower_g / count])

    def lower_dy(r):
        dyg[1, r, own_lanes] = grad_rows(
            hold[2, r, :], ys[1, r, :], kcol[1, r, 0:1], kcol[1, r, 10:11], kcol[6, r, 0:1], kcol[6, r, 10:11]
        )

    blocks(lower_dy)
    shift_all(1)
    sc2 = Scatter(2)
    sc2.compute(w1, 0)
    sc2.send()
    dy_start(1)

    def lower_dr(r):
        dv = hold[2, r, :]
        for s in range(9):
            drcat[s, r, :] = grad_rows(
                dv,
                resid[s, r, :],
                kcol[1, r, 1 + s : 2 + s],
                kcol[1, r, 11 + s : 12 + s],
                kcol[6, r, 1 + s : 2 + s],
                kcol[6, r, 11 + s : 12 + s],
            )

    blocks(lower_dr)

    for s in range(8):
        at, width = pn.pieces[s]
        dpart[at : at + width, :] = dot_first(rcat[:, at : at + width], drcat[s]).astype(BF16)

    def dp_rows(zz, qq, n):
        return pl.ds(mult((zz * 2 + qq) * E), n)

    def dp_sib(zz, n):
        return rcopy(
            dpart.at[dp_rows(zz, other, n)], dpsib.at[zz, 0:n], pn.s_dp + zz, pn.s_dp + zz, {"ch": sib}
        )

    def dp_sib_in(zz, n):
        v = dpsib.at[zz, 0:n]
        return rcopy(v, v, pn.s_dp + zz, pn.s_dp + zz, {"ch": sib})

    def dp_chip(zz, n):
        return rcopy(
            dpart.at[dp_rows(zz, q, n)],
            dprecv.at[z, 0:n],
            pn.s_dp + nz + zz,
            pn.s_dp + nz + z,
            chip(zz, q),
        )

    def dp_in(zz, n):
        v = dprecv.at[zz, 0:n]
        return rcopy(v, v, pn.s_dp + nz + zz, pn.s_dp + nz + zz, {"ch": sib})

    for d in range(nz):
        zz = lax.rem(z + d, nz)
        sized(zz * 2 + other, lambda n: dp_sib(zz, n).start())

    def dp_fold(zz, n):
        def body(i, carry):
            here = pl.ds(mult(i * RB), RB)
            there = pl.ds(mult((zz * 2 + q) * E + i * RB), RB)
            dpart[there, :] = (dpart[there, :].astype(F32) + dpsib[zz, here, :].astype(F32)).astype(BF16)
            return carry

        lax.fori_loop(0, n // RB, body, 0)

    for d in range(1, nz):
        zz = lax.rem(z + d, nz)

        def go(n):
            dp_sib_in(zz, n).wait_recv()
            dp_fold(zz, n)
            dp_chip(zz, n).start()

        sized(zz * 2 + q, go)

    def go_own(n):
        dp_sib_in(z, n).wait_recv()
        dp_fold(z, n)

    sized(c, go_own)
    weight_grad(2, g23_hbm, 0)
    sc2.end()

    inner_back(0, 0)
    sum_start(7)
    total = sum_finish(7)
    lsg_ref[0:1, :] = total[0:1, 0:C]
    lgg_ref[0:1, :] = total[1:2, 0:C]
    l0_scale = kcol[0].T
    columns(7, [l0_scale[0:1] * total[0:1] / count, l0_scale[0:1] * l0_scale[3:4] * total[1:2] / count])
    inner_dy(7, 0, 0)
    shift_all(0)
    dbuf[K * C : (K + 2) * C, :] = drcat[8]
    cut = (PRE // 2 + LANES - 1) // LANES * LANES
    back_rows(w0, 2, slice(0, cut), slice(0, cut))
    back_rows(w0, 2, slice(cut, PRE), slice(cut, PRE))
    dy_start(0)

    count_late = len(pn.late)

    def tail_rows(n):
        return dpart.at[pn.late[n][2] : pn.late[n][2] + pn.step]

    def tail_sib(n):
        return rcopy(tail_rows(n), tailsib.at[n], pn.s_tail + n, pn.s_tail + n, {"ch": sib})

    def tail_hop(n, way, device):
        i = pn.s_tail + (1 + way) * count_late + n
        return rcopy(tail_rows(n), tailrecv.at[way, n], i, i, device)

    for n in range(count_late):
        zc, qc, row = pn.late[n]

        @pl.when(q != qc)
        def _():
            dpart[row : row + pn.step, :] = big[row - HEAD : row - HEAD + pn.step, :].astype(BF16)
            tail_sib(n).start()

    for n in range(count_late):
        zc, qc, row = pn.late[n]
        here = slice(row, row + pn.step)
        there = slice(row - HEAD, row - HEAD + pn.step)

        @pl.when(q == qc)
        def _():
            tail_sib(n).wait_recv()
            big[there, :] += tailsib[n].astype(F32)
            if zc > 0:

                @pl.when((z > 0) & (z <= zc))
                def _():
                    tail_hop(n, 0, above).wait_recv()
                    big[there, :] += tailrecv[0, n].astype(F32)

            if zc < nz - 1:

                @pl.when((z < nz - 1) & (z >= zc))
                def _():
                    tail_hop(n, 1, below).wait_recv()
                    big[there, :] += tailrecv[1, n].astype(F32)

            @pl.when(z < zc)
            def _():
                dpart[here, :] = big[there, :].astype(BF16)
                tail_hop(n, 0, above).start()

            if zc < nz - 1:

                @pl.when(z > zc)
                def _():
                    dpart[here, :] = big[there, :].astype(BF16)
                    tail_hop(n, 1, below).start()

            @pl.when(z == zc)
            def _():
                big[WIDE + row % E : WIDE + row % E + pn.step, :] = big[there, :] * valid

    for s in range(9):
        at, width = pn.pieces[s]
        dense_stage(0, at, dot_last(drcat[s, 0:C, :], src[at : at + width, :]))
    dense_start(0)
    weight_grad(1, g1_hbm, 0)
    weight_grad(0, g0_hbm, 0)
    dense_finish(1, rug_ref)

    def own_grad(n):
        for d in range(1, nz):
            dp_in(lax.rem(z + d, nz), n).wait_recv()

        def body(i, carry):
            here = pl.ds(mult(i * RB), RB)
            total = dpart[pl.ds(mult(c * E + i * RB), RB), :].astype(F32)
            for d in range(1, nz):
                total = total + dprecv[lax.rem(z + d, nz), here, :].astype(F32)
            big[pl.ds(mult(WIDE + i * RB), RB), :] = total * valid_rb
            return carry

        lax.fori_loop(0, n // RB, body, 0)

    sized(c, own_grad)
    egrad_copy = pltpu.make_async_copy(big.at[WIDE : WIDE + E], egrad_hbm, osem.at[2])
    egrad_copy.start()
    dense_finish(0, rlg_ref)

    out_copies[-1].wait()
    egrad_copy.wait()
    entry_drain()
    for g in (rest, gx1, gx2, gx3):
        g.drain()
    for p in range(8):
        for _, cp in sum_copies(p):
            cp.wait_send()
    for j in range(4):
        for _, cp in slice_copies(j):
            cp.wait_send()
        for _, cp in dy_copies(j):
            cp.wait_send()
    for n in range(2):
        for _, cp in dense_copies(n):
            cp.wait_send()
    for d in range(nz):
        zz = lax.rem(z + d, nz)
        sized(zz * 2 + other, lambda n: dp_sib(zz, n).wait_send())
    for d in range(1, nz):
        zz = lax.rem(z + d, nz)
        sized(zz * 2 + q, lambda n: dp_chip(zz, n).wait_send())
    for n in range(count_late):
        zc, qc, _ = pn.late[n]

        @pl.when(q != qc)
        def _():
            tail_sib(n).wait_send()

        @pl.when((q == qc) & (z < zc))
        def _():
            tail_hop(n, 0, above).wait_send()

        if zc < nz - 1:

            @pl.when((q == qc) & (z > zc))
            def _():
                tail_hop(n, 1, below).wait_send()


def per_device(
    nb,
    nc,
    earlier,
    lengths,
    lower_entry,
    lower_convs,
    upper_convs,
    lower_dense,
    upper_dense,
    lower_gain,
    lower_shift,
    upper_gain,
    upper_shift,
    cotangent,
):
    _, own, frames = earlier.shape
    taps, cw, pre = lower_entry.shape
    pn = Plan(nb, nc, own, frames, taps, cw, pre)
    T, K, C, E, WIDE, nz = frames, taps, cw, own, pn.wide, pn.nz
    late = len(pn.late)
    share = ((pn.all + WIDE) // nb + LANES - 1) // LANES * LANES
    w0p, wp = up16(pn.iw0), up16(pn.iw)
    staged = 4 if (w0p != pn.iw0 or wp != pn.iw) else 1
    vmem, any_ = pl.BlockSpec(memory_space=pltpu.VMEM), pl.BlockSpec(memory_space=pl.ANY)
    smem = pl.BlockSpec(memory_space=pltpu.SMEM)
    V = pltpu.VMEM
    scratch = [
        V(((K + 2) * C, pre), BF16),
        V((K * C, WIDE), BF16),
        V(((K + 1) * C, WIDE), BF16),
        V((K * C, WIDE), BF16),
        V((2 * C, pn.head), BF16),
        V((pn.all, T), BF16),
        V((WIDE, T), BF16),
        V((WIDE, T), BF16),
        V((WIDE, T), BF16),
        V(((K + 2) * C, T), F32),
        V((9, 2 * C, T), F32),
        V((C, T), F32),
        V((4, C, T), F32),
        V(((K + 2) * C, T), BF16),
        V((pn.group * C, nb * T), BF16),
        V((9, 2 * C, T), BF16),
        V((pn.all, T), BF16),
        V((nz, E, T), BF16),
        V((nz, E, T), BF16),
        V((WIDE, T), BF16),
        V((3, nz, C, T), BF16),
        V((3, nz, C, T), BF16),
        V((late, pn.step, T), BF16),
        V((1 + (pn.late[0][0] < nz - 1), late, pn.step, T), BF16),
        V((4, C, nb * T), BF16),
        V((w0p, nb * T), BF16),
        V((3, wp, nb * T), BF16),
        V((4, nb, max(w0p, wp), T) if staged == 4 else (1, 1, 16, T), BF16),
        V((2, nb, C, share), BF16),
        V((2, nb, C, share), BF16),
        V((8, nb, 40, LANES), F32),
        V((LANES, LANES), F32),
        V((LANES, LANES), F32),
        V((8, LANES, LANES), F32),
        V((4, 16, LANES), F32),
        V((4, C, T), F32),
        V((2, pn.group * C, pn.iw), F32),
        V((pn.group * C, pn.iw0), F32),
        pltpu.SemaphoreType.DMA((10,)),
        pltpu.SemaphoreType.DMA((3,)),
        pltpu.SemaphoreType.DMA((pn.sems,)),
        pltpu.SemaphoreType.DMA((pn.sems,)),
    ]
    shape = jax.ShapeDtypeStruct
    outs = pl.pallas_call(
        functools.partial(kernel, pn),
        out_shape=(
            shape((C, T), BF16),
            shape((E, T), F32),
            shape((K * C, pn.iw0), F32),
            shape((K * C, pn.iw), F32),
            shape((2 * K * C, pn.iw), F32),
            shape((C, pn.all // nb), F32),
            shape((C, (pn.all + WIDE) // nb), F32),
            shape((11, C), F32),
            shape((11, C), F32),
            shape((12, C), F32),
            shape((12, C), F32),
        ),
        in_specs=[smem] + [any_] * 6 + [vmem] * 5,
        out_specs=(vmem, any_, any_, any_, any_, vmem, vmem, vmem, vmem, vmem, vmem),
        scratch_shapes=scratch,
        compiler_params=pltpu.CompilerParams(
            collective_id=0, has_side_effects=True, vmem_limit_bytes=64000 * 1024
        ),
    )(
        lengths,
        earlier.reshape(own, frames),
        lower_entry.reshape(K * C, pre),
        lower_convs.reshape(K * C, WIDE),
        upper_convs.reshape(2 * K * C, WIDE),
        lower_dense,
        upper_dense,
        lower_gain,
        lower_shift,
        upper_gain,
        upper_shift,
        cotangent.reshape(C, T),
    )
    final, egrad, g0, g1, g23, rlg, rug, lgg, lsg, ugg, usg = outs
    return (
        final.reshape(1, C, T),
        egrad.reshape(1, E, T),
        g0.reshape(K, C, pn.iw0),
        g1.reshape(1, K, C, pn.iw),
        g23.reshape(2, K, C, pn.iw),
        rlg,
        rug,
        lgg,
        lsg,
        ugg,
        usg,
    )


def solution(mesh):
    placed = (
        P("batch", "ch", None),
        P("batch"),
        P(None, "ch", None),
        P(None, None, "ch", None),
        P(None, None, "ch", None),
        P("ch", None),
        P("ch", None),
        P(None, "ch"),
        P(None, "ch"),
        P(None, "ch"),
        P(None, "ch"),
        P("batch", "ch", None),
    )
    return jax.shard_map(
        functools.partial(per_device, mesh.shape["batch"], mesh.shape["ch"]),
        mesh=mesh,
        in_specs=placed,
        out_specs=(
            P("batch", "ch", None),
            P("batch", "ch", None),
            P(None, "ch", "batch"),
            P(None, None, "ch", "batch"),
            P(None, None, "ch", "batch"),
            P("ch", "batch"),
            P("ch", "batch"),
            P(None, "ch"),
            P(None, "ch"),
            P(None, "ch"),
            P(None, "ch"),
        ),
        check_vma=False,
    )
```

```python
import functools
import math

import jax
import jax.numpy as jnp
from jax import lax
from jax.experimental import pallas as pl
from jax.experimental.pallas import tpu as pltpu
from jax.sharding import PartitionSpec as P

EPS = 0.001
WIDTHS = (2, 2, 2, 3, 3, 4, 4, 5, 5)
MESH = pl.DeviceIdType.MESH
F32 = jnp.float32
BF16 = jnp.bfloat16
RB = 16
LANES = 128


def shifted(x, by):
    if by == 0:
        return x
    frames = x.shape[1]
    lane = lax.broadcasted_iota(jnp.int32, x.shape, 1)
    rolled = pltpu.roll(x, (-by) % frames, 1)
    keep = (lane < frames - by) if by > 0 else (lane >= -by)
    return jnp.where(keep, rolled, jnp.zeros_like(rolled))


def squash(v):
    return 0.5 * jnp.tanh(0.5 * v) + 0.5


def dot(a, b):
    return jnp.dot(a, b, preferred_element_type=F32)


def dot_first(a, b):
    return lax.dot_general(a, b, (((0,), (0,)), ((), ())), preferred_element_type=F32)


def dot_last(a, b):
    return lax.dot_general(a, b, (((1,), (1,)), ((), ())), preferred_element_type=F32)


class Plan:
    def __init__(self, nb, nc, own, frames, taps, cw, pre):
        self.nb, self.nc, self.nz = nb, nc, nc // 2
        self.own, self.frames, self.taps, self.cw, self.pre = own, frames, taps, cw, pre
        self.wide = cw * nc
        self.all = own * nc
        unit = self.all // 30
        self.pieces = []
        at = 0
        for w in WIDTHS:
            self.pieces.append((at, w * unit))
            at += w * unit
        self.head = self.all - pre
        self.full = self.head // own
        self.part = self.head % own
        step = math.gcd(own, self.head)
        self.step = step // 2 if step % 32 == 0 else step
        self.late = []
        for row in range(self.head, self.all, self.step):
            c = row // own
            self.late.append((c // 2, c % 2, row))
        self.iw0 = pre // nb
        self.iw = self.wide // nb
        self.group = 5
        self.sems = 0
        nz = self.nz
        self.s_entry = self.take(2 * len(self.late))
        self.s_rest = self.take(4 + 2 * nz)
        self.s_x = [self.take(2 * nz) for _ in range(3)]
        self.s_sum = [self.take(nb) for _ in range(8)]
        self.s_xs = [self.take(nb) for _ in range(4)]
        self.s_dy = [self.take(nb) for _ in range(4)]
        self.s_rs = [self.take(2 * nz) for _ in range(3)]
        self.s_dp = self.take(4 + 4 * nz)
        self.s_tail = self.take(3 * len(self.late))
        self.s_dr = [self.take(nb) for _ in range(2)]

    def take(self, count):
        base = self.sems
        self.sems += count
        return base


def up16(n):
    return (n + 15) // 16 * 16


SUM_ROWS = (8, 40, 8, 8, 16, 8, 16, 8)


def kernel(
    pn,
    length_ref,
    earlier_hbm,
    w0_hbm,
    w1_hbm,
    w23_hbm,
    rl_hbm,
    ru_hbm,
    lg_ref,
    lsh_ref,
    ug_ref,
    ush_ref,
    cot_ref,
    final_ref,
    egrad_hbm,
    g0_hbm,
    g1_hbm,
    g23_hbm,
    rlg_ref,
    rug_ref,
    lgg_ref,
    lsg_ref,
    ugg_ref,
    usg_ref,
    w0,
    w1,
    w2,
    w3,
    rcat,
    src,
    x1,
    x2,
    x3,
    big,
    resid,
    rmid,
    ys,
    dbuf,
    drcat,
    dpart,
    dpsib,
    dprecv,
    dpcomb,
    dxpart,
    dxsib,
    dxrecv,
    tailsib,
    tailrecv,
    dyg,
    xs0,
    xs,
    xst,
    drs,
    drr,
    sums,
    colbuf,
    rowbuf,
    kcol,
    prm,
    hold,
    gout,
    lsem,
    osem,
    ss,
    rs,
):
    nb, nc, nz = pn.nb, pn.nc, pn.nz
    T, K, C, E = pn.frames, pn.taps, pn.cw, pn.own
    WIDE, PRE, HEAD = pn.wide, pn.pre, pn.head
    b = lax.axis_index("batch")
    c = lax.axis_index("ch")
    z = c // 2
    q = lax.rem(c, 2)
    sib = z * 2 + 1 - q
    other = 1 - q

    def mult(v, m=16):
        return pl.multiple_of(v, m)

    def rcopy(source, target, i_send, i_recv, device):
        return pltpu.make_async_remote_copy(
            src_ref=source,
            dst_ref=target,
            send_sem=ss.at[i_send],
            recv_sem=rs.at[i_recv],
            device_id=device,
            device_id_type=MESH,
        )

    def chip(zz, qq):
        return {"ch": zz * 2 + qq}

    local_loads = []

    def load(source, target):
        cp = pltpu.make_async_copy(source, target, lsem.at[len(local_loads)])
        local_loads.append(cp)
        cp.start()
        return cp

    raw = dpart
    ld_raw = load(earlier_hbm, raw.at[0:E])
    ld_w0 = load(w0_hbm, w0.at[0 : K * C])
    ld_w0l = load(rl_hbm.at[:, HEAD : HEAD + PRE], w0.at[K * C : (K + 1) * C])
    ld_w0u = load(ru_hbm.at[:, HEAD : HEAD + PRE], w0.at[(K + 1) * C : (K + 2) * C])
    ld_w1 = load(w1_hbm, w1)
    ld_rl = load(rl_hbm.at[:, 0:HEAD], rcat.at[0:C])
    ld_ru = load(ru_hbm.at[:, 0:HEAD], rcat.at[C : 2 * C])
    ld_w2 = load(w23_hbm.at[0 : K * C], w2.at[0 : K * C])
    ld_w2m = load(ru_hbm.at[:, HEAD + PRE : HEAD + PRE + WIDE], w2.at[K * C : (K + 1) * C])
    ld_w3 = load(w23_hbm.at[K * C : 2 * K * C], w3)

    bar = pltpu.get_barrier_semaphore()
    pl.semaphore_signal(bar, inc=1, device_id={"ch": sib}, device_id_type=MESH)
    for d in range(1, nz):
        pl.semaphore_signal(bar, inc=1, device_id=chip(lax.rem(z + d, nz), q), device_id_type=MESH)
    for d in range(1, nb):
        pl.semaphore_signal(bar, inc=1, device_id={"batch": lax.rem(b + d, nb)}, device_id_type=MESH)

    rowbuf[...] = jnp.zeros_like(rowbuf)
    colbuf[...] = jnp.zeros_like(colbuf)
    prm[...] = jnp.zeros_like(prm)
    prm[0, 0:11, 0:C] = lg_ref[...]
    prm[1, 0:11, 0:C] = lsh_ref[...]
    prm[2, 0:12, 0:C] = ug_ref[...]
    prm[3, 0:12, 0:C] = ush_ref[...]
    length = length_ref[0]
    lane_row = lax.broadcasted_iota(jnp.int32, (1, T), 1)
    valid = jnp.where(lane_row < length, 1.0, 0.0).astype(F32)
    valid_rb = jnp.broadcast_to(valid, (RB, T))

    ld_raw.wait()
    valid_b = valid.astype(BF16)

    def mask_rows(i, _):
        src[pl.ds(mult(c * E + i * RB), RB), :] = raw[pl.ds(mult(i * RB), RB), :] * jnp.broadcast_to(
            valid_b, (RB, T)
        )
        return 0

    lax.fori_loop(0, E // RB, mask_rows, 0, unroll=2)
    pl.semaphore_wait(bar, 1 + (nz - 1) + (nb - 1))

    def sized(cc, body):
        @pl.when(cc < pn.full)
        def _():
            body(E)

        if pn.part:

            @pl.when(cc == pn.full)
            def _():
                body(pn.part)

    class Gather:
        def __init__(self, base, buf, rows):
            self.base, self.buf, self.rows = base, buf, rows

        def each(self, zz, qq, body):
            body(self.buf.at[pl.ds(mult((zz * 2 + qq) * self.rows), self.rows)])

        def start(self):
            def go(v):
                for d in range(1, nz):
                    zz = lax.rem(z + d, nz)
                    rcopy(v, v, self.base + zz, self.base + z, chip(zz, q)).start()
                rcopy(v, v, self.base + nz + z, self.base + nz + z, {"ch": sib}).start()

            self.each(z, q, go)

        def step(self, d):
            zz = lax.rem(z + d, nz)

            def go(v):
                rcopy(v, v, self.base + zz, self.base + zz, {"ch": sib}).wait_recv()
                rcopy(v, v, self.base + nz + zz, self.base + nz + zz, {"ch": sib}).start()

            self.each(zz, q, go)

        def end(self):
            for d in range(nz):
                zz = lax.rem(z + d, nz)
                i = self.base + nz + zz
                self.each(zz, other, lambda v: rcopy(v, v, i, i, {"ch": sib}).wait_recv())

        def drain(self):
            def go(v):
                for d in range(1, nz):
                    zz = lax.rem(z + d, nz)
                    rcopy(v, v, self.base + zz, self.base + z, chip(zz, q)).wait_send()

            self.each(z, q, go)
            for d in range(nz):
                zz = lax.rem(z + d, nz)
                i = self.base + nz + zz
                self.each(zz, q, lambda v: rcopy(v, v, i, i, {"ch": sib}).wait_send())

    class Rest:
        base = pn.s_rest

        def view(self, zz, n):
            return src.at[pl.ds(mult((zz * 2 + q) * E), n)]

        def inside(self, zz):
            return (zz >= 0) & (zz < nz)

        def own_copy(self, way, dist, n):
            v = self.view(z, n)
            i = self.base + (0 if way > 0 else 2) + dist - 1
            return rcopy(v, v, i, self.base + 4 + z, chip(z + way * dist, q))

        def own(self, way, dist):
            @pl.when(self.inside(z + way * dist))
            def _():
                sized(c, lambda n: self.own_copy(way, dist, n).start())

        def on_copy(self, way, zz, n):
            v = self.view(zz, n)
            return rcopy(v, v, self.base + 4 + zz, self.base + 4 + zz, chip(z + way, q))

        def sib_copy(self, zz, qq, n):
            v = src.at[pl.ds(mult((zz * 2 + qq) * E), n)]
            i = self.base + 4 + nz + zz
            return rcopy(v, v, i, i, {"ch": sib})

        def sib_own(self):
            sized(c, lambda n: self.sib_copy(z, q, n).start())

        def arrive(self, way, dist):
            zz = z - way * dist

            @pl.when(self.inside(zz))
            def _():
                sized(zz * 2 + q, lambda n: self.on_copy(way, zz, n).wait_recv())
                if dist >= 2:

                    @pl.when(self.inside(z + way))
                    def _():
                        sized(zz * 2 + q, lambda n: self.on_copy(way, zz, n).start())

                sized(zz * 2 + q, lambda n: self.sib_copy(zz, q, n).start())

        def end(self):
            for zz in range(nz):
                sized(zz * 2 + other, lambda n: self.sib_copy(zz, other, n).wait_recv())

        def drain(self):
            for way in (1, -1):
                for dist in (1, 2):

                    @pl.when(self.inside(z + way * dist))
                    def _():
                        sized(c, lambda n: self.own_copy(way, dist, n).wait_send())

                for dist in range(2, nz):
                    zz = z - way * dist

                    @pl.when(self.inside(zz) & self.inside(z + way))
                    def _():
                        sized(zz * 2 + q, lambda n: self.on_copy(way, zz, n).wait_send())

            for zz in range(nz):
                sized(zz * 2 + q, lambda n: self.sib_copy(zz, q, n).wait_send())

    rest = Rest()
    rest.own(1, 1)
    rest.own(1, 2)

    def entry_rows(n):
        return src.at[pn.late[n][2] : pn.late[n][2] + pn.step]

    def entry_hop(n, device):
        v = entry_rows(n)
        return rcopy(v, v, pn.s_entry + n, pn.s_entry + n, device)

    def entry_sib(n):
        i = pn.s_entry + len(pn.late) + n
        return rcopy(entry_rows(n), entry_rows(n), i, i, {"ch": sib})

    order = [n for n in range(len(pn.late))]
    below = chip(jnp.maximum(z - 1, 0), q)
    above = chip(jnp.minimum(z + 1, nz - 1), q)

    def entry_up(n):
        return rcopy(entry_rows(n), entry_rows(n), pn.s_tail + n, pn.s_entry + n, above)

    owners = sorted({(zc, qc) for zc, qc, _ in pn.late})
    for zc, qc in owners:
        mine = [n for n in order if pn.late[n][:2] == (zc, qc)]

        @pl.when((q == qc) & (z == zc))
        def _():
            for at, n in enumerate(mine):
                if at >= 3:
                    if zc > 0:
                        entry_hop(mine[at - 3], below).wait_send()
                    if zc < nz - 1:
                        entry_up(mine[at - 3]).wait_send()
                if zc > 0:
                    entry_hop(n, below).start()
                if zc < nz - 1:
                    entry_up(n).start()
                entry_sib(n).start()
            for n in mine[-3:]:
                if zc > 0:
                    entry_hop(n, below).wait_send()
                if zc < nz - 1:
                    entry_up(n).wait_send()

    for n in order:
        zc, qc, _ = pn.late[n]

        @pl.when((q == qc) & (z < zc))
        def _():
            entry_hop(n, below).wait_recv()

            @pl.when(z > 0)
            def _():
                entry_hop(n, below).start()

            entry_sib(n).start()

        if zc < nz - 1:

            @pl.when((q == qc) & (z > zc))
            def _():
                entry_hop(n, above).wait_recv()

                @pl.when(z < nz - 1)
                def _():
                    entry_hop(n, above).start()

                entry_sib(n).start()

    for n in order:

        @pl.when(q != pn.late[n][1])
        def _():
            entry_sib(n).wait_recv()

    def entry_drain():
        for n in order:
            zc, qc, _ = pn.late[n]

            @pl.when(q == qc)
            def _():
                entry_sib(n).wait_send()

            @pl.when((q == qc) & (z < zc) & (z > 0))
            def _():
                entry_hop(n, below).wait_send()

            if zc < nz - 1:

                @pl.when((q == qc) & (z > zc) & (z < nz - 1))
                def _():
                    entry_hop(n, above).wait_send()

    def sum_copies(p):
        rows = SUM_ROWS[p]
        for d in range(1, nb):
            bb = lax.rem(b + d, nb)
            v = sums.at[p, b, 0:rows]
            yield bb, rcopy(v, v, pn.s_sum[p] + bb, pn.s_sum[p] + b, {"batch": bb})

    lane_of = lax.broadcasted_iota(jnp.int32, (RB, LANES), 1)

    def pack_sums(r, parts):
        parts = [sum(v[:, i + LANES : i + 2 * LANES] for i in range(0, T - LANES, LANES)) + v[:, 0:LANES] for v in parts]
        size = 1
        while size < len(parts):
            size *= 2
        parts = parts + [None] * (size - len(parts))
        width = LANES
        while len(parts) > 1:
            width //= 2
            low = (lane_of // width) % 2 == 0
            fold = []
            for x, y in zip(parts[: len(parts) // 2], parts[len(parts) // 2 :]):
                y = x if y is None else y
                if x is None:
                    fold.append(None)
                elif width * 2 == LANES:
                    fold.append(jnp.where(low, x, y) + pltpu.roll(jnp.where(low, y, x), width, 1))
                else:
                    fold.append(
                        jnp.where(low, x + pltpu.roll(x, LANES - width, 1), y + pltpu.roll(y, width, 1))
                    )
            parts = fold
        total = parts[0]
        while width > 1:
            width //= 2
            total = total + pltpu.roll(total, LANES - width, 1)
        colbuf[r, :] = total

    def sum_start(p, count, constant=None):
        size = 1
        while size < count:
            size *= 2
        rowbuf[...] = colbuf[...].T
        sums[p, b, 0:count, :] = rowbuf[pl.ds(0, count, stride=LANES // size), :]
        if constant is not None:
            sums[p, b, count : count + 1, :] = constant
        for _, cp in sum_copies(p):
            cp.start()

    def sum_finish(p):
        rows = SUM_ROWS[p]
        for bb, _ in sum_copies(p):
            v = sums.at[p, bb, 0:rows]
            rcopy(v, v, pn.s_sum[p] + bb, pn.s_sum[p] + bb, {"batch": bb}).wait_recv()
        total = sums[p, 0, 0:rows, :]
        for bb in range(1, nb):
            total = total + sums[p, bb, 0:rows, :]
        return total

    def columns(p, parts):
        at = 0
        for part in parts:
            rowbuf[at : at + part.shape[0], :] = part
            at += part.shape[0]
        kcol[p] = rowbuf[...].T

    def norm_rows(first, second, count, gain, shift):
        average = first / count
        scaling = lax.rsqrt(second / count - average * average + EPS)
        scale = scaling * gain
        return average, scaling, scale, shift - average * scale

    def blocks(body):
        for i in range(0, C, RB):
            body(pl.ds(i, RB))

    def rolled(body):
        def step(i, carry):
            body(pl.ds(mult(i * RB), RB))
            return carry

        lax.fori_loop(0, C // RB, step, 0)

    def at_row(base, r):
        if isinstance(base, int) and isinstance(r.start, int):
            return pl.ds(base + r.start, RB)
        return pl.ds(mult(base + r.start), RB)

    def conv(w, x, y_index, more=None):
        if more is not None:
            more[...] = dot(w[K * C : K * C + more.shape[0], :], x)
        for i in range(0, C, RB):
            taps = jnp.concatenate([w[k * C + i : k * C + i + RB, :] for k in range(K)], axis=0)
            rows = dot(taps, x)
            total = None
            for k in range(K):
                v = shifted(rows[k * RB : (k + 1) * RB], k - K // 2)
                total = v if total is None else total + v
            ys[y_index, i : i + RB, :] = total

    def conv_sums(y_index):
        def body(r):
            y = ys[y_index, r, :] * valid_rb
            pack_sums(r, [y, y * y])

        blocks(body)

    def slices(j):
        if j == 0:
            return src, HEAD, pn.iw0, xs0
        return (None, x1, x2, x3)[j], 0, pn.iw, xs.at[j - 1]

    def slice_copies(j):
        x, base, iw, target = slices(j)
        rows = up16(iw)
        for d in range(1, nb):
            bb = lax.rem(b + d, nb)
            if rows == iw:
                source = x.at[pl.ds(mult(base + bb * iw), iw)]
            else:
                source = xst.at[j, bb, 0:rows]
            there = target.at[:, pl.ds(mult(b * T, LANES), T)]
            yield bb, rcopy(source, there, pn.s_xs[j] + bb, pn.s_xs[j] + b, {"batch": bb})

    def slice_start(j):
        x, base, iw, target = slices(j)
        rows = up16(iw)
        here = pl.ds(mult(b * T, LANES), T)
        if rows == iw:
            target[:, here] = x[pl.ds(mult(base + b * iw), iw), :]
        else:
            for bb in range(nb):
                xst[j, bb, 0:rows, :] = jnp.zeros((rows, T), BF16)
                xst[j, bb, 0:iw, :] = x[base + bb * iw : base + (bb + 1) * iw, :]
            target[:, here] = xst[j, b, 0:rows, :]
        for _, cp in slice_copies(j):
            cp.start()

    def slice_finish(j):
        target = slices(j)[3]
        for bb, _ in slice_copies(j):
            v = target.at[:, pl.ds(mult(bb * T, LANES), T)]
            rcopy(v, v, pn.s_xs[j] + bb, pn.s_xs[j] + bb, {"batch": bb}).wait_recv()

    def dy_copies(j):
        v = dyg.at[j, :, pl.ds(mult(b * T, LANES), T)]
        for d in range(1, nb):
            bb = lax.rem(b + d, nb)
            yield bb, rcopy(v, v, pn.s_dy[j] + bb, pn.s_dy[j] + b, {"batch": bb})

    def dy_start(j):
        for _, cp in dy_copies(j):
            cp.start()

    def dy_finish(j):
        for bb, _ in dy_copies(j):
            v = dyg.at[j, :, pl.ds(mult(bb * T, LANES), T)]
            rcopy(v, v, pn.s_dy[j] + bb, pn.s_dy[j] + bb, {"batch": bb}).wait_recv()

    out_copies = []

    def weight_grad(j, out, first, groups=range(K // pn.group)):
        _, _, iw, target = slices(j)
        rows = pn.group * C
        for g in groups:
            if g == 0:
                if out_copies:
                    out_copies[-1].wait()
                slice_finish(j)
                dy_finish(j)

            grad = None
            for u in range(nb):
                here = slice(u * T, (u + 1) * T)
                dy = dyg[j, :, here]
                taps = [shifted(dy, K // 2 - g * pn.group - i) for i in range(pn.group)]
                v = dot_last(jnp.concatenate(taps, axis=0), target[:, here])
                grad = v if grad is None else grad + v
            gout[g * rows : (g + 1) * rows, 0:iw] = grad[:, 0:iw]
            if g == K // pn.group - 1:
                cp = pltpu.make_async_copy(gout, out.at[first : first + K * C], osem.at[len(out_copies)])
                cp.start()
                out_copies.append(cp)

    half = WIDE // 2
    hz = nz // 2
    upper_half = z // hz

    def shift_all(j):
        dy = dyg[j, :, pl.ds(mult(b * T, LANES), T)]
        for k in range(K):
            dbuf[k * C : (k + 1) * C, :] = shifted(dy, K // 2 - k)

    def back_rows(w, extra, lanes, to):
        rows = (K + extra) * C
        big[to, :] = dot_first(w[0:rows, lanes], dbuf[0:rows, :])

    class Scatter:
        def __init__(self, n):
            self.base, self.part, self.sibs, self.recv = pn.s_rs[n], dxpart, dxsib.at[n], dxrecv.at[n]

        def rows(self, zz, qq):
            return pl.ds(mult((zz * 2 + qq) * C), C)

        def to_sib(self, zz):
            return rcopy(
                self.part.at[self.rows(zz, other)],
                self.sibs.at[zz],
                self.base + zz,
                self.base + zz,
                {"ch": sib},
            )

        def to_chip(self, zz):
            return rcopy(
                self.part.at[self.rows(zz, q)],
                self.recv.at[z],
                self.base + nz + zz,
                self.base + nz + z,
                chip(zz, q),
            )

        def compute(self, w, extra):
            for far in (1, 0):
                m = upper_half + far - 2 * upper_half * far
                at = pl.ds(mult(m * half, LANES), half)
                back_rows(w, extra, at, at)
                for i in range(hz):
                    zz = m * hz + i
                    r = self.rows(zz, other)
                    self.part[r, :] = big[r, :].astype(BF16)
                    self.to_sib(zz).start()

        def fold(self, zz):
            self.to_sib(zz).wait_recv()
            return big[self.rows(zz, q), :] + self.sibs[zz].astype(F32)

        def send(self):
            for i in range(hz):
                zz = (1 - upper_half) * hz + i
                self.part[self.rows(zz, q), :] = self.fold(zz).astype(BF16)
                self.to_chip(zz).start()
            for i in range(1, hz):
                zz = upper_half * hz + lax.rem(z - upper_half * hz + i, hz)
                self.part[self.rows(zz, q), :] = self.fold(zz).astype(BF16)
                self.to_chip(zz).start()
            hold[0] = self.fold(z)

        def end(self):
            total = hold[0]
            for d in range(1, nz):
                zz = lax.rem(z + d, nz)
                v = self.recv.at[zz]
                rcopy(v, v, self.base + nz + zz, self.base + nz + zz, {"ch": sib}).wait_recv()
                total = total + self.recv[zz].astype(F32)
            hold[0] = total
            self.drain()

        def drain(self):
            for d in range(nz):
                self.to_sib(lax.rem(z + d, nz)).wait_send()
            for d in range(1, nz):
                self.to_chip(lax.rem(z + d, nz)).wait_send()

    rest.sib_own()
    ld_w0.wait()
    ld_w0l.wait()
    ld_w0u.wait()
    conv(w0, src[HEAD : HEAD + PRE, :], 0, resid.at[8])
    conv_sums(0)
    sum_start(0, 2, jnp.broadcast_to(length.astype(F32), (1, LANES)))
    rest.own(-1, 1)
    rest.own(-1, 2)
    total = sum_finish(0)
    count = jnp.broadcast_to(total[2:3, 0:1], (1, LANES))
    av, rsd, sc, off = norm_rows(total[0:1], total[1:2], count, prm[0, 0:1], prm[1, 0:1])
    columns(0, [sc, off, av, rsd])

    def activate(p, y_index, out):
        def body(r):
            v = ys[y_index, r, :] * kcol[p, r, 0:1] + kcol[p, r, 1:2]
            out[at_row(c * C, r), :] = (v * squash(v) * valid_rb).astype(BF16)

        blocks(body)

    activate(0, 0, x1)
    gx1 = Gather(pn.s_x[0], x1, C)
    gx1.start()
    slice_start(0)
    for d in range(1, nz):
        gx1.step(d)
    gx1.end()
    ld_w1.wait()
    conv(w1, x1[...], 1)
    for dist in range(2, nz):
        rest.arrive(1, dist)
        rest.arrive(-1, dist)
        if dist == 2:
            rest.arrive(1, 1)
            rest.arrive(-1, 1)
    rest.end()
    ld_rl.wait()
    ld_ru.wait()
    for s in range(8):
        at, width = pn.pieces[s]
        resid[s] = dot(rcat[:, at : at + width], src[at : at + width, :])

    def first_sums(r):
        y = ys[1, r, :] * valid_rb
        lo = [resid[s, r, :] for s in range(9)]
        up = [resid[s, at_row(C, r), :] for s in range(9)]
        pack_sums(r, [y] + lo + [y * y] + [v * v for v in lo] + up + [v * v for v in up])

    blocks(first_sums)
    sum_start(1, 38)
    total = sum_finish(1)
    lo = norm_rows(total[0:10], total[10:20], count, prm[0, 1:11], prm[1, 1:11])
    lo_scale_rows, lo_rsd_rows = lo[2], lo[1]
    off_sum = jnp.sum(lo[3], axis=0, keepdims=True)
    columns(1, [lo[2], lo[0], lo[1], off_sum])
    up_av, up_rsd, up_sc, up_off = norm_rows(total[20:29], total[29:38], count, prm[2, 2:11], prm[3, 2:11])
    up_off_sum = jnp.sum(up_off, axis=0, keepdims=True)

    def lower_value(r):
        v = ys[1, r, :] * kcol[1, r, 0:1] + kcol[1, r, 30:31]
        for s in range(9):
            v = v + resid[s, r, :] * kcol[1, r, 1 + s : 2 + s]
        return v

    def lower_out(r):
        v = lower_value(r)
        hold[1, r, :] = v
        x2[at_row(c * C, r), :] = (v * squash(v) * valid_rb).astype(BF16)

    blocks(lower_out)
    gx2 = Gather(pn.s_x[1], x2, C)
    gx2.start()
    slice_start(1)
    for d in range(1, nz):
        gx2.step(d)
    gx2.end()
    ld_w2.wait()
    ld_w2m.wait()
    conv(w2, x2[...], 2, rmid)

    def mid_sums(r):
        y = ys[2, r, :] * valid_rb
        v = rmid[r, :]
        pack_sums(r, [y, y * y, v, v * v])

    blocks(mid_sums)
    sum_start(2, 4)
    total = sum_finish(2)
    u2 = norm_rows(total[0:1], total[1:2], count, prm[2, 0:1], prm[3, 0:1])
    mid = norm_rows(total[2:3], total[3:4], count, prm[2, 11:12], prm[3, 11:12])
    columns(2, [u2[2], u2[3], u2[0], u2[1]])
    activate(2, 2, x3)
    gx3 = Gather(pn.s_x[2], x3, C)
    gx3.start()
    slice_start(2)
    for d in range(1, nz):
        gx3.step(d)
    gx3.end()
    ld_w3.wait()
    conv(w3, x3[...], 3)
    conv_sums(3)
    sum_start(3, 2)
    total = sum_finish(3)
    u3 = norm_rows(total[0:1], total[1:2], count, prm[2, 1:2], prm[3, 1:2])
    up_scale_rows = [u3[2], up_sc, mid[2]]
    columns(
        3,
        [
            u3[2], up_sc, mid[2],
            u3[0], up_av, mid[0],
            u3[1], up_rsd, mid[1],
            u3[3] + up_off_sum + mid[3],
        ],
    )

    def value_back(v, gradient):
        s = squash(v)
        return gradient * valid_rb * s * (1.0 + v * (1.0 - s))

    def upper_out(r):
        v = ys[3, r, :] * kcol[3, r, 0:1] + kcol[3, r, 33:34]
        for s in range(9):
            v = v + resid[s, at_row(C, r), :] * kcol[3, r, 1 + s : 2 + s]
        v = v + rmid[r, :] * kcol[3, r, 10:11]
        final_ref[r, :] = (v * squash(v) * valid_rb).astype(BF16)
        dv = value_back(v, cot_ref[r, :].astype(F32))
        hold[2, r, :] = dv
        parts = [dv, dv * (ys[3, r, :] - kcol[3, r, 11:12])]
        parts += [dv * (resid[s, at_row(C, r), :] - kcol[3, r, 12 + s : 13 + s]) for s in range(9)]
        pack_sums(r, parts + [dv * (rmid[r, :] - kcol[3, r, 21:22])])

    rolled(upper_out)
    sum_start(4, 12)
    total = sum_finish(4)
    slice_start(3)
    upper_q = total[0:1]
    rsd_rows = jnp.concatenate([u3[1], up_rsd, mid[1]], axis=0)
    upper_g = total[1:12] * rsd_rows
    usg_ref[1:12, :] = jnp.broadcast_to(upper_q[:, 0:C], (11, C))
    ugg_ref[1:12, :] = upper_g[:, 0:C]
    sc_rows = jnp.concatenate(up_scale_rows, axis=0)
    columns(4, [sc_rows * upper_q / count, sc_rows * rsd_rows * upper_g / count])

    def grad_rows(gradient, values, sc_col, av_col, a_col, b_col):
        return ((sc_col * gradient - (a_col + b_col * (values - av_col))) * valid_rb).astype(BF16)

    own_lanes = pl.ds(mult(b * T, LANES), T)

    def upper_dy(r):
        dyg[3, r, own_lanes] = grad_rows(
            hold[2, r, :], ys[3, r, :], kcol[3, r, 0:1], kcol[3, r, 11:12], kcol[4, r, 0:1], kcol[4, r, 11:12]
        )

    blocks(upper_dy)
    shift_all(3)
    sc0 = Scatter(0)
    sc0.compute(w3, 0)
    sc0.send()
    dy_start(3)

    def upper_dr(r):
        dv = hold[2, r, :]
        for s in range(9):
            drcat[s, at_row(C, r), :] = grad_rows(
                dv,
                resid[s, at_row(C, r), :],
                kcol[3, r, 1 + s : 2 + s],
                kcol[3, r, 12 + s : 13 + s],
                kcol[4, r, 1 + s : 2 + s],
                kcol[4, r, 12 + s : 13 + s],
            )
        dbuf[at_row(K * C, r), :] = grad_rows(
            dv, rmid[r, :], kcol[3, r, 10:11], kcol[3, r, 21:22], kcol[4, r, 10:11], kcol[4, r, 21:22]
        )

    blocks(upper_dr)

    def dense_stage(n, first_col, value):
        share = (pn.all + (WIDE if n else 0)) // nb
        end = first_col + value.shape[1]
        for bb in range(nb):
            lo_c, hi_c = max(first_col, bb * share), min(end, (bb + 1) * share)
            if lo_c < hi_c:
                drs[n, bb, :, lo_c - bb * share : hi_c - bb * share] = value[
                    :, lo_c - first_col : hi_c - first_col
                ].astype(BF16)

    def dense_copies(n):
        for d in range(1, nb):
            bb = lax.rem(b + d, nb)
            yield bb, rcopy(drs.at[n, bb], drr.at[n, b], pn.s_dr[n] + bb, pn.s_dr[n] + b, {"batch": bb})

    def dense_start(n):
        for _, cp in dense_copies(n):
            cp.start()

    def dense_finish(n, out):
        share = (pn.all + (WIDE if n else 0)) // nb
        total = drs[n, b, :, 0:share].astype(F32)
        for bb, _ in dense_copies(n):
            v = drr.at[n, bb]
            rcopy(v, v, pn.s_dr[n] + bb, pn.s_dr[n] + bb, {"batch": bb}).wait_recv()
            total = total + drr[n, bb, :, 0:share].astype(F32)
        out[...] = total

    for s in range(9):
        at, width = pn.pieces[s]
        dense_stage(1, at, dot_last(drcat[s, C : 2 * C, :], src[at : at + width, :]))
    dense_stage(1, HEAD + PRE, dot_last(dbuf[K * C : (K + 1) * C, :], x2[...]))
    sc0.end()

    def inner_back(p, y_index):
        def body(r):
            y = ys[y_index, r, :]
            dz = value_back(y * kcol[p, r, 0:1] + kcol[p, r, 1:2], hold[0, r, :])
            hold[3, r, :] = dz
            pack_sums(r, [dz, dz * (y - kcol[p, r, 2:3])])

        blocks(body)

    def inner_dy(p, kept, y_index):
        def body(r):
            dyg[y_index, r, own_lanes] = grad_rows(
                hold[3, r, :], ys[y_index, r, :], kcol[kept, r, 0:1], kcol[kept, r, 2:3], kcol[p, r, 0:1], kcol[p, r, 1:2]
            )

        blocks(body)

    inner_back(2, 2)
    sum_start(5, 2)
    total = sum_finish(5)
    dense_start(1)
    inner_q, inner_g = total[0:1], total[1:2] * u2[1]
    usg_ref[0:1, :] = inner_q[:, 0:C]
    ugg_ref[0:1, :] = inner_g[:, 0:C]
    columns(5, [u2[2] * inner_q / count, u2[2] * u2[1] * inner_g / count])
    inner_dy(5, 2, 2)
    shift_all(2)
    sc1 = Scatter(1)
    sc1.compute(w2, 1)
    sc1.send()
    dy_start(2)
    weight_grad(3, g23_hbm, K * C)
    sc1.end()

    def lower_back(r):
        v = hold[1, r, :]
        dv = value_back(v, hold[0, r, :])
        hold[2, r, :] = dv
        parts = [dv, dv * (ys[1, r, :] - kcol[1, r, 10:11])]
        pack_sums(r, parts + [dv * (resid[s, r, :] - kcol[1, r, 11 + s : 12 + s]) for s in range(9)])

    rolled(lower_back)
    sum_start(6, 11)
    total = sum_finish(6)
    lower_q = total[0:1]
    lower_g = total[1:11] * lo_rsd_rows
    lsg_ref[1:11, :] = jnp.broadcast_to(lower_q[:, 0:C], (10, C))
    lgg_ref[1:11, :] = lower_g[:, 0:C]
    columns(6, [lo_scale_rows * lower_q / count, lo_scale_rows * lo_rsd_rows * lower_g / count])

    def lower_dy(r):
        dyg[1, r, own_lanes] = grad_rows(
            hold[2, r, :], ys[1, r, :], kcol[1, r, 0:1], kcol[1, r, 10:11], kcol[6, r, 0:1], kcol[6, r, 10:11]
        )

    blocks(lower_dy)
    shift_all(1)
    sc2 = Scatter(2)
    sc2.compute(w1, 0)
    sc2.send()
    dy_start(1)

    def lower_dr(r):
        dv = hold[2, r, :]
        for s in range(9):
            drcat[s, r, :] = grad_rows(
                dv,
                resid[s, r, :],
                kcol[1, r, 1 + s : 2 + s],
                kcol[1, r, 11 + s : 12 + s],
                kcol[6, r, 1 + s : 2 + s],
                kcol[6, r, 11 + s : 12 + s],
            )

    blocks(lower_dr)

    for s in range(8):
        at, width = pn.pieces[s]
        dpart[at : at + width, :] = dot_first(rcat[:, at : at + width], drcat[s]).astype(BF16)

    def dp_rows(zz, qq, n):
        return pl.ds(mult((zz * 2 + qq) * E), n)

    def dp_sib(zz, n):
        return rcopy(
            dpart.at[dp_rows(zz, other, n)], dpsib.at[zz, 0:n], pn.s_dp + 4 + 3 * nz + zz, pn.s_dp + 4 + 3 * nz + zz, {"ch": sib}
        )

    def dp_sib_in(zz, n):
        v = dpsib.at[zz, 0:n]
        return rcopy(v, v, pn.s_dp + 4 + 3 * nz + zz, pn.s_dp + 4 + 3 * nz + zz, {"ch": sib})

    def dp_inside(zz):
        return (zz >= 0) & (zz < nz)

    def dp_slot(way, dist):
        return (0 if way > 0 else 2) + dist - 1

    def dp_comb(way, dist):
        return dpcomb.at[0 if way > 0 or nz <= 4 else 1, dist - 2]

    def dp_comb_sem(way, dist):
        return pn.s_dp + 4 + (0 if way > 0 else nz) + dist

    def dp_out(way, dist, n):
        zz = z + way * dist
        source = dpart.at[dp_rows(zz, q, n)]
        i_send = pn.s_dp + 4 + 2 * nz + zz
        if dist <= 2:
            slot = dp_slot(way, dist)
            return rcopy(source, dprecv.at[slot, 0:n], i_send, pn.s_dp + slot, chip(zz, q))
        target = dp_comb(way, dist - 1).at[0:n]
        return rcopy(source, target, i_send, dp_comb_sem(way, dist - 1), chip(z + way, q))

    def dp_send(way, dist):
        zz = z + way * dist

        def go(n):
            if dist >= 2:

                @pl.when(dp_inside(z - way))
                def _():
                    v = dp_comb(way, dist).at[0:n]
                    i = dp_comb_sem(way, dist)
                    rcopy(v, v, i, i, {"ch": sib}).wait_recv()
                    dp_add(zz, n, dp_comb(way, dist))

            dp_out(way, dist, n).start()

        @pl.when(dp_inside(zz))
        def _():
            sized(zz * 2 + q, go)

    for d in range(nz):
        zz = lax.rem(z + d, nz)
        sized(zz * 2 + other, lambda n: dp_sib(zz, n).start())

    def dp_add(zz, n, ref):
        def body(i, carry):
            there = pl.ds(mult((zz * 2 + q) * E + i * RB), RB)
            dpart[there, :] = (dpart[there, :].astype(F32) + ref[pl.ds(mult(i * RB), RB), :].astype(F32)).astype(BF16)
            return carry

        lax.fori_loop(0, n // RB, body, 0)

    for s in range(9):
        at, width = pn.pieces[s]
        dense_stage(0, at, dot_last(drcat[s, 0:C, :], src[at : at + width, :]))
    dense_start(0)
    for d in range(nz):
        zz = lax.rem(z + d, nz)

        def fold(n):
            dp_sib_in(zz, n).wait_recv()
            dp_add(zz, n, dpsib.at[zz])

        sized(zz * 2 + q, fold)
    for way in (1, -1):
        for dist in range(nz - 1, 2, -1):
            dp_send(way, dist)
        dp_send(way, 1)
    weight_grad(2, g23_hbm, 0)
    sc2.end()

    inner_back(0, 0)
    sum_start(7, 2)
    weight_grad(1, g1_hbm, 0, [0])
    total = sum_finish(7)
    inner_q, inner_g = total[0:1], total[1:2] * rsd
    lsg_ref[0:1, :] = inner_q[:, 0:C]
    lgg_ref[0:1, :] = inner_g[:, 0:C]
    columns(7, [sc * inner_q / count, sc * rsd * inner_g / count])
    inner_dy(7, 0, 0)
    shift_all(0)
    dbuf[K * C : (K + 2) * C, :] = drcat[8]
    cut = (PRE // 2 + LANES - 1) // LANES * LANES
    back_rows(w0, 2, slice(0, cut), slice(0, cut))
    back_rows(w0, 2, slice(cut, PRE), slice(cut, PRE))
    dy_start(0)

    dp_send(-1, 2)
    count_late = len(pn.late)

    def tail_rows(n):
        return dpart.at[pn.late[n][2] : pn.late[n][2] + pn.step]

    def tail_sib(n):
        return rcopy(tail_rows(n), tailsib.at[n], pn.s_tail + n, pn.s_tail + n, {"ch": sib})

    def tail_hop(n, way, device):
        i = pn.s_tail + (1 + way) * count_late + n
        return rcopy(tail_rows(n), tailrecv.at[way, n], i, i, device)

    for n in range(count_late):
        zc, qc, row = pn.late[n]

        @pl.when(q != qc)
        def _():
            dpart[row : row + pn.step, :] = big[row - HEAD : row - HEAD + pn.step, :].astype(BF16)
            tail_sib(n).start()

    before, after = [], [True] * count_late
    for n in range(count_late):
        same = [m for m in range(n) if pn.late[m][:2] == pn.late[n][:2]]
        before.append(same[-2] if len(same) >= 2 else None)
        if len(same) >= 2:
            after[same[-2]] = False
    for n in range(count_late):
        if n % 2 == 1 and n // 2 + 1 < K // pn.group:
            weight_grad(1, g1_hbm, 0, [n // 2 + 1])
        zc, qc, row = pn.late[n]
        here = slice(row, row + pn.step)
        there = slice(row - HEAD, row - HEAD + pn.step)

        @pl.when(q == qc)
        def _():
            tail_sib(n).wait_recv()
            big[there, :] += tailsib[n].astype(F32)
            if zc > 0:

                @pl.when((z > 0) & (z <= zc))
                def _():
                    tail_hop(n, 0, above).wait_recv()
                    big[there, :] += tailrecv[0, n].astype(F32)

            if zc < nz - 1:

                @pl.when((z < nz - 1) & (z >= zc))
                def _():
                    tail_hop(n, 1, below).wait_recv()
                    big[there, :] += tailrecv[1, n].astype(F32)

            @pl.when(z < zc)
            def _():
                dpart[here, :] = big[there, :].astype(BF16)
                if before[n] is not None:
                    tail_hop(before[n], 0, above).wait_send()
                tail_hop(n, 0, above).start()

            if zc < nz - 1:

                @pl.when(z > zc)
                def _():
                    dpart[here, :] = big[there, :].astype(BF16)
                    if before[n] is not None:
                        tail_hop(before[n], 1, below).wait_send()
                    tail_hop(n, 1, below).start()

            @pl.when(z == zc)
            def _():
                big[WIDE + row % E : WIDE + row % E + pn.step, :] = big[there, :] * valid

    dp_send(1, 2)
    weight_grad(1, g1_hbm, 0, range(min(count_late // 2 + 1, K // pn.group), K // pn.group))
    weight_grad(0, g0_hbm, 0)
    dense_finish(1, rug_ref)

    def own_grad(n):
        def begin(i, carry):
            here = pl.ds(mult(i * RB), RB)
            big[pl.ds(mult(WIDE + i * RB), RB), :] = dpart[pl.ds(mult(c * E + i * RB), RB), :].astype(F32)
            return carry

        lax.fori_loop(0, n // RB, begin, 0)
        for way in (1, -1):
            for dist in (1, 2):

                @pl.when(dp_inside(z - way * dist))
                def _():
                    slot = dp_slot(way, dist)
                    v = dprecv.at[slot, 0:n]
                    rcopy(v, v, pn.s_dp + slot, pn.s_dp + slot, {"ch": sib}).wait_recv()

                    def body(i, carry):
                        there = pl.ds(mult(WIDE + i * RB), RB)
                        big[there, :] += dprecv[slot, pl.ds(mult(i * RB), RB), :].astype(F32)
                        return carry

                    lax.fori_loop(0, n // RB, body, 0)

        def last(i, carry):
            there = pl.ds(mult(WIDE + i * RB), RB)
            big[there, :] = big[there, :] * valid_rb
            return carry

        lax.fori_loop(0, n // RB, last, 0)

    sized(c, own_grad)
    egrad_copy = pltpu.make_async_copy(big.at[WIDE : WIDE + E], egrad_hbm, osem.at[4])
    egrad_copy.start()
    dense_finish(0, rlg_ref)

    out_copies[-1].wait()
    egrad_copy.wait()
    entry_drain()
    for g in (rest, gx1, gx2, gx3):
        g.drain()
    for p in range(8):
        for _, cp in sum_copies(p):
            cp.wait_send()
    for j in range(4):
        for _, cp in slice_copies(j):
            cp.wait_send()
        for _, cp in dy_copies(j):
            cp.wait_send()
    for n in range(2):
        for _, cp in dense_copies(n):
            cp.wait_send()
    for d in range(nz):
        zz = lax.rem(z + d, nz)
        sized(zz * 2 + other, lambda n: dp_sib(zz, n).wait_send())
    for way in (1, -1):
        for dist in range(1, nz):
            zz = z + way * dist

            @pl.when(dp_inside(zz))
            def _():
                sized(zz * 2 + q, lambda n: dp_out(way, dist, n).wait_send())

    for n in range(count_late):
        zc, qc, _ = pn.late[n]

        @pl.when(q != qc)
        def _():
            tail_sib(n).wait_send()

        if after[n]:

            @pl.when((q == qc) & (z < zc))
            def _():
                tail_hop(n, 0, above).wait_send()

        if after[n] and zc < nz - 1:

            @pl.when((q == qc) & (z > zc))
            def _():
                tail_hop(n, 1, below).wait_send()


def per_device(
    nb,
    nc,
    earlier,
    lengths,
    lower_entry,
    lower_convs,
    upper_convs,
    lower_dense,
    upper_dense,
    lower_gain,
    lower_shift,
    upper_gain,
    upper_shift,
    cotangent,
):
    _, own, frames = earlier.shape
    taps, cw, pre = lower_entry.shape
    pn = Plan(nb, nc, own, frames, taps, cw, pre)
    T, K, C, E, WIDE, nz = frames, taps, cw, own, pn.wide, pn.nz
    late = len(pn.late)
    share = ((pn.all + WIDE) // nb + LANES - 1) // LANES * LANES
    w0p, wp = up16(pn.iw0), up16(pn.iw)
    staged = 4 if (w0p != pn.iw0 or wp != pn.iw) else 1
    vmem, any_ = pl.BlockSpec(memory_space=pltpu.VMEM), pl.BlockSpec(memory_space=pl.ANY)
    smem = pl.BlockSpec(memory_space=pltpu.SMEM)
    V = pltpu.VMEM
    scratch = [
        V(((K + 2) * C, pre), BF16),
        V((K * C, WIDE), BF16),
        V(((K + 1) * C, WIDE), BF16),
        V((K * C, WIDE), BF16),
        V((2 * C, pn.head), BF16),
        V((pn.all, T), BF16),
        V((WIDE, T), BF16),
        V((WIDE, T), BF16),
        V((WIDE, T), BF16),
        V((WIDE + E, T), F32),
        V((9, 2 * C, T), F32),
        V((C, T), F32),
        V((4, C, T), F32),
        V(((K + 2) * C, T), BF16),
        V((9, 2 * C, T), BF16),
        V((pn.all, T), BF16),
        V((nz, E, T), BF16),
        V((4, E, T), BF16),
        V((2 if nz > 4 else 1, max(nz - 3, 1), E, T), BF16),
        V((WIDE, T), BF16),
        V((3, nz, C, T), BF16),
        V((3, nz, C, T), BF16),
        V((late, pn.step, T), BF16),
        V((1 + (pn.late[0][0] < nz - 1), late, pn.step, T), BF16),
        V((4, C, nb * T), BF16),
        V((w0p, nb * T), BF16),
        V((3, wp, nb * T), BF16),
        V((4, nb, max(w0p, wp), T) if staged == 4 else (1, 1, 16, T), BF16),
        V((2, nb, C, share), BF16),
        V((2, nb, C, share), BF16),
        V((8, nb, 40, LANES), F32),
        V((LANES, LANES), F32),
        V((LANES, LANES), F32),
        V((8, LANES, LANES), F32),
        V((4, 16, LANES), F32),
        V((4, C, T), F32),
        V((K * C, pn.iw), F32),
        pltpu.SemaphoreType.DMA((10,)),
        pltpu.SemaphoreType.DMA((5,)),
        pltpu.SemaphoreType.DMA((pn.sems,)),
        pltpu.SemaphoreType.DMA((pn.sems,)),
    ]
    shape = jax.ShapeDtypeStruct
    outs = pl.pallas_call(
        functools.partial(kernel, pn),
        out_shape=(
            shape((C, T), BF16),
            shape((E, T), F32),
            shape((K * C, pn.iw), F32),
            shape((K * C, pn.iw), F32),
            shape((2 * K * C, pn.iw), F32),
            shape((C, pn.all // nb), F32),
            shape((C, (pn.all + WIDE) // nb), F32),
            shape((11, C), F32),
            shape((11, C), F32),
            shape((12, C), F32),
            shape((12, C), F32),
        ),
        in_specs=[smem] + [any_] * 6 + [vmem] * 5,
        out_specs=(vmem, any_, any_, any_, any_, vmem, vmem, vmem, vmem, vmem, vmem),
        scratch_shapes=scratch,
        compiler_params=pltpu.CompilerParams(
            collective_id=0, has_side_effects=True, vmem_limit_bytes=64000 * 1024
        ),
    )(
        lengths,
        earlier.reshape(own, frames),
        lower_entry.reshape(K * C, pre),
        lower_convs.reshape(K * C, WIDE),
        upper_convs.reshape(2 * K * C, WIDE),
        lower_dense,
        upper_dense,
        lower_gain,
        lower_shift,
        upper_gain,
        upper_shift,
        cotangent.reshape(C, T),
    )
    final, egrad, g0, g1, g23, rlg, rug, lgg, lsg, ugg, usg = outs
    return (
        final.reshape(1, C, T),
        egrad.reshape(1, E, T),
        g0.reshape(K, C, pn.iw)[:, :, 0 : pn.iw0],
        g1.reshape(1, K, C, pn.iw),
        g23.reshape(2, K, C, pn.iw),
        rlg,
        rug,
        lgg,
        lsg,
        ugg,
        usg,
    )


def solution(mesh):
    placed = (
        P("batch", "ch", None),
        P("batch"),
        P(None, "ch", None),
        P(None, None, "ch", None),
        P(None, None, "ch", None),
        P("ch", None),
        P("ch", None),
        P(None, "ch"),
        P(None, "ch"),
        P(None, "ch"),
        P(None, "ch"),
        P("batch", "ch", None),
    )
    return jax.shard_map(
        functools.partial(per_device, mesh.shape["batch"], mesh.shape["ch"]),
        mesh=mesh,
        in_specs=placed,
        out_specs=(
            P("batch", "ch", None),
            P("batch", "ch", None),
            P(None, "ch", "batch"),
            P(None, None, "ch", "batch"),
            P(None, None, "ch", "batch"),
            P("ch", "batch"),
            P("ch", "batch"),
            P(None, "ch"),
            P(None, "ch"),
            P(None, "ch"),
            P(None, "ch"),
        ),
        check_vma=False,
    )
```

```python
import functools
import math

import jax
import jax.numpy as jnp
from jax import lax
from jax.experimental import pallas as pl
from jax.experimental.pallas import tpu as pltpu
from jax.sharding import PartitionSpec as P

EPS = 0.001
WIDTHS = (2, 2, 2, 3, 3, 4, 4, 5, 5)
MESH = pl.DeviceIdType.MESH
F32 = jnp.float32
BF16 = jnp.bfloat16
RB = 16
LANES = 128


def shifted(x, by):
    if by == 0:
        return x
    frames = x.shape[1]
    lane = lax.broadcasted_iota(jnp.int32, x.shape, 1)
    rolled = pltpu.roll(x, (-by) % frames, 1)
    keep = (lane < frames - by) if by > 0 else (lane >= -by)
    return jnp.where(keep, rolled, jnp.zeros_like(rolled))


def squash(v):
    return 0.5 * jnp.tanh(0.5 * v) + 0.5


def dot(a, b):
    return jnp.dot(a, b, preferred_element_type=F32)


def dot_first(a, b):
    return lax.dot_general(a, b, (((0,), (0,)), ((), ())), preferred_element_type=F32)


def dot_last(a, b):
    return lax.dot_general(a, b, (((1,), (1,)), ((), ())), preferred_element_type=F32)


class Plan:
    def __init__(self, nb, nc, own, frames, taps, cw, pre):
        self.nb, self.nc, self.nz = nb, nc, nc // 2
        self.own, self.frames, self.taps, self.cw, self.pre = own, frames, taps, cw, pre
        self.wide = cw * nc
        self.all = own * nc
        unit = self.all // 30
        self.pieces = []
        at = 0
        for w in WIDTHS:
            self.pieces.append((at, w * unit))
            at += w * unit
        self.head = self.all - pre
        self.full = self.head // own
        self.part = self.head % own
        step = math.gcd(own, self.head)
        self.step = max(n for n in (16, 32, 48) if step % n == 0)
        self.flight = 5
        self.late = []
        for row in range(self.head, self.all, self.step):
            c = row // own
            self.late.append((c // 2, c % 2, row))
        self.iw0 = pre // nb
        self.iw = self.wide // nb
        self.group = 5
        self.sems = 0
        nz = self.nz
        self.srcs = [[] for _ in range(nz)]
        for s, (at, width) in enumerate(self.pieces[:-1]):
            self.srcs[(at + width - 1) // (2 * own)].append(s)
        self.lo, self.width = [0] * nz, [0] * nz
        self.bound, self.final = [], [[] for _ in range(nz)]
        for zc in range(nz):
            if not self.srcs[zc]:
                continue
            first, last = self.pieces[self.srcs[zc][0]], self.pieces[self.srcs[zc][-1]]
            self.lo[zc], self.width[zc] = first[0], last[0] + last[1] - first[0]
            row = first[0]
            while row < last[0] + last[1]:
                end = min((row // own + 1) * own, last[0] + last[1])
                self.final[zc].append((row // own, row, end - row))
                if row // own // 2 < zc:
                    self.bound.append((zc, row // own % 2, row, end - row))
                row = end
        self.slots = max(len(x) for x in self.srcs)
        self.pw = max(self.width)
        self.split = 4 if cw % 32 == 0 else 2
        self.units = [(zc, u, u % nb) for zc in range(nz) for u in range(self.width[zc] // LANES)]
        self.nu = self.pw // LANES
        self.ku = (self.nu + nb - 1) // nb
        self.s_entry = self.take(2 * len(self.late))
        self.s_src = self.take(3)
        self.s_r1 = self.take(nz)
        self.s_r2 = self.take(self.split * nz)
        self.s_prm = self.take(nz)
        self.s_q = self.take(2 * nz)
        self.s_plane = [self.take(nb) for _ in range(3)]
        self.s_dv = self.take(2 * nz)
        self.s_gain = self.take(2 * nz)
        self.s_d1 = [self.take(nb * self.nu) for _ in range(2)]
        self.s_d2 = [self.take(max(self.ku * nz * 2, len(self.units))) for _ in range(2)]
        self.s_x = [self.take(4 + 2 * nz) for _ in range(3)]
        self.s_sum = [self.take(nb) for _ in range(8)]
        self.s_xs = [self.take(nb) for _ in range(4)]
        self.s_dy = [self.take(nb) for _ in range(4)]
        self.s_rs = [self.take(4 + 4 * nz) for _ in range(3)]
        self.s_dp = self.take(1 + max(len(x) for x in self.final))
        self.s_tail = self.take(3 * len(self.late))
        self.s_dr = [self.take(nb) for _ in range(2)]

    def share(self, blk):
        return (self.all + (self.wide if blk else 0)) // self.nb

    def dense_owners(self, blk):
        return [bb for bb in range(self.nb) if (bb + 1) * self.share(blk) > self.head]

    def take(self, count):
        base = self.sems
        self.sems += count
        return base


def up16(n):
    return (n + 15) // 16 * 16


SUM_ROWS = (8, 8, 8, 8, 8, 8, 8, 8)


def kernel(
    pn,
    length_ref,
    earlier_hbm,
    w0_hbm,
    w1_hbm,
    w23_hbm,
    rl_hbm,
    ru_hbm,
    lg_ref,
    lsh_ref,
    ug_ref,
    ush_ref,
    cot_ref,
    final_ref,
    egrad_hbm,
    g0_hbm,
    g1_hbm,
    g23_hbm,
    rlg_ref,
    rug_ref,
    lgg_ref,
    lsg_ref,
    ugg_ref,
    usg_ref,
    w0,
    w1,
    w2,
    w3,
    rp,
    rown,
    src,
    x1,
    x2,
    x3,
    big,
    resid,
    rmid,
    ys,
    dbuf,
    pr,
    drp,
    dr8,
    qpart,
    qrecv,
    dvx,
    gsend,
    grecv,
    dpo,
    dpsib,
    dpbnd,
    d1send,
    d1recv,
    d2send,
    d2recv,
    dxsib,
    dxrecv,
    dxcomb,
    tailsib,
    tailrecv,
    dyg,
    xs0,
    xs,
    xst,
    drs,
    drr,
    sums,
    colbuf,
    rowbuf,
    kcol,
    psums,
    pcol,
    prow,
    pk,
    prms,
    hold,
    gout,
    lsem,
    osem,
    ss,
    rs,
):
    nb, nc, nz = pn.nb, pn.nc, pn.nz
    T, K, C, E = pn.frames, pn.taps, pn.cw, pn.own
    WIDE, PRE, HEAD = pn.wide, pn.pre, pn.head
    b = lax.axis_index("batch")
    c = lax.axis_index("ch")
    z = c // 2
    q = lax.rem(c, 2)
    sib = z * 2 + 1 - q
    other = 1 - q

    def mult(v, m=16):
        return pl.multiple_of(v, m)

    def rcopy(source, target, i_send, i_recv, device):
        return pltpu.make_async_remote_copy(
            src_ref=source,
            dst_ref=target,
            send_sem=ss.at[i_send],
            recv_sem=rs.at[i_recv],
            device_id=device,
            device_id_type=MESH,
        )

    def chip(zz, qq):
        return {"ch": zz * 2 + qq}

    local_loads = []

    def load(source, target):
        cp = pltpu.make_async_copy(source, target, lsem.at[len(local_loads)])
        local_loads.append(cp)
        cp.start()
        return cp

    raw = dpo
    ld_raw = load(earlier_hbm, raw.at[0:E])
    ld_w0 = load(w0_hbm, w0.at[0 : K * C])
    ld_w0l = load(rl_hbm.at[:, HEAD : HEAD + PRE], w0.at[K * C : (K + 1) * C])
    ld_w0u = load(ru_hbm.at[:, HEAD : HEAD + PRE], w0.at[(K + 1) * C : (K + 2) * C])
    ld_w1 = load(w1_hbm, w1)
    dense = (rl_hbm, ru_hbm)

    def at_chip(body):
        for zc in range(nz):
            if pn.srcs[zc]:

                @pl.when(z == zc)
                def _():
                    body(zc)

    def own_dense(zc, blk):
        w = pn.width[zc]
        source = dense[blk].at[:, pn.lo[zc] : pn.lo[zc] + w]
        return pltpu.make_async_copy(source, rp.at[blk, zc * C : (zc + 1) * C, 0:w], lsem.at[8 + blk])

    ld_w2 = load(w23_hbm.at[0 : K * C], w2.at[0 : K * C])
    ld_w2m = load(ru_hbm.at[:, HEAD + PRE : HEAD + PRE + WIDE], w2.at[K * C : (K + 1) * C])
    ld_w3 = load(w23_hbm.at[K * C : 2 * K * C], w3)

    def start_own_dense(zc):
        own_dense(zc, 0).start()
        own_dense(zc, 1).start()

    at_chip(start_own_dense)

    bar = pltpu.get_barrier_semaphore()
    pl.semaphore_signal(bar, inc=1, device_id={"ch": sib}, device_id_type=MESH)
    for d in range(1, nz):
        pl.semaphore_signal(bar, inc=1, device_id=chip(lax.rem(z + d, nz), q), device_id_type=MESH)
    for d in range(1, nb):
        pl.semaphore_signal(bar, inc=1, device_id={"batch": lax.rem(b + d, nb)}, device_id_type=MESH)

    rowbuf[...] = jnp.zeros_like(rowbuf)
    colbuf[...] = jnp.zeros_like(colbuf)
    pcol[...] = jnp.zeros_like(pcol)
    prow[...] = jnp.zeros_like(prow)
    prm = prms.at[z]
    prm[...] = jnp.zeros(prm.shape, F32)
    prm[0, 0:11, 0:C] = lg_ref[...]
    prm[1, 0:11, 0:C] = lsh_ref[...]
    prm[2, 0:12, 0:C] = ug_ref[...]
    prm[3, 0:12, 0:C] = ush_ref[...]
    length = length_ref[0]
    lane_row = lax.broadcasted_iota(jnp.int32, (1, T), 1)
    valid = jnp.where(lane_row < length, 1.0, 0.0).astype(F32)
    valid_rb = jnp.broadcast_to(valid, (RB, T))

    ld_raw.wait()
    valid_b = valid.astype(BF16)

    def mask_rows(i, _):
        src[pl.ds(mult(c * E + i * RB), RB), :] = raw[pl.ds(mult(i * RB), RB), :] * jnp.broadcast_to(
            valid_b, (RB, T)
        )
        return 0

    lax.fori_loop(0, E // RB, mask_rows, 0, unroll=2)
    pl.semaphore_wait(bar, 1 + (nz - 1) + (nb - 1))

    def sized(cc, body):
        @pl.when(cc < pn.full)
        def _():
            body(E)

        if pn.part:

            @pl.when(cc == pn.full)
            def _():
                body(pn.part)

    def inside(zz):
        return (zz >= 0) & (zz < nz)

    class Gather:
        def __init__(self, base, buf, rows):
            self.base, self.buf, self.rows = base, buf, rows

        def view(self, zz, qq):
            return self.buf.at[pl.ds(mult((zz * 2 + qq) * self.rows), self.rows)]

        def own_copy(self, way, dist):
            v = self.view(z, q)
            i = self.base + (0 if way > 0 else 2) + dist - 1
            return rcopy(v, v, i, self.base + 4 + z, chip(z + way * dist, q))

        def on_copy(self, way, zz):
            v = self.view(zz, q)
            return rcopy(v, v, self.base + 4 + zz, self.base + 4 + zz, chip(z + way, q))

        def sib_copy(self, zz, qq):
            i = self.base + 4 + nz + zz
            return rcopy(self.view(zz, qq), self.view(zz, qq), i, i, {"ch": sib})

        def start(self):
            for dist in (2, 1):
                for way in (1, -1):

                    @pl.when(inside(z + way * dist))
                    def _():
                        self.own_copy(way, dist).start()

            self.sib_copy(z, q).start()

        def arrive(self):
            for dist in [2, 1] + list(range(3, nz)):
                for way in (1, -1):
                    zz = z - way * dist

                    @pl.when(inside(zz))
                    def _():
                        self.on_copy(way, zz).wait_recv()
                        if dist >= 2:

                            @pl.when(inside(z + way))
                            def _():
                                self.on_copy(way, zz).start()

                        self.sib_copy(zz, q).start()

        def end(self):
            for zz in range(nz):
                self.sib_copy(zz, other).wait_recv()

        def drain(self):
            for way in (1, -1):
                for dist in (1, 2):

                    @pl.when(inside(z + way * dist))
                    def _():
                        self.own_copy(way, dist).wait_send()

                for dist in range(2, nz):

                    @pl.when(inside(z - way * dist) & inside(z + way))
                    def _():
                        self.on_copy(way, z - way * dist).wait_send()

            for zz in range(nz):
                self.sib_copy(zz, q).wait_send()

    above = chip(jnp.minimum(z + 1, nz - 1), q)
    below = chip(jnp.maximum(z - 1, 0), q)

    def own_rows(cc, n):
        v = src.at[pl.ds(mult(cc * E), n)]
        return rcopy(v, v, pn.s_src, pn.s_src, {"ch": sib})

    def bound_hop(row, n):
        v = src.at[row : row + n]
        return rcopy(v, v, pn.s_src + 1, pn.s_src + 1, above)

    def bound_sib(row, n):
        v = src.at[row : row + n]
        return rcopy(v, v, pn.s_src + 2, pn.s_src + 2, {"ch": sib})

    share_rows = C // (pn.split // 2)
    in_group = lax.rem(b, pn.split)

    def share_of(member):
        return member // (pn.split // 2), mult(lax.rem(member, pn.split // 2) * share_rows)

    share_blk, share_row = share_of(in_group)

    for blk in (0, 1):

        @pl.when(share_blk == blk)
        def _():
            own_share = dense[blk].at[pl.ds(share_row, share_rows), 0:HEAD]
            pltpu.make_async_copy(own_share, rown, lsem.at[10]).start()

    def r_hop(blk, zz):
        w = pn.width[zz]
        source = rown.at[:, pn.lo[zz] : pn.lo[zz] + w]
        target = rp.at[blk, pl.ds(mult(z * C + share_row), share_rows), 0:w]
        return rcopy(source, target, pn.s_r1 + zz, pn.s_r1 + z, chip(zz, q))

    def r_hops(way, act):
        for zz in range(nz):
            if pn.width[zz]:
                for blk in (0, 1):

                    @pl.when(((z < zz) if way > 0 else (z > zz)) & (share_blk == blk))
                    def _():
                        act(r_hop(blk, zz))

    def r_shared(zc, zf, member):
        v = rp.at[share_blk, pl.ds(mult(zf * C + share_row), share_rows), 0 : pn.width[zc]]
        to = b - in_group + member
        return rcopy(v, v, pn.s_r2 + member * nz + zf, pn.s_r2 + in_group * nz + zf, {"batch": to})

    def r_arrive(zc):
        for zf in range(nz):
            if zf != zc:
                v = rp.at[share_blk, pl.ds(mult(zf * C + share_row), share_rows), 0 : pn.width[zc]]
                rcopy(v, v, pn.s_r1 + zf, pn.s_r1 + zf, {"ch": sib}).wait_recv()
                for k in range(1, pn.split):
                    r_shared(zc, zf, lax.rem(in_group + k, pn.split)).start()

    def r_finish(zc):
        own_dense(zc, 0).wait()
        own_dense(zc, 1).wait()
        for k in range(1, pn.split):
            member = lax.rem(in_group + k, pn.split)
            blk, row = share_of(member)
            for zf in range(nz):
                if zf != zc:
                    v = rp.at[blk, pl.ds(mult(zf * C + row), share_rows), 0 : pn.width[zc]]
                    i = pn.s_r2 + member * nz + zf
                    rcopy(v, v, i, i, {"ch": sib}).wait_recv()

    def r_drain(zc):
        for zf in range(nz):
            if zf != zc:
                for k in range(1, pn.split):
                    r_shared(zc, zf, lax.rem(in_group + k, pn.split)).wait_send()

    def others(body):
        for d in range(1, nz):
            body(lax.rem(z + d, nz))

    def prm_copy(zz):
        return rcopy(prms.at[z], prms.at[z], pn.s_prm + zz, pn.s_prm + z, chip(zz, q))

    def prm_arrive(zz):
        rcopy(prms.at[zz], prms.at[zz], pn.s_prm + zz, pn.s_prm + zz, {"ch": sib}).wait_recv()

    sized(c, lambda n: own_rows(c, n).start())
    for zc, qq, row, n in pn.bound:

        @pl.when((z == zc - 1) & (q == qq))
        def _():
            bound_hop(row, n).start()

    def entry_rows(n):
        return src.at[pn.late[n][2] : pn.late[n][2] + pn.step]

    def entry_hop(n, device):
        v = entry_rows(n)
        return rcopy(v, v, pn.s_entry + n, pn.s_entry + n, device)

    def entry_sib(n):
        i = pn.s_entry + len(pn.late) + n
        return rcopy(entry_rows(n), entry_rows(n), i, i, {"ch": sib})

    order = [n for n in range(len(pn.late))]
    def entry_up(n):
        return rcopy(entry_rows(n), entry_rows(n), pn.s_tail + n, pn.s_entry + n, above)

    owners = sorted({(zc, qc) for zc, qc, _ in pn.late})
    for zc, qc in owners:
        mine = [n for n in order if pn.late[n][:2] == (zc, qc)]

        @pl.when((q == qc) & (z == zc))
        def _():
            for at, n in enumerate(mine):
                if at >= pn.flight:
                    if zc > 0:
                        entry_hop(mine[at - pn.flight], below).wait_send()
                    if zc < nz - 1:
                        entry_up(mine[at - pn.flight]).wait_send()
                if zc > 0:
                    entry_hop(n, below).start()
                if zc < nz - 1:
                    entry_up(n).start()
                entry_sib(n).start()
            for n in mine[-pn.flight :]:
                if zc > 0:
                    entry_hop(n, below).wait_send()
                if zc < nz - 1:
                    entry_up(n).wait_send()

    pltpu.make_async_copy(rl_hbm.at[0:share_rows, 0:HEAD], rown, lsem.at[10]).wait()
    r_hops(1, lambda cp: cp.start())
    for n in order:
        zc, qc, _ = pn.late[n]

        @pl.when((q == qc) & (z < zc))
        def _():
            entry_hop(n, below).wait_recv()

            @pl.when(z > 0)
            def _():
                entry_hop(n, below).start()

            entry_sib(n).start()

        if zc < nz - 1:

            @pl.when((q == qc) & (z > zc))
            def _():
                entry_hop(n, above).wait_recv()

                @pl.when(z < nz - 1)
                def _():
                    entry_hop(n, above).start()

                entry_sib(n).start()

    for n in order:

        @pl.when(q != pn.late[n][1])
        def _():
            entry_sib(n).wait_recv()

    def entry_drain():
        for n in order:
            zc, qc, _ = pn.late[n]

            @pl.when(q == qc)
            def _():
                entry_sib(n).wait_send()

            @pl.when((q == qc) & (z < zc) & (z > 0))
            def _():
                entry_hop(n, below).wait_send()

            if zc < nz - 1:

                @pl.when((q == qc) & (z > zc) & (z < nz - 1))
                def _():
                    entry_hop(n, above).wait_send()

    def sum_copies(p):
        rows = SUM_ROWS[p]
        for d in range(1, nb):
            bb = lax.rem(b + d, nb)
            v = sums.at[p, b, 0:rows]
            yield bb, rcopy(v, v, pn.s_sum[p] + bb, pn.s_sum[p] + b, {"batch": bb})


    def tree(parts):
        tiles = range(0, T, LANES)
        parts = [v if v is None else functools.reduce(jnp.add, [v[:, i : i + LANES] for i in tiles]) for v in parts]
        lane_of = lax.broadcasted_iota(jnp.int32, (parts[0].shape[0], LANES), 1)
        size = 1
        while size < len(parts):
            size *= 2
        parts = parts + [None] * (size - len(parts))
        width = LANES
        while len(parts) > 1:
            width //= 2
            low = (lane_of // width) % 2 == 0
            fold = []
            for x, y in zip(parts[: len(parts) // 2], parts[len(parts) // 2 :]):
                y = x if y is None else y
                if x is None:
                    fold.append(None)
                elif width * 2 == LANES:
                    fold.append(jnp.where(low, x, y) + pltpu.roll(jnp.where(low, y, x), width, 1))
                else:
                    fold.append(
                        jnp.where(low, x + pltpu.roll(x, LANES - width, 1), y + pltpu.roll(y, width, 1))
                    )
            parts = fold
        total = parts[0]
        while width > 1:
            width //= 2
            total = total + pltpu.roll(total, LANES - width, 1)
        return total

    def pack_sums(r, parts):
        colbuf[r, :] = tree(parts)

    def sum_start(p, count, constant=None):
        size = 1
        while size < count:
            size *= 2
        rowbuf[...] = colbuf[...].T
        sums[p, b, 0:count, :] = rowbuf[pl.ds(0, count, stride=LANES // size), :]
        if constant is not None:
            sums[p, b, count : count + 1, :] = constant
        for _, cp in sum_copies(p):
            cp.start()

    def sum_finish(p):
        rows = SUM_ROWS[p]
        for bb, _ in sum_copies(p):
            v = sums.at[p, bb, 0:rows]
            rcopy(v, v, pn.s_sum[p] + bb, pn.s_sum[p] + bb, {"batch": bb}).wait_recv()
        total = sums[p, 0, 0:rows, :]
        for bb in range(1, nb):
            total = total + sums[p, bb, 0:rows, :]
        return total

    def columns(p, parts):
        at = 0
        for part in parts:
            rowbuf[at : at + part.shape[0], :] = part
            at += part.shape[0]
        kcol[p] = rowbuf[...].T

    def norm_rows(first, second, count, gain, shift):
        average = first / count
        scaling = lax.rsqrt(second / count - average * average + EPS)
        scale = scaling * gain
        return average, scaling, scale, shift - average * scale

    def blocks(body):
        for i in range(0, C, RB):
            body(pl.ds(i, RB))

    def rolled(body):
        def step(i, carry):
            body(pl.ds(mult(i * RB), RB))
            return carry

        lax.fori_loop(0, C // RB, step, 0)

    def at_row(base, r):
        if isinstance(base, int) and isinstance(r.start, int):
            return pl.ds(base + r.start, RB)
        return pl.ds(mult(base + r.start), RB)

    def conv(w, x, y_index, more=None):
        if more is not None:
            more[...] = dot(w[K * C : K * C + more.shape[0], :], x)
        for i in range(0, C, RB):
            taps = jnp.concatenate([w[k * C + i : k * C + i + RB, :] for k in range(K)], axis=0)
            rows = dot(taps, x)
            total = None
            for k in range(K):
                v = shifted(rows[k * RB : (k + 1) * RB], k - K // 2)
                total = v if total is None else total + v
            ys[y_index, i : i + RB, :] = total

    def conv_sums(y_index):
        def body(r):
            y = ys[y_index, r, :] * valid_rb
            pack_sums(r, [y, y * y])

        blocks(body)

    def slices(j):
        if j == 0:
            return src, HEAD, pn.iw0, xs0
        return (None, x1, x2, x3)[j], 0, pn.iw, xs.at[j - 1]

    def slice_copies(j):
        x, base, iw, target = slices(j)
        rows = up16(iw)
        for d in range(1, nb):
            bb = lax.rem(b + d, nb)
            if rows == iw:
                source = x.at[pl.ds(mult(base + bb * iw), iw)]
            else:
                source = xst.at[j, bb, 0:rows]
            there = target.at[:, pl.ds(mult(b * T, LANES), T)]
            yield bb, rcopy(source, there, pn.s_xs[j] + bb, pn.s_xs[j] + b, {"batch": bb})

    def slice_start(j):
        x, base, iw, target = slices(j)
        rows = up16(iw)
        here = pl.ds(mult(b * T, LANES), T)
        if rows == iw:
            target[:, here] = x[pl.ds(mult(base + b * iw), iw), :]
        else:
            for bb in range(nb):
                xst[j, bb, 0:rows, :] = jnp.zeros((rows, T), BF16)
                xst[j, bb, 0:iw, :] = x[base + bb * iw : base + (bb + 1) * iw, :]
            target[:, here] = xst[j, b, 0:rows, :]
        for _, cp in slice_copies(j):
            cp.start()

    def slice_finish(j):
        target = slices(j)[3]
        for bb, _ in slice_copies(j):
            v = target.at[:, pl.ds(mult(bb * T, LANES), T)]
            rcopy(v, v, pn.s_xs[j] + bb, pn.s_xs[j] + bb, {"batch": bb}).wait_recv()

    def dy_copies(j):
        v = dyg.at[j, :, pl.ds(mult(b * T, LANES), T)]
        for d in range(1, nb):
            bb = lax.rem(b + d, nb)
            yield bb, rcopy(v, v, pn.s_dy[j] + bb, pn.s_dy[j] + b, {"batch": bb})

    def dy_start(j):
        for _, cp in dy_copies(j):
            cp.start()

    def dy_finish(j):
        for bb, _ in dy_copies(j):
            v = dyg.at[j, :, pl.ds(mult(bb * T, LANES), T)]
            rcopy(v, v, pn.s_dy[j] + bb, pn.s_dy[j] + bb, {"batch": bb}).wait_recv()

    out_copies = []

    def weight_grad(j, out, first, groups=range(K // pn.group)):
        _, _, iw, target = slices(j)
        rows = pn.group * C
        for g in groups:
            if g == 0:
                if out_copies:
                    out_copies[-1].wait()
                slice_finish(j)
                dy_finish(j)

            grad = None
            for u in range(nb):
                here = slice(u * T, (u + 1) * T)
                dy = dyg[j, :, here]
                taps = [shifted(dy, K // 2 - g * pn.group - i) for i in range(pn.group)]
                v = dot_last(jnp.concatenate(taps, axis=0), target[:, here])
                grad = v if grad is None else grad + v
            gout[g * rows : (g + 1) * rows, 0:iw] = grad[:, 0:iw]
            if g == K // pn.group - 1:
                cp = pltpu.make_async_copy(gout, out.at[first : first + K * C], osem.at[len(out_copies)])
                cp.start()
                out_copies.append(cp)

    half = WIDE // 2
    hz = nz // 2
    upper_half = z // hz

    def shift_all(j):
        dy = dyg[j, :, pl.ds(mult(b * T, LANES), T)]
        for k in range(K):
            dbuf[k * C : (k + 1) * C, :] = shifted(dy, K // 2 - k)

    def back_rows(w, extra, lanes, to):
        rows = (K + extra) * C
        big[to, :] = dot_first(w[0:rows, lanes], dbuf[0:rows, :])

    class Scatter:
        def __init__(self, n):
            self.base, self.part, self.sibs, self.recv = pn.s_rs[n], x1, dxsib.at[n], dxrecv.at[n]
            self.combs = dxcomb.at[n]

        def rows(self, zz, qq):
            return pl.ds(mult((zz * 2 + qq) * C), C)

        def to_sib(self, zz):
            return rcopy(
                self.part.at[self.rows(zz, other)],
                self.sibs.at[zz],
                self.base + 4 + zz,
                self.base + 4 + zz,
                {"ch": sib},
            )

        def slot(self, way, dist):
            return (0 if way > 0 else 2) + dist - 1

        def comb(self, way, dist):
            first = 0 if way > 0 or nz <= 4 else nz - 3
            return self.combs.at[first + dist - 2], self.base + 4 + nz + (0 if way > 0 else nz) + dist

        def out(self, way, dist):
            zz = z + way * dist
            source = self.part.at[self.rows(zz, q)]
            i_send = self.base + 4 + 3 * nz + zz
            if dist <= 2:
                at = self.slot(way, dist)
                return rcopy(source, self.recv.at[at], i_send, self.base + at, chip(zz, q))
            target, i = self.comb(way, dist - 1)
            return rcopy(source, target, i_send, i, chip(z + way, q))

        def compute(self, w, extra):
            for far in (1, 0):
                m = upper_half + far - 2 * upper_half * far
                at = pl.ds(mult(m * half, LANES), half)
                back_rows(w, extra, at, at)
                for i in range(hz):
                    zz = m * hz + i
                    r = self.rows(zz, other)
                    self.part[r, :] = big[r, :].astype(BF16)
                    self.to_sib(zz).start()

        def fold(self, zz):
            self.to_sib(zz).wait_recv()
            return big[self.rows(zz, q), :] + self.sibs[zz].astype(F32)

        def send_dist(self, dist):
            for way in (1, -1):
                zz = z + way * dist

                @pl.when(inside(zz))
                def _():
                    total = self.fold(zz)
                    if dist >= 2:
                        big[self.rows(zz, q), :] = total

                        @pl.when(inside(z - way))
                        def _():
                            v, i = self.comb(way, dist)
                            rcopy(v, v, i, i, {"ch": sib}).wait_recv()
                            big[self.rows(zz, q), :] += v[...].astype(F32)

                        total = big[self.rows(zz, q), :]
                    self.part[self.rows(zz, q), :] = total.astype(BF16)
                    self.out(way, dist).start()

        def send(self):
            for dist in list(range(nz - 1, 2, -1)) + [1]:
                self.send_dist(dist)
            hold[0] = self.fold(z)

        def end(self):
            for dist in (1, 2):
                for way in (1, -1):

                    @pl.when(inside(z - way * dist))
                    def _():
                        at = self.slot(way, dist)
                        v = self.recv.at[at]
                        rcopy(v, v, self.base + at, self.base + at, {"ch": sib}).wait_recv()
                        hold[0] += v[...].astype(F32)

            self.drain()

        def drain(self):
            for d in range(nz):
                self.to_sib(lax.rem(z + d, nz)).wait_send()
            for way in (1, -1):
                for dist in range(1, nz):

                    @pl.when(inside(z + way * dist))
                    def _():
                        self.out(way, dist).wait_send()

    rows_all = nz * C

    def plane_rows(body, straight=False):
        if straight:
            for zz in range(nz):
                body(zz * C, zz, pl.ds(0, C))
            return

        def step(zz, carry):
            body(mult(zz * C), zz, pl.ds(0, C))
            return carry

        lax.fori_loop(0, nz, step, 0)


    def plane_sums(body, slot, groups):
        def run(row, zz, r):
            total = tree(body(row))
            if slot > 0:
                lane_mod = lax.broadcasted_iota(jnp.int32, total.shape, 1) % 32
                total = jnp.where(lane_mod == slot, pltpu.roll(total, slot, 1), pcol[zz, r, :])
            pcol[zz, r, :] = total

        plane_rows(run, True)

    def at_slot(i, body):
        chips = [zc for zc in range(nz) if len(pn.srcs[zc]) > i]
        pl.when(functools.reduce(jnp.logical_or, [z == zc for zc in chips]))(body)

    def plane_copies(p):
        v = psums.at[p, b]
        for d in range(1, nb):
            bb = lax.rem(b + d, nb)
            yield bb, rcopy(v, v, pn.s_plane[p] + bb, pn.s_plane[p] + b, {"batch": bb})

    def plane_start(p, groups):
        for zz in range(nz):
            prow[zz] = pcol[zz].T
            for n in range(groups):
                psums[p, b, zz, 4 * n : 4 * n + 4, :] = prow[zz, 32 * n : 32 * n + 4, :]
        for _, cp in plane_copies(p):
            cp.start()

    def plane_finish(p):
        for bb, _ in plane_copies(p):
            v = psums.at[p, bb]
            rcopy(v, v, pn.s_plane[p] + bb, pn.s_plane[p] + bb, {"batch": bb}).wait_recv()
        total = psums[p, 0]
        for bb in range(1, nb):
            total = total + psums[p, bb]
        return total

    def project(zc, s):
        at, width = pn.pieces[s]
        place = at - pn.lo[zc]
        for blk in (0, 1):
            big[blk * rows_all : (blk + 1) * rows_all, :] = dot(
                rp[blk, :, place : place + width], src[at : at + width, :]
            )

    def project_slot(i):
        def run(zc):
            if len(pn.srcs[zc]) > i:
                project(zc, pn.srcs[zc][i])

        at_chip(run)

    def plane_first():
        for i in range(pn.slots):
            project_slot(i)

            def parts(row):
                lo = big[pl.ds(row, C), :]
                up = big[pl.ds(rows_all + row, C), :]
                return [lo, lo * lo, up, up * up]

            at_slot(i, lambda: plane_sums(parts, i, 4))

    def base(blk, i):
        return blk * 4 + i

    def plane_norms(zc, total):
        for blk in (0, 1):
            shift_sum = None
            for i, s in enumerate(pn.srcs[zc]):
                gain, shift = prms[:, 2 * blk, 2 + s, :], prms[:, 2 * blk + 1, 2 + s, :]
                p_av, p_rsd, p_sc, _ = norm_rows(total[:, 8 * blk + i], total[:, 8 * blk + 4 + i], count, gain, shift)
                pk[:, base(blk, i), :] = p_rsd
                pk[:, 8 + base(blk, i), :] = p_av
                pk[:, 16 + base(blk, i), :] = gain
                pk[:, 48 + base(blk, i), :] = p_sc
                shift_sum = shift if shift_sum is None else shift_sum + shift
            pk[:, 24 + blk, :] = shift_sum
        for zz in range(nz):
            prow[zz] = pk[zz].T

    def plane_col(zz, r, n):
        return prow[zz, r, n : n + 1]

    def plane_values():
        for i in range(pn.slots):
            project_slot(i)

            def scale(row, zz, r):
                for blk in (0, 1):
                    v = big[pl.ds(mult(blk * rows_all + row), C), :]
                    v = (v - plane_col(zz, r, 8 + base(blk, i))) * plane_col(zz, r, base(blk, i))
                    pr[i, blk, pl.ds(row, C), :] = v.astype(BF16)
                    v = v * plane_col(zz, r, 16 + base(blk, i))
                    if i == 0:
                        v = v + plane_col(zz, r, 24 + blk)
                    else:
                        v = v + qpart[blk, pl.ds(row, C), :].astype(F32)
                    qpart[blk, pl.ds(row, C), :] = v.astype(BF16)

            at_slot(i, lambda: plane_rows(scale))

    def q_send(blk):
        def send(zc):
            for zz in range(nz):
                if zz != zc:
                    q_copy(blk, zz).start()
            qrecv[blk, zc] = qpart[blk, zc * C : (zc + 1) * C, :]

        at_chip(send)

    def q_copy(blk, zz):
        i = pn.s_q + blk * nz
        return rcopy(qpart.at[blk, zz * C : (zz + 1) * C], qrecv.at[blk, z], i + zz, i + z, chip(zz, q))

    def q_finish(blk):
        for zc in range(nz):
            if pn.srcs[zc]:

                @pl.when(z != zc)
                def _():
                    v = qrecv.at[blk, zc]
                    i = pn.s_q + blk * nz + zc
                    rcopy(v, v, i, i, {"ch": sib}).wait_recv()

    def q_sum(blk, r, v):
        for zc in range(nz):
            if pn.srcs[zc]:
                v = v + qrecv[blk, zc, r, :].astype(F32)
        return v

    ld_w0.wait()
    ld_w0l.wait()
    ld_w0u.wait()
    conv(w0, src[HEAD : HEAD + PRE, :], 0, resid)
    conv_sums(0)
    sum_start(0, 2, jnp.broadcast_to(length.astype(F32), (1, LANES)))
    r_hops(-1, lambda cp: cp.start())
    others(lambda zz: prm_copy(zz).start())
    for zc, qq, row, n in pn.bound:

        @pl.when((z == zc) & (q == qq))
        def _():
            bound_hop(row, n).wait_recv()
            bound_sib(row, n).start()

    at_chip(r_arrive)
    total = sum_finish(0)
    count = jnp.broadcast_to(total[2:3, 0:1], (1, LANES))
    av, rsd, sc, off = norm_rows(total[0:1], total[1:2], count, prm[0, 0:1], prm[1, 0:1])
    columns(0, [sc, off, av, rsd])

    def activate(p, y_index, out):
        def body(r):
            v = ys[y_index, r, :] * kcol[p, r, 0:1] + kcol[p, r, 1:2]
            out[at_row(c * C, r), :] = (v * squash(v) * valid_rb).astype(BF16)

        blocks(body)

    activate(0, 0, x1)
    gx1 = Gather(pn.s_x[0], x1, C)
    gx1.start()
    for zc, qq, row, n in pn.bound:

        @pl.when((z == zc) & (q != qq))
        def _():
            bound_sib(row, n).wait_recv()

    sized(sib, lambda n: own_rows(sib, n).wait_recv())
    gx1.arrive()
    at_chip(r_finish)
    plane_first()
    plane_start(0, 4)
    gx1.end()
    ld_w1.wait()
    conv(w1, x1[...], 1)

    def first_sums(r):
        y = ys[1, r, :] * valid_rb
        lo, up = resid[r, :], resid[at_row(C, r), :]
        pack_sums(r, [y, y * y, lo, lo * lo, up, up * up])

    blocks(first_sums)
    sum_start(1, 6)
    others(prm_arrive)
    plane_total = plane_finish(0)
    at_chip(lambda zc: plane_norms(zc, plane_total))
    plane_values()
    q_send(0)
    total = sum_finish(1)
    l1 = norm_rows(total[0:1], total[1:2], count, prm[0, 1:2], prm[1, 1:2])
    l8 = norm_rows(total[2:3], total[3:4], count, prm[0, 10:11], prm[1, 10:11])
    u8 = norm_rows(total[4:5], total[5:6], count, prm[2, 10:11], prm[3, 10:11])
    columns(1, [l1[2], l8[2], l1[0], l8[0], l1[3] + l8[3]])
    q_finish(0)

    def lower_out(r):
        v = ys[1, r, :] * kcol[1, r, 0:1] + kcol[1, r, 4:5] + resid[r, :] * kcol[1, r, 1:2]
        v = q_sum(0, r, v)
        hold[1, r, :] = v
        x2[at_row(c * C, r), :] = (v * squash(v) * valid_rb).astype(BF16)

    blocks(lower_out)
    gx2 = Gather(pn.s_x[1], x2, C)
    gx2.start()
    slice_start(1)
    slice_start(0)
    gx2.arrive()
    gx2.end()
    q_send(1)
    ld_w2.wait()
    ld_w2m.wait()
    conv(w2, x2[...], 2, rmid)

    def mid_sums(r):
        y = ys[2, r, :] * valid_rb
        v = rmid[r, :]
        pack_sums(r, [y, y * y, v, v * v])

    blocks(mid_sums)
    sum_start(2, 4)
    total = sum_finish(2)
    u2 = norm_rows(total[0:1], total[1:2], count, prm[2, 0:1], prm[3, 0:1])
    mid = norm_rows(total[2:3], total[3:4], count, prm[2, 11:12], prm[3, 11:12])
    columns(2, [u2[2], u2[3], u2[0], u2[1]])
    activate(2, 2, x3)
    gx3 = Gather(pn.s_x[2], x3, C)
    gx3.start()
    slice_start(2)
    gx3.arrive()
    gx3.end()
    ld_w3.wait()
    conv(w3, x3[...], 3)
    conv_sums(3)
    sum_start(3, 2)
    q_finish(1)
    total = sum_finish(3)
    u3 = norm_rows(total[0:1], total[1:2], count, prm[2, 1:2], prm[3, 1:2])
    columns(3, [u3[2], u8[2], mid[2], u3[0], u8[0], mid[0], u3[3] + u8[3] + mid[3]])

    def value_back(v, gradient):
        s = squash(v)
        return gradient * valid_rb * s * (1.0 + v * (1.0 - s))

    def upper_out(r):
        up = resid[at_row(C, r), :]
        v = ys[3, r, :] * kcol[3, r, 0:1] + kcol[3, r, 6:7] + up * kcol[3, r, 1:2] + rmid[r, :] * kcol[3, r, 2:3]
        v = q_sum(1, r, v)
        final_ref[r, :] = (v * squash(v) * valid_rb).astype(BF16)
        dv = value_back(v, cot_ref[r, :].astype(F32))
        hold[2, r, :] = dv
        dvx[1, at_row(z * C, r), :] = dv.astype(BF16)
        parts = [dv]
        for n, x in enumerate((ys[3, r, :], up, rmid[r, :])):
            parts.append(dv * (x - kcol[3, r, 3 + n : 4 + n]))
        pack_sums(r, parts)

    blocks(upper_out)

    def dv_copy(blk, zz):
        v = dvx.at[blk, pl.ds(mult(z * C), C)]
        return rcopy(v, v, pn.s_dv + blk * nz + zz, pn.s_dv + blk * nz + z, chip(zz, q))

    def dv_copies(blk, act):
        for zz in range(nz):
            if pn.srcs[zz]:

                @pl.when(z != zz)
                def _():
                    act(dv_copy(blk, zz))

    def plane_back(blk, p):
        def wait(zc):
            for zf in range(nz):
                if zf != zc:
                    v = dvx.at[blk, zf * C : (zf + 1) * C]
                    i = pn.s_dv + blk * nz + zf
                    rcopy(v, v, i, i, {"ch": sib}).wait_recv()

        at_chip(wait)
        counts = sorted({len(x) for x in pn.srcs} - {0})
        for many in counts:

            def parts(row):
                dv = dvx[blk, pl.ds(row, C), :].astype(F32)
                found = [dv * pr[i, blk, pl.ds(row, C), :].astype(F32) for i in range(many)]
                return [dv] + found + [None] * (3 - many)

            chips = [z == zc for zc in range(nz) if len(pn.srcs[zc]) == many]
            pl.when(functools.reduce(jnp.logical_or, chips))(lambda: plane_sums(parts, 0, 4))
        plane_start(p, 4)

    def gain_copy(blk, zz):
        i = pn.s_gain + blk * nz
        return rcopy(gsend.at[blk, zz], grecv.at[blk, z], i + zz, i + z, chip(zz, q))

    def plane_coefficients(blk, total):
        def run(zc):
            dv_sum = total[:, 0]
            for i in range(len(pn.srcs[zc])):
                g = total[:, 4 * (i + 1)]
                gsend[blk, :, i, :] = g
                p_sc = pk[:, 48 + base(blk, i), :]
                pk[:, 32 + base(blk, i), :] = p_sc * dv_sum / count
                pk[:, 40 + base(blk, i), :] = p_sc * g / count
            for zz in range(nz):
                prow[zz] = pk[zz].T
                if zz != zc:
                    gain_copy(blk, zz).start()
            grecv[blk, zc] = gsend[blk, zc]

        at_chip(run)

    def plane_dr(blk):
        def run(zc):
            def body(row, zz, r):
                dv = dvx[blk, pl.ds(row, C), :].astype(F32)
                for i in range(len(pn.srcs[zc])):
                    n = base(blk, i)
                    v = pr[i, blk, pl.ds(row, C), :].astype(F32)
                    v = plane_col(zz, r, 48 + n) * dv - (
                        plane_col(zz, r, 32 + n) + plane_col(zz, r, 40 + n) * v
                    )
                    drp[i, blk, pl.ds(row, C), :] = (v * valid).astype(BF16)

            plane_rows(body)

        at_chip(run)

    def unit_copy(blk, u):
        i = pn.s_d1[blk]
        target = d1recv.at[blk, b, u // nb]
        return rcopy(d1send.at[u], target, i + u, i + b * pn.nu + u, {"batch": u % nb})

    def unit_grads(blk):
        def run(zc):
            for i, s in enumerate(pn.srcs[zc]):
                at, width = pn.pieces[s]
                grad = dot_last(drp[i, blk], src[at : at + width, :])
                first = (at - pn.lo[zc]) // LANES
                for n in range(width // LANES):
                    d1send[first + n] = grad[:, n * LANES : (n + 1) * LANES].astype(BF16)

        at_chip(run)

    def unit_send(blk):
        def run(zc):
            for u in range(pn.width[zc] // LANES):

                @pl.when(b != u % nb)
                def _():
                    unit_copy(blk, u).start()

        at_chip(run)

    def unit_drain(blk):
        def run(zc):
            for u in range(pn.width[zc] // LANES):

                @pl.when(b != u % nb)
                def _():
                    unit_copy(blk, u).wait_send()

        at_chip(run)

    def unit_blocks(blk, zc, u):
        col = pn.lo[zc] + u * LANES
        return list(range(col // pn.share(blk), (col + LANES - 1) // pn.share(blk) + 1))

    def unit_number(zc, u):
        return [n for n, (a, e, _) in enumerate(pn.units) if (a, e) == (zc, u)][0]

    def result_copies(blk, zc, u, act_far, act_own):
        k = u // nb
        number = unit_number(zc, u)
        for zz in range(nz):
            for jj, j in enumerate(unit_blocks(blk, zc, u)):
                source = d2send.at[blk, k, zz * C : (zz + 1) * C]
                cp = rcopy(
                    source,
                    d2recv.at[blk, number],
                    pn.s_d2[blk] + (k * nz + zz) * 2 + jj,
                    pn.s_d2[blk] + number,
                    {"batch": j, "ch": zz * 2 + q},
                )
                if zz == zc and j == u % nb:
                    if act_own is not None:
                        act_own(number, k, zz)
                else:
                    act_far(cp)

    def unit_finish(blk):
        def run(zc):
            for u in range(pn.width[zc] // LANES):

                @pl.when(b == u % nb)
                def _():
                    total = d1send[u].astype(F32)
                    for d in range(1, nb):
                        bb = lax.rem(b + d, nb)
                        v = d1recv.at[blk, bb, u // nb]
                        i = pn.s_d1[blk] + bb * pn.nu + u
                        rcopy(v, v, i, i, {"ch": sib}).wait_recv()
                        total = total + d1recv[blk, bb, u // nb].astype(F32)
                    d2send[blk, u // nb] = total.astype(BF16)

                    def keep(number, k, zz):
                        d2recv[blk, number] = d2send[blk, k, zz * C : (zz + 1) * C, :]

                    result_copies(blk, zc, u, lambda cp: cp.start(), keep)

        at_chip(run)

    def result_drain(blk):
        def run(zc):
            for u in range(pn.width[zc] // LANES):

                @pl.when(b == u % nb)
                def _():
                    result_copies(blk, zc, u, lambda cp: cp.wait_send(), None)

        at_chip(run)

    def result_finish(blk, out):
        share = pn.share(blk)
        for j in range(nb):

            @pl.when(b == j)
            def _():
                for number, (zc, u, ub) in enumerate(pn.units):
                    col = pn.lo[zc] + u * LANES
                    lo_c, hi_c = max(col, j * share), min(col + LANES, (j + 1) * share)
                    if lo_c >= hi_c:
                        continue
                    v = d2recv.at[blk, number]
                    i = pn.s_d2[blk] + number
                    arrived = rcopy(v, v, i, i, {"ch": sib})
                    if ub == j:

                        @pl.when(z != zc)
                        def _():
                            arrived.wait_recv()

                    else:
                        arrived.wait_recv()
                    out[:, lo_c - j * share : hi_c - j * share] = d2recv[blk, number][
                        :, lo_c - col : hi_c - col
                    ].astype(F32)

    sum_start(4, 4)
    dv_copies(1, lambda cp: cp.start())
    total = sum_finish(4)
    slice_start(3)
    upper_q = total[0:1]
    upper_rsd = jnp.concatenate([u3[1], u8[1], mid[1]], axis=0)
    upper_sc = jnp.concatenate([u3[2], u8[2], mid[2]], axis=0)
    upper_g = total[1:4] * upper_rsd
    usg_ref[1:12, :] = jnp.broadcast_to(upper_q[:, 0:C], (11, C))
    ugg_ref[1:2, :] = upper_g[0:1, 0:C]
    ugg_ref[10:12, :] = upper_g[1:3, 0:C]
    columns(4, [upper_sc * upper_q / count, upper_sc * upper_rsd * upper_g / count])

    def grad_rows(gradient, values, sc_col, av_col, a_col, b_col):
        return ((sc_col * gradient - (a_col + b_col * (values - av_col))) * valid_rb).astype(BF16)

    own_lanes = pl.ds(mult(b * T, LANES), T)

    def upper_grad(r, values, n):
        return grad_rows(
            hold[2, r, :],
            values,
            kcol[3, r, n : n + 1],
            kcol[3, r, 3 + n : 4 + n],
            kcol[4, r, n : n + 1],
            kcol[4, r, 3 + n : 4 + n],
        )

    def upper_dy(r):
        dyg[3, r, own_lanes] = upper_grad(r, ys[3, r, :], 0)

    blocks(upper_dy)
    gx1.drain()
    for _, cp in slice_copies(1):
        cp.wait_send()
    shift_all(3)
    sc0 = Scatter(0)
    sc0.compute(w3, 0)
    sc0.send()
    dy_start(3)
    sc0.send_dist(2)

    def upper_dr(r):
        dr8[at_row(C, r), :] = upper_grad(r, resid[at_row(C, r), :], 1)
        dbuf[at_row(K * C, r), :] = upper_grad(r, rmid[r, :], 2)

    blocks(upper_dr)

    def dense_stage(n, first_col, value):
        share = pn.share(n)
        end = first_col + value.shape[1]
        for k, bb in enumerate(pn.dense_owners(n)):
            lo_c, hi_c = max(first_col, bb * share), min(end, (bb + 1) * share)
            if lo_c < hi_c:
                drs[n, k, :, lo_c - bb * share : hi_c - bb * share] = value[
                    :, lo_c - first_col : hi_c - first_col
                ].astype(BF16)

    def dense_cut(n, bb):
        first = max(HEAD - bb * pn.share(n), 0)
        return first, first // LANES * LANES

    def dense_copy(n, k, bb):
        tile = dense_cut(n, bb)[1]
        i = pn.s_dr[n]
        return rcopy(drs.at[n, k, :, tile:], drr.at[n, b, :, tile:], i + bb, i + b, {"batch": bb})

    def dense_copies(n, act):
        for k, bb in enumerate(pn.dense_owners(n)):

            @pl.when(b != bb)
            def _():
                act(dense_copy(n, k, bb))

    def dense_finish(n, out):
        share = pn.share(n)
        for k, bb in enumerate(pn.dense_owners(n)):

            @pl.when(b == bb)
            def _():
                first, tile = dense_cut(n, bb)
                total = drs[n, k, :, first:share].astype(F32)
                for d in range(1, nb):
                    other_b = lax.rem(b + d, nb)
                    v = drr.at[n, other_b, :, tile:]
                    i = pn.s_dr[n] + other_b
                    rcopy(v, v, i, i, {"ch": sib}).wait_recv()
                    total = total + drr[n, other_b, :, first:share].astype(F32)
                out[:, first:share] = total

    dense_stage(1, HEAD, dot_last(dr8[C : 2 * C, :], src[HEAD : HEAD + PRE, :]))
    dense_stage(1, HEAD + PRE, dot_last(dbuf[K * C : (K + 1) * C, :], x2[...]))
    plane_back(1, 1)
    sc0.end()

    def inner_back(p, y_index):
        def body(r):
            y = ys[y_index, r, :]
            dz = value_back(y * kcol[p, r, 0:1] + kcol[p, r, 1:2], hold[0, r, :])
            hold[3, r, :] = dz
            pack_sums(r, [dz, dz * (y - kcol[p, r, 2:3])])

        blocks(body)

    def inner_dy(p, kept, y_index):
        def body(r):
            dyg[y_index, r, own_lanes] = grad_rows(
                hold[3, r, :], ys[y_index, r, :], kcol[kept, r, 0:1], kcol[kept, r, 2:3], kcol[p, r, 0:1], kcol[p, r, 1:2]
            )

        blocks(body)

    inner_back(2, 2)
    sum_start(5, 2)
    plane_total = plane_finish(1)
    plane_coefficients(1, plane_total)
    total = sum_finish(5)
    dense_copies(1, lambda cp: cp.start())
    inner_q, inner_g = total[0:1], total[1:2] * u2[1]
    usg_ref[0:1, :] = inner_q[:, 0:C]
    ugg_ref[0:1, :] = inner_g[:, 0:C]
    columns(5, [u2[2] * inner_q / count, u2[2] * u2[1] * inner_g / count])
    inner_dy(5, 2, 2)
    shift_all(2)
    sc1 = Scatter(1)
    sc1.compute(w2, 1)
    sc1.send()
    dy_start(2)
    plane_dr(1)
    sc1.send_dist(2)
    unit_grads(1)
    weight_grad(3, g23_hbm, K * C)
    sc1.end()

    def lower_back(r):
        v = hold[1, r, :]
        dv = value_back(v, hold[0, r, :])
        hold[2, r, :] = dv
        dvx[0, at_row(z * C, r), :] = dv.astype(BF16)
        pack_sums(r, [dv, dv * (ys[1, r, :] - kcol[1, r, 2:3]), dv * (resid[r, :] - kcol[1, r, 3:4])])

    blocks(lower_back)
    sum_start(6, 3)
    dv_copies(0, lambda cp: cp.start())
    total = sum_finish(6)
    unit_send(1)
    lower_q = total[0:1]
    lower_rsd = jnp.concatenate([l1[1], l8[1]], axis=0)
    lower_sc = jnp.concatenate([l1[2], l8[2]], axis=0)
    lower_g = total[1:3] * lower_rsd
    lsg_ref[1:11, :] = jnp.broadcast_to(lower_q[:, 0:C], (10, C))
    lgg_ref[1:2, :] = lower_g[0:1, 0:C]
    lgg_ref[10:11, :] = lower_g[1:2, 0:C]
    columns(6, [lower_sc * lower_q / count, lower_sc * lower_rsd * lower_g / count])

    def lower_grad(r, values, n):
        return grad_rows(
            hold[2, r, :],
            values,
            kcol[1, r, n : n + 1],
            kcol[1, r, 2 + n : 3 + n],
            kcol[6, r, n : n + 1],
            kcol[6, r, 2 + n : 3 + n],
        )

    def lower_dy(r):
        dyg[1, r, own_lanes] = lower_grad(r, ys[1, r, :], 0)

    blocks(lower_dy)
    shift_all(1)
    sc2 = Scatter(2)
    sc2.compute(w1, 0)
    sc2.send()
    dy_start(1)
    sc2.send_dist(2)

    def lower_dr(r):
        dr8[r, :] = lower_grad(r, resid[r, :], 1)

    blocks(lower_dr)
    dense_stage(0, HEAD, dot_last(dr8[0:C, :], src[HEAD : HEAD + PRE, :]))
    dense_copies(0, lambda cp: cp.start())
    plane_back(0, 2)
    weight_grad(2, g23_hbm, 0)
    unit_drain(1)
    unit_finish(1)
    sc2.end()

    inner_back(0, 0)
    sum_start(7, 2)
    plane_total = plane_finish(2)
    plane_coefficients(0, plane_total)
    weight_grad(1, g1_hbm, 0, [0, 1])
    total = sum_finish(7)
    inner_q, inner_g = total[0:1], total[1:2] * rsd
    lsg_ref[0:1, :] = inner_q[:, 0:C]
    lgg_ref[0:1, :] = inner_g[:, 0:C]
    columns(7, [sc * inner_q / count, sc * rsd * inner_g / count])
    inner_dy(7, 0, 0)
    shift_all(0)
    dbuf[K * C : (K + 2) * C, :] = dr8[...]
    split = (PRE // 2 + LANES - 1) // LANES * LANES
    back_rows(w0, 2, slice(0, split), slice(0, split))
    back_rows(w0, 2, slice(split, PRE), slice(split, PRE))
    dy_start(0)

    def dp_sib(lc, n, k):
        v = dpo.at[lc : lc + n]
        i = pn.s_dp + 1 + k
        return rcopy(v, dpsib.at[lc : lc + n], i, i, {"ch": sib})

    def dp_bound(lc, n):
        return rcopy(dpo.at[lc : lc + n], dpbnd.at[0:n], pn.s_dp, pn.s_dp, below)

    def dp_compute(zc):
        for i, s in enumerate(pn.srcs[zc]):
            at, width = pn.pieces[s]
            lc = at - pn.lo[zc]
            r = rp[:, :, lc : lc + width].reshape(2 * rows_all, width)
            grad = dot_first(r, drp[i].reshape(2 * rows_all, T))
            dpo[lc : lc + width, :] = grad.astype(BF16)
        for k, (owner, row, n) in enumerate(pn.final[zc]):

            @pl.when(q != owner % 2)
            def _():
                dp_sib(row - pn.lo[zc], n, k).start()

    def dp_add(zc):
        for k, (owner, row, n) in enumerate(pn.final[zc]):
            lc = row - pn.lo[zc]

            @pl.when(q == owner % 2)
            def _():
                dp_sib(lc, n, k).wait_recv()
                total = dpo[lc : lc + n, :].astype(F32) + dpsib[lc : lc + n, :].astype(F32)
                if owner // 2 == zc:
                    at = WIDE + row - owner * E
                    big[at : at + n, :] = total * valid
                else:
                    dpo[lc : lc + n, :] = total.astype(BF16)
                    dp_bound(lc, n).start()

    def dp_drain(zc):
        for k, (owner, row, n) in enumerate(pn.final[zc]):
            lc = row - pn.lo[zc]

            @pl.when(q != owner % 2)
            def _():
                dp_sib(lc, n, k).wait_send()

            if owner // 2 != zc:

                @pl.when(q == owner % 2)
                def _():
                    dp_bound(lc, n).wait_send()

    count_late = len(pn.late)
    gx3.drain()
    for _, cp in slice_copies(3):
        cp.wait_send()

    def tail_rows(n):
        return x3.at[pn.late[n][2] - HEAD : pn.late[n][2] - HEAD + pn.step]

    def tail_sib(n):
        return rcopy(tail_rows(n), tailsib.at[n], pn.s_tail + n, pn.s_tail + n, {"ch": sib})

    def tail_hop(n, way, device):
        i = pn.s_tail + (1 + way) * count_late + n
        return rcopy(tail_rows(n), tailrecv.at[way, n], i, i, device)

    for n in range(count_late):
        there = slice(pn.late[n][2] - HEAD, pn.late[n][2] - HEAD + pn.step)

        @pl.when(q != pn.late[n][1])
        def _():
            x3[there, :] = big[there, :].astype(BF16)
            tail_sib(n).start()

    before, after = [], [True] * count_late
    for n in range(count_late):
        same = [m for m in range(n) if pn.late[m][:2] == pn.late[n][:2]]
        before.append(same[-pn.flight] if len(same) >= pn.flight else None)
        if len(same) >= pn.flight:
            after[same[-pn.flight]] = False

    work = [
        lambda: plane_dr(0),
        lambda: at_chip(dp_compute),
        lambda: (unit_grads(0), unit_send(0)),
        lambda: weight_grad(1, g1_hbm, 0, [2]),
        lambda: weight_grad(1, g1_hbm, 0, [3]),
        lambda: at_chip(dp_add),
        lambda: weight_grad(1, g1_hbm, 0, [4]),
        lambda: weight_grad(0, g0_hbm, 0, [0]),
        lambda: weight_grad(0, g0_hbm, 0, [1]),
    ]
    apart = max(count_late // (len(work) + 1), 1)
    for n in range(count_late):
        zc, qc, row = pn.late[n]
        there = slice(row - HEAD, row - HEAD + pn.step)

        @pl.when(q == qc)
        def _():
            tail_sib(n).wait_recv()
            big[there, :] += tailsib[n].astype(F32)
            if zc > 0:

                @pl.when((z > 0) & (z <= zc))
                def _():
                    tail_hop(n, 0, above).wait_recv()
                    big[there, :] += tailrecv[0, n].astype(F32)

            if zc < nz - 1:

                @pl.when((z < nz - 1) & (z >= zc))
                def _():
                    tail_hop(n, 1, below).wait_recv()
                    big[there, :] += tailrecv[1, n].astype(F32)

            @pl.when(z < zc)
            def _():
                x3[there, :] = big[there, :].astype(BF16)
                if before[n] is not None:
                    tail_hop(before[n], 0, above).wait_send()
                tail_hop(n, 0, above).start()

            if zc < nz - 1:

                @pl.when(z > zc)
                def _():
                    x3[there, :] = big[there, :].astype(BF16)
                    if before[n] is not None:
                        tail_hop(before[n], 1, below).wait_send()
                    tail_hop(n, 1, below).start()

            @pl.when(z == zc)
            def _():
                big[WIDE + row % E : WIDE + row % E + pn.step, :] = big[there, :] * valid

        if n % apart == apart - 1 and work:
            work.pop(0)()
    while work:
        work.pop(0)()

    for zc, qq, row, n in pn.bound:

        @pl.when((z == zc - 1) & (q == qq))
        def _():
            dp_v = dpbnd.at[0:n]
            rcopy(dp_v, dp_v, pn.s_dp, pn.s_dp, above).wait_recv()
            at = WIDE + row % E
            big[at : at + n, :] = dpbnd[0:n, :].astype(F32) * valid

    egrad_copy = pltpu.make_async_copy(big.at[WIDE : WIDE + E], egrad_hbm, osem.at[4])
    egrad_copy.start()
    weight_grad(0, g0_hbm, 0, [2])
    unit_finish(0)
    weight_grad(0, g0_hbm, 0, range(3, K // pn.group))
    result_finish(1, rug_ref)
    dense_finish(1, rug_ref)
    for blk, ref in ((0, lgg_ref), (1, ugg_ref)):
        for zc in range(nz):
            if pn.srcs[zc]:
                gain_v = grecv.at[blk, zc]

                @pl.when(z != zc)
                def _():
                    i = pn.s_gain + blk * nz + zc
                    rcopy(gain_v, gain_v, i, i, {"ch": sib}).wait_recv()

                for i, s in enumerate(pn.srcs[zc]):
                    ref[2 + s : 3 + s, :] = grecv[blk, zc, i : i + 1, 0:C]
    dense_finish(0, rlg_ref)
    result_finish(0, rlg_ref)

    out_copies[-1].wait()
    egrad_copy.wait()
    entry_drain()
    sized(c, lambda n: own_rows(c, n).wait_send())
    for zc, qq, row, n in pn.bound:

        @pl.when((z == zc - 1) & (q == qq))
        def _():
            bound_hop(row, n).wait_send()

        @pl.when((z == zc) & (q == qq))
        def _():
            bound_sib(row, n).wait_send()

    r_hops(1, lambda cp: cp.wait_send())
    r_hops(-1, lambda cp: cp.wait_send())
    at_chip(r_drain)
    others(lambda zz: prm_copy(zz).wait_send())

    def q_drain(zc):
        for blk in (0, 1):
            for zz in range(nz):
                if zz != zc:
                    q_copy(blk, zz).wait_send()
                    gain_copy(blk, zz).wait_send()

    at_chip(q_drain)
    at_chip(dp_drain)
    for blk in (0, 1):
        dv_copies(blk, lambda cp: cp.wait_send())
        dense_copies(blk, lambda cp: cp.wait_send())
        result_drain(blk)
    unit_drain(0)
    gx2.drain()
    for p in range(8):
        for _, cp in sum_copies(p):
            cp.wait_send()
    for p in range(3):
        for _, cp in plane_copies(p):
            cp.wait_send()
    for j in range(4):
        if j not in (1, 3):
            for _, cp in slice_copies(j):
                cp.wait_send()
        for _, cp in dy_copies(j):
            cp.wait_send()
    for n in range(count_late):
        zc, qc, _ = pn.late[n]

        @pl.when(q != qc)
        def _():
            tail_sib(n).wait_send()

        if after[n]:

            @pl.when((q == qc) & (z < zc))
            def _():
                tail_hop(n, 0, above).wait_send()

        if after[n] and zc < nz - 1:

            @pl.when((q == qc) & (z > zc))
            def _():
                tail_hop(n, 1, below).wait_send()


def per_device(
    nb,
    nc,
    earlier,
    lengths,
    lower_entry,
    lower_convs,
    upper_convs,
    lower_dense,
    upper_dense,
    lower_gain,
    lower_shift,
    upper_gain,
    upper_shift,
    cotangent,
):
    _, own, frames = earlier.shape
    taps, cw, pre = lower_entry.shape
    pn = Plan(nb, nc, own, frames, taps, cw, pre)
    T, K, C, E, WIDE, nz = frames, taps, cw, own, pn.wide, pn.nz
    late = len(pn.late)
    share = ((pn.all + WIDE) // nb + LANES - 1) // LANES * LANES
    w0p, wp = up16(pn.iw0), up16(pn.iw)
    staged = 4 if (w0p != pn.iw0 or wp != pn.iw) else 1
    vmem, any_ = pl.BlockSpec(memory_space=pltpu.VMEM), pl.BlockSpec(memory_space=pl.ANY)
    smem = pl.BlockSpec(memory_space=pltpu.SMEM)
    V = pltpu.VMEM
    scratch = [
        V(((K + 2) * C, pre), BF16),
        V((K * C, WIDE), BF16),
        V(((K + 1) * C, WIDE), BF16),
        V((K * C, WIDE), BF16),
        V((2, nz * C, pn.pw), BF16),
        V((C // (pn.split // 2), pn.head), BF16),
        V((pn.all, T), BF16),
        V((WIDE, T), BF16),
        V((WIDE, T), BF16),
        V((WIDE, T), BF16),
        V((WIDE + E, T), F32),
        V((2 * C, T), F32),
        V((C, T), F32),
        V((4, C, T), F32),
        V(((K + 2) * C, T), BF16),
        V((pn.slots, 2, nz * C, T), BF16),
        V((pn.slots, 2, nz * C, T), BF16),
        V((2 * C, T), BF16),
        V((2, nz * C, T), BF16),
        V((2, nz, C, T), BF16),
        V((2, nz * C, T), BF16),
        V((2, nz, 8, LANES), F32),
        V((2, nz, 8, LANES), F32),
        V((max(pn.pw, E), T), BF16),
        V((pn.pw, T), BF16),
        V((max([n for _, _, _, n in pn.bound] + [16]), T), BF16),
        V((pn.nu, nz * C, LANES), BF16),
        V((2, nb, pn.ku, nz * C, LANES), BF16),
        V((2, pn.ku, nz * C, LANES), BF16),
        V((2, len(pn.units), C, LANES), BF16),
        V((3, nz, C, T), BF16),
        V((3, 4, C, T), BF16),
        V((3, max(nz - 3, 1) * (2 if nz > 4 else 1), C, T), BF16),
        V((late, pn.step, T), BF16),
        V((1 + (pn.late[0][0] < nz - 1), late, pn.step, T), BF16),
        V((4, C, nb * T), BF16),
        V((w0p, nb * T), BF16),
        V((3, wp, nb * T), BF16),
        V((4, nb, max(w0p, wp), T) if staged == 4 else (1, 1, 16, T), BF16),
        V((2, len(pn.dense_owners(1)), C, share), BF16),
        V((2, nb, C, share), BF16),
        V((8, nb, 40, LANES), F32),
        V((LANES, LANES), F32),
        V((LANES, LANES), F32),
        V((8, LANES, LANES), F32),
        V((3, nb, nz, 16, LANES), F32),
        V((nz, LANES, LANES), F32),
        V((nz, LANES, LANES), F32),
        V((nz, LANES, LANES), F32),
        V((nz, 4, 16, LANES), F32),
        V((4, C, T), F32),
        V((K * C, pn.iw), F32),
        pltpu.SemaphoreType.DMA((11,)),
        pltpu.SemaphoreType.DMA((5,)),
        pltpu.SemaphoreType.DMA((pn.sems,)),
        pltpu.SemaphoreType.DMA((pn.sems,)),
    ]
    shape = jax.ShapeDtypeStruct
    outs = pl.pallas_call(
        functools.partial(kernel, pn),
        out_shape=(
            shape((C, T), BF16),
            shape((E, T), F32),
            shape((K * C, pn.iw), F32),
            shape((K * C, pn.iw), F32),
            shape((2 * K * C, pn.iw), F32),
            shape((C, pn.all // nb), F32),
            shape((C, (pn.all + WIDE) // nb), F32),
            shape((11, C), F32),
            shape((11, C), F32),
            shape((12, C), F32),
            shape((12, C), F32),
        ),
        in_specs=[smem] + [any_] * 6 + [vmem] * 5,
        out_specs=(vmem, any_, any_, any_, any_, vmem, vmem, vmem, vmem, vmem, vmem),
        scratch_shapes=scratch,
        compiler_params=pltpu.CompilerParams(
            collective_id=0, has_side_effects=True, vmem_limit_bytes=64000 * 1024
        ),
    )(
        lengths,
        earlier.reshape(own, frames),
        lower_entry.reshape(K * C, pre),
        lower_convs.reshape(K * C, WIDE),
        upper_convs.reshape(2 * K * C, WIDE),
        lower_dense,
        upper_dense,
        lower_gain,
        lower_shift,
        upper_gain,
        upper_shift,
        cotangent.reshape(C, T),
    )
    final, egrad, g0, g1, g23, rlg, rug, lgg, lsg, ugg, usg = outs
    return (
        final.reshape(1, C, T),
        egrad.reshape(1, E, T),
        g0.reshape(K, C, pn.iw)[:, :, 0 : pn.iw0],
        g1.reshape(1, K, C, pn.iw),
        g23.reshape(2, K, C, pn.iw),
        rlg,
        rug,
        lgg,
        lsg,
        ugg,
        usg,
    )


def solution(mesh):
    placed = (
        P("batch", "ch", None),
        P("batch"),
        P(None, "ch", None),
        P(None, None, "ch", None),
        P(None, None, "ch", None),
        P("ch", None),
        P("ch", None),
        P(None, "ch"),
        P(None, "ch"),
        P(None, "ch"),
        P(None, "ch"),
        P("batch", "ch", None),
    )
    return jax.shard_map(
        functools.partial(per_device, mesh.shape["batch"], mesh.shape["ch"]),
        mesh=mesh,
        in_specs=placed,
        out_specs=(
            P("batch", "ch", None),
            P("batch", "ch", None),
            P(None, "ch", "batch"),
            P(None, None, "ch", "batch"),
            P(None, None, "ch", "batch"),
            P("ch", "batch"),
            P("ch", "batch"),
            P(None, "ch"),
            P(None, "ch"),
            P(None, "ch"),
            P(None, "ch"),
        ),
        check_vma=False,
    )
```

```python
import functools
import math

import jax
import jax.numpy as jnp
from jax import lax
from jax.experimental import pallas as pl
from jax.experimental.pallas import tpu as pltpu
from jax.sharding import PartitionSpec as P

EPS = 0.001
WIDTHS = (2, 2, 2, 3, 3, 4, 4, 5, 5)
MESH = pl.DeviceIdType.MESH
F32 = jnp.float32
BF16 = jnp.bfloat16
RB = 16
LANES = 128


def shifted(x, by):
    if by == 0:
        return x
    frames = x.shape[1]
    lane = lax.broadcasted_iota(jnp.int32, x.shape, 1)
    rolled = pltpu.roll(x, (-by) % frames, 1)
    keep = (lane < frames - by) if by > 0 else (lane >= -by)
    return jnp.where(keep, rolled, jnp.zeros_like(rolled))


def squash(v):
    return 0.5 * jnp.tanh(0.5 * v) + 0.5


def dot(a, b):
    return jnp.dot(a, b, preferred_element_type=F32)


def dot_first(a, b):
    return lax.dot_general(a, b, (((0,), (0,)), ((), ())), preferred_element_type=F32)


def dot_last(a, b):
    return lax.dot_general(a, b, (((1,), (1,)), ((), ())), preferred_element_type=F32)


class Plan:
    def __init__(self, nb, nc, own, frames, taps, cw, pre):
        self.nb, self.nc, self.nz = nb, nc, nc // 2
        self.own, self.frames, self.taps, self.cw, self.pre = own, frames, taps, cw, pre
        self.wide = cw * nc
        self.all = own * nc
        unit = self.all // 30
        self.pieces = []
        at = 0
        for w in WIDTHS:
            self.pieces.append((at, w * unit))
            at += w * unit
        self.head = self.all - pre
        self.full = self.head // own
        self.part = self.head % own
        step = math.gcd(own, self.head)
        self.step = max(n for n in (16, 32, 48) if step % n == 0)
        self.flight = 5
        self.late = []
        for chip in range(self.nz):
            rows = [[r for r in range(self.head, self.all, self.step) if r // own == chip * 2 + core] for core in (0, 1)]
            heavy = 0 if len(rows[0]) > len(rows[1]) else 1
            extra = (len(rows[heavy]) - len(rows[1 - heavy])) // 2
            moved = rows[heavy][len(rows[heavy]) - extra :]
            for core in (0, 1):
                keep = [r for r in rows[core] if r not in moved]
                self.late += [(chip, core, r, False) for r in keep]
                if core != heavy:
                    self.late += [(chip, core, r, True) for r in moved]
        self.iw0 = pre // nb
        self.iw = self.wide // nb
        self.group = 5
        self.sems = 0
        nz = self.nz
        self.srcs = [[] for _ in range(nz)]
        for s, (at, width) in enumerate(self.pieces[:-1]):
            self.srcs[(at + width - 1) // (2 * own)].append(s)
        if len(self.srcs[0]) > 2:
            self.srcs[1].insert(0, self.srcs[0].pop())
        self.lo, self.width = [0] * nz, [0] * nz
        self.bound, self.final = [], [[] for _ in range(nz)]
        for zc in range(nz):
            if not self.srcs[zc]:
                continue
            first, last = self.pieces[self.srcs[zc][0]], self.pieces[self.srcs[zc][-1]]
            self.lo[zc], self.width[zc] = first[0], last[0] + last[1] - first[0]
            row = first[0]
            while row < last[0] + last[1]:
                end = min((row // own + 1) * own, last[0] + last[1])
                self.final[zc].append((row // own, row, end - row))
                if row // own // 2 < zc:
                    self.bound.append((zc, row // own % 2, row, end - row))
                row = end
        self.slots = max(len(x) for x in self.srcs)
        self.pw = max(self.width)
        self.split = 4
        self.units = [(zc, u, u % nb) for zc in range(nz) for u in range(self.width[zc] // LANES)]
        self.nu = self.pw // LANES
        self.ku = (self.nu + nb - 1) // nb
        self.s_entry = self.take(2 * len(self.late))
        self.s_src = self.take(3)
        self.kr = (self.nu + self.split - 1) // self.split
        self.s_r1 = [self.take(nz * self.kr) for _ in range(2)]
        self.s_r2 = [self.take(self.split * nz * self.kr) for _ in range(2)]
        self.s_prm = self.take(nz)
        self.s_q = self.take(2 * nz)
        self.s_plane = [self.take(nb) for _ in range(4)]
        self.s_dv = self.take(2 * nz)
        self.s_gain = self.take(2 * nz)
        self.s_d1 = [self.take(nb * self.nu) for _ in range(2)]
        self.s_d2 = [self.take(max(self.ku * nz * 2, len(self.units))) for _ in range(2)]
        self.s_x = [self.take(4 + 2 * nz) for _ in range(3)]
        self.s_sum = [self.take(nb) for _ in range(8)]
        self.s_xs = [self.take(nb) for _ in range(4)]
        self.s_xp = [self.take(nb) for _ in range(4)]
        self.s_dy = [self.take(nb) for _ in range(4)]
        self.s_rs = [self.take(4 + 4 * nz) for _ in range(3)]
        self.s_dp = self.take(1 + max(len(x) for x in self.final))
        self.s_tail = self.take(4 * len(self.late))
        self.s_dr = [self.take(nb) for _ in range(2)]

    def share(self, blk):
        return (self.all + (self.wide if blk else 0)) // self.nb

    def dense_owners(self, blk):
        return [bb for bb in range(self.nb) if (bb + 1) * self.share(blk) > self.head]

    def take(self, count):
        base = self.sems
        self.sems += count
        return base


def up16(n):
    return (n + 15) // 16 * 16


SUM_ROWS = (8, 8, 8, 8, 8, 8, 8, 8)


def kernel(
    pn,
    length_ref,
    earlier_hbm,
    w0_hbm,
    w1_hbm,
    w23_hbm,
    rl_hbm,
    ru_hbm,
    lg_ref,
    lsh_ref,
    ug_ref,
    ush_ref,
    cot_ref,
    final_ref,
    egrad_hbm,
    g0_hbm,
    g1_hbm,
    g23_hbm,
    rlg_ref,
    rug_ref,
    lgg_ref,
    lsg_ref,
    ugg_ref,
    usg_ref,
    w0,
    w1,
    w2,
    w3,
    rp,
    rown,
    src,
    x1,
    x2,
    x3,
    big,
    resid,
    rmid,
    ys,
    dbuf,
    pr,
    drp,
    dr8,
    qpart,
    qrecv,
    dvx,
    gsend,
    grecv,
    dpo,
    dpsib,
    dpbnd,
    d1send,
    d1recv,
    d2send,
    d2recv,
    dxsib,
    dxrecv,
    dxcomb,
    tailsib,
    tailrecv,
    tailfin,
    dyg,
    xs0,
    xs,
    xst,
    drs,
    drr,
    sums,
    colbuf,
    rowbuf,
    kcol,
    psums,
    pcol,
    prow,
    pk,
    prm,
    prms,
    hold,
    gout,
    lsem,
    osem,
    ss,
    rs,
):
    nb, nc, nz = pn.nb, pn.nc, pn.nz
    T, K, C, E = pn.frames, pn.taps, pn.cw, pn.own
    WIDE, PRE, HEAD = pn.wide, pn.pre, pn.head
    b = lax.axis_index("batch")
    c = lax.axis_index("ch")
    z = c // 2
    q = lax.rem(c, 2)
    sib = z * 2 + 1 - q
    other = 1 - q

    def mult(v, m=16):
        return pl.multiple_of(v, m)

    def rcopy(source, target, i_send, i_recv, device):
        return pltpu.make_async_remote_copy(
            src_ref=source,
            dst_ref=target,
            send_sem=ss.at[i_send],
            recv_sem=rs.at[i_recv],
            device_id=device,
            device_id_type=MESH,
        )

    def chip(zz, qq):
        return {"ch": zz * 2 + qq}

    local_loads = []

    def load(source, target):
        cp = pltpu.make_async_copy(source, target, lsem.at[len(local_loads)])
        local_loads.append(cp)
        cp.start()
        return cp

    raw = dpo
    ld_raw = load(earlier_hbm, raw.at[0:E])
    ld_w0 = load(w0_hbm, w0.at[0 : K * C])
    ld_w0l = load(rl_hbm.at[:, HEAD : HEAD + PRE], w0.at[K * C : (K + 1) * C])
    ld_w0u = load(ru_hbm.at[:, HEAD : HEAD + PRE], w0.at[(K + 1) * C : (K + 2) * C])
    ld_w1 = load(w1_hbm, w1)
    dense = (rl_hbm, ru_hbm)

    def at_chip(body):
        for zc in range(nz):
            if pn.srcs[zc]:

                @pl.when(z == zc)
                def _():
                    body(zc)

    def own_dense(zc, blk):
        w = pn.width[zc]
        source = dense[blk].at[:, pn.lo[zc] : pn.lo[zc] + w]
        return pltpu.make_async_copy(source, rp.at[blk, zc * C : (zc + 1) * C, 0:w], lsem.at[8 + blk])

    ld_w2 = load(w23_hbm.at[0 : K * C], w2.at[0 : K * C])
    ld_w2m = load(ru_hbm.at[:, HEAD + PRE : HEAD + PRE + WIDE], w2.at[K * C : (K + 1) * C])
    ld_w3 = load(w23_hbm.at[K * C : 2 * K * C], w3)

    def start_own_dense(zc):
        own_dense(zc, 0).start()
        own_dense(zc, 1).start()

    at_chip(start_own_dense)

    bar = pltpu.get_barrier_semaphore()
    pl.semaphore_signal(bar, inc=1, device_id={"ch": sib}, device_id_type=MESH)
    for d in range(1, nz):
        pl.semaphore_signal(bar, inc=1, device_id=chip(lax.rem(z + d, nz), q), device_id_type=MESH)
    for d in range(1, nb):
        pl.semaphore_signal(bar, inc=1, device_id={"batch": lax.rem(b + d, nb)}, device_id_type=MESH)

    rowbuf[...] = jnp.zeros_like(rowbuf)
    colbuf[...] = jnp.zeros_like(colbuf)
    pcol[...] = jnp.zeros_like(pcol)
    prow[...] = jnp.zeros_like(prow)
    prm[...] = jnp.zeros_like(prm)
    prm[0, 0:11, 0:C] = lg_ref[...]
    prm[1, 0:11, 0:C] = lsh_ref[...]
    prm[2, 0:12, 0:C] = ug_ref[...]
    prm[3, 0:12, 0:C] = ush_ref[...]
    prms[z] = prm[:, 2:10, :]
    length = length_ref[0]
    lane_row = lax.broadcasted_iota(jnp.int32, (1, T), 1)
    valid = jnp.where(lane_row < length, 1.0, 0.0).astype(F32)
    valid_rb = jnp.broadcast_to(valid, (RB, T))

    ld_raw.wait()
    valid_b = valid.astype(BF16)

    def mask_rows(i, _):
        src[pl.ds(mult(c * E + i * RB), RB), :] = raw[pl.ds(mult(i * RB), RB), :] * jnp.broadcast_to(
            valid_b, (RB, T)
        )
        return 0

    lax.fori_loop(0, E // RB, mask_rows, 0, unroll=2)
    pl.semaphore_wait(bar, 1 + (nz - 1) + (nb - 1))

    def sized(cc, body):
        @pl.when(cc < pn.full)
        def _():
            body(E)

        if pn.part:

            @pl.when(cc == pn.full)
            def _():
                body(pn.part)

    def inside(zz):
        return (zz >= 0) & (zz < nz)

    class Gather:
        def __init__(self, base, buf, rows):
            self.base, self.buf, self.rows = base, buf, rows

        def view(self, zz, qq):
            return self.buf.at[pl.ds(mult((zz * 2 + qq) * self.rows), self.rows)]

        def own_copy(self, way, dist):
            v = self.view(z, q)
            i = self.base + (0 if way > 0 else 2) + dist - 1
            return rcopy(v, v, i, self.base + 4 + z, chip(z + way * dist, q))

        def on_copy(self, way, zz):
            v = self.view(zz, q)
            return rcopy(v, v, self.base + 4 + zz, self.base + 4 + zz, chip(z + way, q))

        def sib_copy(self, zz, qq):
            i = self.base + 4 + nz + zz
            return rcopy(self.view(zz, qq), self.view(zz, qq), i, i, {"ch": sib})

        def start(self):
            for dist in (2, 1):
                for way in (1, -1):

                    @pl.when(inside(z + way * dist))
                    def _():
                        self.own_copy(way, dist).start()

            self.sib_copy(z, q).start()

        def arrive(self):
            for dist in [2, 1] + list(range(3, nz)):
                for way in (1, -1):
                    zz = z - way * dist

                    @pl.when(inside(zz))
                    def _():
                        self.on_copy(way, zz).wait_recv()
                        if dist >= 2:

                            @pl.when(inside(z + way))
                            def _():
                                self.on_copy(way, zz).start()

                        self.sib_copy(zz, q).start()

        def end(self):
            for zz in range(nz):
                self.sib_copy(zz, other).wait_recv()

        def drain(self):
            for way in (1, -1):
                for dist in (1, 2):

                    @pl.when(inside(z + way * dist))
                    def _():
                        self.own_copy(way, dist).wait_send()

                for dist in range(2, nz):

                    @pl.when(inside(z - way * dist) & inside(z + way))
                    def _():
                        self.on_copy(way, z - way * dist).wait_send()

            for zz in range(nz):
                self.sib_copy(zz, q).wait_send()

    above = chip(jnp.minimum(z + 1, nz - 1), q)
    below = chip(jnp.maximum(z - 1, 0), q)

    def own_rows(cc, n):
        v = src.at[pl.ds(mult(cc * E), n)]
        return rcopy(v, v, pn.s_src, pn.s_src, {"ch": sib})

    def bound_hop(row, n):
        v = src.at[row : row + n]
        return rcopy(v, v, pn.s_src + 1, pn.s_src + 1, above)

    def bound_sib(row, n):
        v = src.at[row : row + n]
        return rcopy(v, v, pn.s_src + 2, pn.s_src + 2, {"ch": sib})

    in_group = lax.rem(b, pn.split)

    def r_units(zc, member, body):
        for k in range(pn.kr):
            u = member + pn.split * k

            @pl.when(u < pn.width[zc] // LANES)
            def _():
                body(k, pl.ds(mult(u * LANES, LANES), LANES))

    def r_load(blk, zc, k, cols):
        first = mult(pn.lo[zc] + cols.start, LANES)
        i = 10 + (blk * nz + zc) * pn.kr + k
        return pltpu.make_async_copy(dense[blk].at[:, pl.ds(first, LANES)], rown.at[blk, zc, k], lsem.at[i])

    def r_loads(blk, act):
        for zc in range(nz):
            if pn.width[zc]:

                @pl.when(z != zc)
                def _():
                    r_units(zc, in_group, lambda k, cols: act(r_load(blk, zc, k, cols)))

    def r_hop(blk, zc, k, cols):
        target = rp.at[blk, pl.ds(mult(z * C), C), cols]
        i = pn.s_r1[blk]
        return rcopy(rown.at[blk, zc, k], target, i + zc * pn.kr + k, i + z * pn.kr + k, chip(zc, q))

    def r_hops(blk, way, act):
        for zc in range(nz):
            if pn.width[zc]:

                @pl.when((z < zc) if way > 0 else (z > zc))
                def _():
                    r_units(zc, in_group, lambda k, cols: act(r_hop(blk, zc, k, cols)))

    def r_shared(blk, zf, k, cols, member):
        v = rp.at[blk, zf * C : (zf + 1) * C, cols]
        i = pn.s_r2[blk] + k
        to = b - in_group + member
        return rcopy(v, v, i + (member * nz + zf) * pn.kr, i + (in_group * nz + zf) * pn.kr, {"batch": to})

    def r_passes(blk, act):
        def run(zc):
            for zf in range(nz):
                if zf != zc:

                    def unit(k, cols):
                        for d in range(1, pn.split):
                            act(r_shared(blk, zf, k, cols, lax.rem(in_group + d, pn.split)))

                    r_units(zc, in_group, unit)

        at_chip(run)

    def r_arrive(blk):
        def run(zc):
            for zf in range(nz):
                if zf != zc:

                    def unit(k, cols):
                        v = rp.at[blk, zf * C : (zf + 1) * C, cols]
                        i = pn.s_r1[blk] + zf * pn.kr + k
                        rcopy(v, v, i, i, {"ch": sib}).wait_recv()
                        for d in range(1, pn.split):
                            r_shared(blk, zf, k, cols, lax.rem(in_group + d, pn.split)).start()

                    r_units(zc, in_group, unit)

        at_chip(run)

    def r_finish(blk):
        def run(zc):
            own_dense(zc, blk).wait()
            for d in range(1, pn.split):
                member = lax.rem(in_group + d, pn.split)
                for zf in range(nz):
                    if zf != zc:

                        def unit(k, cols):
                            v = rp.at[blk, zf * C : (zf + 1) * C, cols]
                            i = pn.s_r2[blk] + (member * nz + zf) * pn.kr + k
                            rcopy(v, v, i, i, {"ch": sib}).wait_recv()

                        r_units(zc, member, unit)

        at_chip(run)

    for blk in (0, 1):
        r_loads(blk, lambda cp: cp.start())

    def others(body):
        for d in range(1, nz):
            body(lax.rem(z + d, nz))

    def prm_copy(zz):
        return rcopy(prms.at[z], prms.at[z], pn.s_prm + zz, pn.s_prm + z, chip(zz, q))

    def prm_copies(way, act):
        for zz in range(nz):

            @pl.when((z < zz) if way > 0 else (z > zz))
            def _():
                act(prm_copy(zz))

    def prm_arrive(zz):
        rcopy(prms.at[zz], prms.at[zz], pn.s_prm + zz, pn.s_prm + zz, {"ch": sib}).wait_recv()

    sized(c, lambda n: own_rows(c, n).start())
    for zc, qq, row, n in pn.bound:

        @pl.when((z == zc - 1) & (q == qq))
        def _():
            bound_hop(row, n).start()

    def entry_rows(n):
        return src.at[pn.late[n][2] : pn.late[n][2] + pn.step]

    def entry_hop(n, device):
        v = entry_rows(n)
        return rcopy(v, v, pn.s_entry + n, pn.s_entry + n, device)

    def entry_sib(n):
        i = pn.s_entry + len(pn.late) + n
        return rcopy(entry_rows(n), entry_rows(n), i, i, {"ch": sib})

    order = [n for n in range(len(pn.late))]
    def entry_up(n):
        return rcopy(entry_rows(n), entry_rows(n), pn.s_tail + n, pn.s_entry + n, above)

    for n in order:
        zc, qc, _, moved = pn.late[n]
        if moved:

            @pl.when((q != qc) & (z == zc))
            def _():
                entry_sib(n).start()

    for zc, qc in sorted({x[:2] for x in pn.late}):
        mine = [n for n in order if pn.late[n][:2] == (zc, qc)]

        @pl.when((q == qc) & (z == zc))
        def _():
            for at, n in enumerate(mine):
                if at >= pn.flight:
                    if zc > 0:
                        entry_hop(mine[at - pn.flight], below).wait_send()
                    if zc < nz - 1:
                        entry_up(mine[at - pn.flight]).wait_send()
                if pn.late[n][3]:
                    entry_sib(n).wait_recv()
                else:
                    entry_sib(n).start()
                if zc > 0:
                    entry_hop(n, below).start()
                if zc < nz - 1:
                    entry_up(n).start()
            for n in mine[-pn.flight :]:
                if zc > 0:
                    entry_hop(n, below).wait_send()
                if zc < nz - 1:
                    entry_up(n).wait_send()

    for blk in (0, 1):
        r_loads(blk, lambda cp: cp.wait())
        r_hops(blk, 1, lambda cp: cp.start())
    prm_copies(1, lambda cp: cp.start())
    for n in order:
        zc, qc, _, moved = pn.late[n]

        @pl.when((q == qc) & (z < zc))
        def _():
            entry_hop(n, below).wait_recv()

            @pl.when(z > 0)
            def _():
                entry_hop(n, below).start()

            entry_sib(n).start()

        if zc < nz - 1:

            @pl.when((q == qc) & (z > zc))
            def _():
                entry_hop(n, above).wait_recv()

                @pl.when(z < nz - 1)
                def _():
                    entry_hop(n, above).start()

                entry_sib(n).start()

    for n in order:

        zc, qc, _, moved = pn.late[n]

        @pl.when((q != qc) & (z != zc) if moved else q != qc)
        def _():
            entry_sib(n).wait_recv()

    def entry_drain():
        for n in order:
            zc, qc, _, moved = pn.late[n]

            @pl.when(((q == qc) & (z != zc)) | ((q != qc) & (z == zc)) if moved else q == qc)
            def _():
                entry_sib(n).wait_send()

            @pl.when((q == qc) & (z < zc) & (z > 0))
            def _():
                entry_hop(n, below).wait_send()

            if zc < nz - 1:

                @pl.when((q == qc) & (z > zc) & (z < nz - 1))
                def _():
                    entry_hop(n, above).wait_send()

    def sum_copies(p):
        rows = SUM_ROWS[p]
        for d in range(1, nb):
            bb = lax.rem(b + d, nb)
            v = sums.at[p, b, 0:rows]
            yield bb, rcopy(v, v, pn.s_sum[p] + bb, pn.s_sum[p] + b, {"batch": bb})


    def tree(parts):
        tiles = range(0, T, LANES)
        parts = [v if v is None else functools.reduce(jnp.add, [v[:, i : i + LANES] for i in tiles]) for v in parts]
        lane_of = lax.broadcasted_iota(jnp.int32, (parts[0].shape[0], LANES), 1)
        size = 1
        while size < len(parts):
            size *= 2
        parts = parts + [None] * (size - len(parts))
        width = LANES
        while len(parts) > 1:
            width //= 2
            low = (lane_of // width) % 2 == 0
            fold = []
            for x, y in zip(parts[: len(parts) // 2], parts[len(parts) // 2 :]):
                y = x if y is None else y
                if x is None:
                    fold.append(None)
                elif width * 2 == LANES:
                    fold.append(jnp.where(low, x, y) + pltpu.roll(jnp.where(low, y, x), width, 1))
                else:
                    fold.append(
                        jnp.where(low, x + pltpu.roll(x, LANES - width, 1), y + pltpu.roll(y, width, 1))
                    )
            parts = fold
        total = parts[0]
        while width > 1:
            width //= 2
            total = total + pltpu.roll(total, LANES - width, 1)
        return total

    def pack_sums(r, parts):
        colbuf[r, :] = tree(parts)

    def sum_start(p, count, constant=None):
        size = 1
        while size < count:
            size *= 2
        rowbuf[...] = colbuf[...].T
        sums[p, b, 0:count, :] = rowbuf[pl.ds(0, count, stride=LANES // size), :]
        if constant is not None:
            sums[p, b, count : count + 1, :] = constant
        for _, cp in sum_copies(p):
            cp.start()

    def sum_finish(p):
        rows = SUM_ROWS[p]
        for bb, _ in sum_copies(p):
            v = sums.at[p, bb, 0:rows]
            rcopy(v, v, pn.s_sum[p] + bb, pn.s_sum[p] + bb, {"batch": bb}).wait_recv()
        total = sums[p, 0, 0:rows, :]
        for bb in range(1, nb):
            total = total + sums[p, bb, 0:rows, :]
        return total

    def columns(p, parts):
        at = 0
        for part in parts:
            rowbuf[at : at + part.shape[0], :] = part
            at += part.shape[0]
        kcol[p] = rowbuf[...].T

    def norm_rows(first, second, count, gain, shift):
        average = first / count
        scaling = lax.rsqrt(second / count - average * average + EPS)
        scale = scaling * gain
        return average, scaling, scale, shift - average * scale

    def blocks(body):
        for i in range(0, C, RB):
            body(pl.ds(i, RB))

    def rolled(body):
        def step(i, carry):
            body(pl.ds(mult(i * RB), RB))
            return carry

        lax.fori_loop(0, C // RB, step, 0)

    def at_row(base, r):
        if isinstance(base, int) and isinstance(r.start, int):
            return pl.ds(base + r.start, RB)
        return pl.ds(mult(base + r.start), RB)

    def conv(w, x, y_index, more=None):
        if more is not None:
            more[...] = dot(w[K * C : K * C + more.shape[0], :], x)
        for i in range(0, C, RB):
            taps = jnp.concatenate([w[k * C + i : k * C + i + RB, :] for k in range(K)], axis=0)
            rows = dot(taps, x)
            total = None
            for k in range(K):
                v = shifted(rows[k * RB : (k + 1) * RB], k - K // 2)
                total = v if total is None else total + v
            ys[y_index, i : i + RB, :] = total

    def conv_sums(y_index):
        def body(r):
            y = ys[y_index, r, :] * valid_rb
            pack_sums(r, [y, y * y])

        blocks(body)

    def slices(j):
        if j == 0:
            return src, HEAD, pn.iw0, xs0
        return (None, x1, x2, x3)[j], 0, pn.iw, xs.at[j - 1]

    def half_rows(j, core):
        iw = slices(j)[2]
        if iw % 32:
            return 0, up16(iw)
        return mult(core * (iw // 2)), iw // 2

    def slice_half(j, core, bb):
        first, many = half_rows(j, core)
        return slices(j)[3].at[pl.ds(first, many), pl.ds(mult(bb * T, LANES), T)]

    def slice_pass(j, act):
        if slices(j)[2] % 32 == 0:
            for d in range(1, nb):
                bb = lax.rem(b + d, nb)
                i = pn.s_xp[j] + bb
                v = slice_half(j, q, bb)
                act(bb, rcopy(v, v, i, i, {"ch": sib}))

    def slice_arrive(j):
        def take(bb, cp):
            v = slice_half(j, q, bb)
            rcopy(v, v, pn.s_xs[j] + bb, pn.s_xs[j] + bb, {"batch": bb}).wait_recv()
            cp.start()

        slice_pass(j, take)

    def slice_copies(j):
        x, base, iw, target = slices(j)
        rows = up16(iw)
        for d in range(1, nb):
            bb = lax.rem(b + d, nb)
            if rows == iw:
                first, many = half_rows(j, q)
                source = x.at[pl.ds(mult(base + bb * iw + first), many)]
            else:
                source = xst.at[j, bb, 0:rows]
            there = slice_half(j, q, b)
            yield bb, rcopy(source, there, pn.s_xs[j] + bb, pn.s_xs[j] + b, {"batch": bb})

    def slice_start(j):
        x, base, iw, target = slices(j)
        rows = up16(iw)
        here = pl.ds(mult(b * T, LANES), T)
        if rows == iw:
            target[:, here] = x[pl.ds(mult(base + b * iw), iw), :]
        else:
            for bb in range(nb):
                xst[j, bb, 0:rows, :] = jnp.zeros((rows, T), BF16)
                xst[j, bb, 0:iw, :] = x[base + bb * iw : base + (bb + 1) * iw, :]
            target[:, here] = xst[j, b, 0:rows, :]
        for _, cp in slice_copies(j):
            cp.start()

    def slice_finish(j):
        for bb, _ in slice_copies(j):
            if slices(j)[2] % 32 == 0:
                v, i = slice_half(j, other, bb), pn.s_xp[j] + bb
            else:
                v, i = slice_half(j, q, bb), pn.s_xs[j] + bb
            rcopy(v, v, i, i, {"ch": sib}).wait_recv()

    def dy_copies(j):
        v = dyg.at[j, :, pl.ds(mult(b * T, LANES), T)]
        for d in range(1, nb):
            bb = lax.rem(b + d, nb)
            yield bb, rcopy(v, v, pn.s_dy[j] + bb, pn.s_dy[j] + b, {"batch": bb})

    def dy_start(j):
        for _, cp in dy_copies(j):
            cp.start()

    def dy_finish(j):
        for bb, _ in dy_copies(j):
            v = dyg.at[j, :, pl.ds(mult(bb * T, LANES), T)]
            rcopy(v, v, pn.s_dy[j] + bb, pn.s_dy[j] + bb, {"batch": bb}).wait_recv()

    out_copies = []

    def out_copy():
        out, first, k = out_copies[-1]
        return pltpu.make_async_copy(gout, out.at[first : first + K * C], osem.at[k])

    def weight_grad(j, out, first, groups=range(K // pn.group)):
        _, _, iw, target = slices(j)
        rows = pn.group * C
        for g in groups:
            if g == 0:
                if out_copies:
                    out_copy().wait()
                slice_finish(j)
                dy_finish(j)

            grad = None
            for u in range(nb):
                here = slice(u * T, (u + 1) * T)
                dy = dyg[j, :, here]
                taps = [shifted(dy, K // 2 - g * pn.group - i) for i in range(pn.group)]
                v = dot_last(jnp.concatenate(taps, axis=0), target[:, here])
                grad = v if grad is None else grad + v
            gout[g * rows : (g + 1) * rows, 0:iw] = grad[:, 0:iw]
            if g == K // pn.group - 1:
                out_copies.append((out, first, len(out_copies)))
                out_copy().start()

    half = WIDE // 2
    hz = nz // 2
    upper_half = z // hz

    def shift_all(j):
        dy = dyg[j, :, pl.ds(mult(b * T, LANES), T)]
        for k in range(K):
            dbuf[k * C : (k + 1) * C, :] = shifted(dy, K // 2 - k)

    def back_rows(w, extra, lanes, to):
        rows = (K + extra) * C
        big[to, :] = dot_first(w[0:rows, lanes], dbuf[0:rows, :])

    class Scatter:
        def __init__(self, n):
            self.base, self.part, self.sibs, self.recv = pn.s_rs[n], x1, dxsib.at[n], dxrecv.at[n]
            self.combs = dxcomb.at[n]

        def rows(self, zz, qq):
            return pl.ds(mult((zz * 2 + qq) * C), C)

        def to_sib(self, zz):
            return rcopy(
                self.part.at[self.rows(zz, other)],
                self.sibs.at[zz],
                self.base + 4 + zz,
                self.base + 4 + zz,
                {"ch": sib},
            )

        def slot(self, way, dist):
            return (0 if way > 0 else 2) + dist - 1

        def comb(self, way, dist):
            first = 0 if way > 0 or nz <= 4 else nz - 3
            return self.combs.at[first + dist - 2], self.base + 4 + nz + (0 if way > 0 else nz) + dist

        def out(self, way, dist):
            zz = z + way * dist
            source = self.part.at[self.rows(zz, q)]
            i_send = self.base + 4 + 3 * nz + zz
            if dist <= 2:
                at = self.slot(way, dist)
                return rcopy(source, self.recv.at[at], i_send, self.base + at, chip(zz, q))
            target, i = self.comb(way, dist - 1)
            return rcopy(source, target, i_send, i, chip(z + way, q))

        def compute(self, w, extra):
            for far in (1, 0):
                m = upper_half + far - 2 * upper_half * far
                at = pl.ds(mult(m * half, LANES), half)
                back_rows(w, extra, at, at)
                for i in range(hz):
                    zz = m * hz + i
                    r = self.rows(zz, other)
                    self.part[r, :] = big[r, :].astype(BF16)
                    self.to_sib(zz).start()

        def fold(self, zz):
            self.to_sib(zz).wait_recv()
            return big[self.rows(zz, q), :] + self.sibs[zz].astype(F32)

        def send_dist(self, dist):
            for way in (1, -1):
                zz = z + way * dist

                @pl.when(inside(zz))
                def _():
                    total = self.fold(zz)
                    if dist >= 2:
                        big[self.rows(zz, q), :] = total

                        @pl.when(inside(z - way))
                        def _():
                            v, i = self.comb(way, dist)
                            rcopy(v, v, i, i, {"ch": sib}).wait_recv()
                            big[self.rows(zz, q), :] += v[...].astype(F32)

                        total = big[self.rows(zz, q), :]
                    self.part[self.rows(zz, q), :] = total.astype(BF16)
                    self.out(way, dist).start()

        def send(self):
            for dist in list(range(nz - 1, 2, -1)) + [1]:
                self.send_dist(dist)
            hold[0] = self.fold(z)

        def end(self):
            for dist in (1, 2):
                for way in (1, -1):

                    @pl.when(inside(z - way * dist))
                    def _():
                        at = self.slot(way, dist)
                        v = self.recv.at[at]
                        rcopy(v, v, self.base + at, self.base + at, {"ch": sib}).wait_recv()
                        hold[0] += v[...].astype(F32)

            self.drain()

        def drain(self):
            for d in range(nz):
                self.to_sib(lax.rem(z + d, nz)).wait_send()
            for way in (1, -1):
                for dist in range(1, nz):

                    @pl.when(inside(z + way * dist))
                    def _():
                        self.out(way, dist).wait_send()

    rows_all = nz * C

    def plane_rows(body, straight=False):
        if straight:
            for zz in range(nz):
                body(zz * C, zz, pl.ds(0, C))
            return

        def step(zz, carry):
            body(mult(zz * C), zz, pl.ds(0, C))
            return carry

        lax.fori_loop(0, nz, step, 0)


    def plane_sums(body, slot, step):
        def run(row, zz, r):
            total = tree(body(row))
            if slot > 0:
                lane_mod = lax.broadcasted_iota(jnp.int32, total.shape, 1) % step
                total = jnp.where(lane_mod == slot, pltpu.roll(total, slot, 1), pcol[zz, r, :])
            pcol[zz, r, :] = total

        plane_rows(run, True)

    def at_slot(i, body):
        chips = [zc for zc in range(nz) if len(pn.srcs[zc]) > i]
        pl.when(functools.reduce(jnp.logical_or, [z == zc for zc in chips]))(body)

    def plane_copies(p):
        v = psums.at[p, b]
        for d in range(1, nb):
            bb = lax.rem(b + d, nb)
            yield bb, rcopy(v, v, pn.s_plane[p] + bb, pn.s_plane[p] + b, {"batch": bb})

    def plane_start(p, groups, step):
        for zz in range(nz):
            prow[zz] = pcol[zz].T
            for n in range(groups):
                psums[p, b, zz, 4 * n : 4 * n + 4, :] = prow[zz, step * n : step * n + 4, :]
        for _, cp in plane_copies(p):
            cp.start()

    def plane_finish(p):
        for bb, _ in plane_copies(p):
            v = psums.at[p, bb]
            rcopy(v, v, pn.s_plane[p] + bb, pn.s_plane[p] + bb, {"batch": bb}).wait_recv()
        total = psums[p, 0]
        for bb in range(1, nb):
            total = total + psums[p, bb]
        return total

    def project(zc, s, blk):
        at, width = pn.pieces[s]
        place = at - pn.lo[zc]
        big[0:rows_all, :] = dot(rp[blk, :, place : place + width], src[at : at + width, :])

    def project_slot(i, blk):
        def run(zc):
            if len(pn.srcs[zc]) > i:
                project(zc, pn.srcs[zc][i], blk)

        at_chip(run)

    def plane_first(blk):
        for i in range(pn.slots):
            project_slot(i, blk)

            def parts(row):
                v = big[pl.ds(row, C), :]
                return [v, v * v]

            at_slot(i, lambda: plane_sums(parts, i, 64))

    def base(blk, i):
        return blk * 4 + i

    def plane_norms(zc, total, blk):
        shift_sum = None
        for i, s in enumerate(pn.srcs[zc]):
            gain, shift = prms[:, 2 * blk, s, :], prms[:, 2 * blk + 1, s, :]
            p_av, p_rsd, p_sc, _ = norm_rows(total[:, i], total[:, 4 + i], count, gain, shift)
            pk[:, base(blk, i), :] = p_rsd
            pk[:, 8 + base(blk, i), :] = p_av
            pk[:, 16 + base(blk, i), :] = gain
            pk[:, 48 + base(blk, i), :] = p_sc
            shift_sum = shift if shift_sum is None else shift_sum + shift
        pk[:, 24 + blk, :] = shift_sum
        for zz in range(nz):
            prow[zz] = pk[zz].T

    def plane_col(zz, r, n):
        return prow[zz, r, n : n + 1]

    def plane_values(blk):
        for i in range(pn.slots):
            project_slot(i, blk)

            def scale(row, zz, r):
                v = big[pl.ds(row, C), :]
                v = (v - plane_col(zz, r, 8 + base(blk, i))) * plane_col(zz, r, base(blk, i))
                pr[i, blk, pl.ds(row, C), :] = v.astype(BF16)
                v = v * plane_col(zz, r, 16 + base(blk, i))
                if i == 0:
                    v = v + plane_col(zz, r, 24 + blk)
                else:
                    v = v + qpart[blk, pl.ds(row, C), :].astype(F32)
                qpart[blk, pl.ds(row, C), :] = v.astype(BF16)

            at_slot(i, lambda: plane_rows(scale))

    def q_send(blk):
        def send(zc):
            for zz in range(nz):
                if zz != zc:
                    q_copy(blk, zz).start()
            qrecv[blk, zc] = qpart[blk, zc * C : (zc + 1) * C, :]

        at_chip(send)

    def q_copy(blk, zz):
        i = pn.s_q + blk * nz
        return rcopy(qpart.at[blk, zz * C : (zz + 1) * C], qrecv.at[blk, z], i + zz, i + z, chip(zz, q))

    def q_finish(blk):
        for zc in range(nz):
            if pn.srcs[zc]:

                @pl.when(z != zc)
                def _():
                    v = qrecv.at[blk, zc]
                    i = pn.s_q + blk * nz + zc
                    rcopy(v, v, i, i, {"ch": sib}).wait_recv()

    def q_sum(blk, r, v):
        for zc in range(nz):
            if pn.srcs[zc]:
                v = v + qrecv[blk, zc, r, :].astype(F32)
        return v

    @pl.when(z == nz - 1)
    def _():
        r_hops(0, -1, lambda cp: cp.start())

    ld_w0.wait()
    ld_w0l.wait()
    ld_w0u.wait()
    conv(w0, src[HEAD : HEAD + PRE, :], 0, resid)
    conv_sums(0)
    sum_start(0, 2, jnp.broadcast_to(length.astype(F32), (1, LANES)))

    @pl.when(z < nz - 1)
    def _():
        r_hops(0, -1, lambda cp: cp.start())

    prm_copies(-1, lambda cp: cp.start())
    for zc, qq, row, n in pn.bound:

        @pl.when((z == zc) & (q == qq))
        def _():
            bound_hop(row, n).wait_recv()
            bound_sib(row, n).start()

    total = sum_finish(0)
    count = jnp.broadcast_to(total[2:3, 0:1], (1, LANES))
    av, rsd, sc, off = norm_rows(total[0:1], total[1:2], count, prm[0, 0:1], prm[1, 0:1])
    columns(0, [sc, off, av, rsd])

    def activate(p, y_index, out):
        def body(r):
            v = ys[y_index, r, :] * kcol[p, r, 0:1] + kcol[p, r, 1:2]
            out[at_row(c * C, r), :] = (v * squash(v) * valid_rb).astype(BF16)

        blocks(body)

    activate(0, 0, x1)
    gx1 = Gather(pn.s_x[0], x1, C)
    gx1.start()
    r_arrive(0)
    for zc, qq, row, n in pn.bound:

        @pl.when((z == zc) & (q != qq))
        def _():
            bound_sib(row, n).wait_recv()

    sized(sib, lambda n: own_rows(sib, n).wait_recv())
    gx1.arrive()
    r_finish(0)
    plane_first(0)
    plane_start(0, 2, 64)
    gx1.end()
    ld_w1.wait()
    conv(w1, x1[...], 1)

    def first_sums(r):
        y = ys[1, r, :] * valid_rb
        lo, up = resid[r, :], resid[at_row(C, r), :]
        pack_sums(r, [y, y * y, lo, lo * lo, up, up * up])

    blocks(first_sums)
    sum_start(1, 6)
    r_hops(1, -1, lambda cp: cp.start())
    others(prm_arrive)
    plane_total = plane_finish(0)
    at_chip(lambda zc: plane_norms(zc, plane_total, 0))
    plane_values(0)
    q_send(0)
    total = sum_finish(1)
    r_arrive(1)
    slice_start(0)
    l1 = norm_rows(total[0:1], total[1:2], count, prm[0, 1:2], prm[1, 1:2])
    l8 = norm_rows(total[2:3], total[3:4], count, prm[0, 10:11], prm[1, 10:11])
    u8 = norm_rows(total[4:5], total[5:6], count, prm[2, 10:11], prm[3, 10:11])
    columns(1, [l1[2], l8[2], l1[0], l8[0], l1[3] + l8[3]])
    q_finish(0)

    def lower_out(r):
        v = ys[1, r, :] * kcol[1, r, 0:1] + kcol[1, r, 4:5] + resid[r, :] * kcol[1, r, 1:2]
        v = q_sum(0, r, v)
        hold[1, r, :] = v
        x2[at_row(c * C, r), :] = (v * squash(v) * valid_rb).astype(BF16)

    blocks(lower_out)
    gx2 = Gather(pn.s_x[1], x2, C)
    gx2.start()
    gx2.arrive()
    r_finish(1)
    plane_first(1)
    plane_start(3, 2, 64)
    gx2.end()
    ld_w2.wait()
    ld_w2m.wait()
    conv(w2, x2[...], 2, rmid)

    def mid_sums(r):
        y = ys[2, r, :] * valid_rb
        v = rmid[r, :]
        pack_sums(r, [y, y * y, v, v * v])

    blocks(mid_sums)
    sum_start(2, 4)
    total = sum_finish(2)
    u2 = norm_rows(total[0:1], total[1:2], count, prm[2, 0:1], prm[3, 0:1])
    mid = norm_rows(total[2:3], total[3:4], count, prm[2, 11:12], prm[3, 11:12])
    columns(2, [u2[2], u2[3], u2[0], u2[1]])
    activate(2, 2, x3)
    gx3 = Gather(pn.s_x[2], x3, C)
    gx3.start()
    plane_total = plane_finish(3)
    at_chip(lambda zc: plane_norms(zc, plane_total, 1))
    plane_values(1)
    slice_start(2)
    slice_start(1)
    gx3.arrive()
    q_send(1)
    gx3.end()
    ld_w3.wait()
    conv(w3, x3[...], 3)
    conv_sums(3)
    sum_start(3, 2)
    q_finish(1)
    total = sum_finish(3)
    u3 = norm_rows(total[0:1], total[1:2], count, prm[2, 1:2], prm[3, 1:2])
    columns(3, [u3[2], u8[2], mid[2], u3[0], u8[0], mid[0], u3[3] + u8[3] + mid[3]])

    def value_back(v, gradient):
        s = squash(v)
        return gradient * valid_rb * s * (1.0 + v * (1.0 - s))

    def upper_out(r):
        up = resid[at_row(C, r), :]
        v = ys[3, r, :] * kcol[3, r, 0:1] + kcol[3, r, 6:7] + up * kcol[3, r, 1:2] + rmid[r, :] * kcol[3, r, 2:3]
        v = q_sum(1, r, v)
        final_ref[r, :] = (v * squash(v) * valid_rb).astype(BF16)
        dv = value_back(v, cot_ref[r, :].astype(F32))
        hold[2, r, :] = dv
        dvx[1, at_row(z * C, r), :] = dv.astype(BF16)
        parts = [dv]
        for n, x in enumerate((ys[3, r, :], up, rmid[r, :])):
            parts.append(dv * (x - kcol[3, r, 3 + n : 4 + n]))
        pack_sums(r, parts)

    blocks(upper_out)

    def dv_copy(blk, zz):
        v = dvx.at[blk, pl.ds(mult(z * C), C)]
        return rcopy(v, v, pn.s_dv + blk * nz + zz, pn.s_dv + blk * nz + z, chip(zz, q))

    def dv_copies(blk, act):
        for zz in range(nz):
            if pn.srcs[zz]:

                @pl.when(z != zz)
                def _():
                    act(dv_copy(blk, zz))

    def plane_back(blk, p):
        def wait(zc):
            for zf in range(nz):
                if zf != zc:
                    v = dvx.at[blk, zf * C : (zf + 1) * C]
                    i = pn.s_dv + blk * nz + zf
                    rcopy(v, v, i, i, {"ch": sib}).wait_recv()

        at_chip(wait)
        counts = sorted({len(x) for x in pn.srcs} - {0})
        for many in counts:

            def parts(row):
                dv = dvx[blk, pl.ds(row, C), :].astype(F32)
                found = [dv * pr[i, blk, pl.ds(row, C), :].astype(F32) for i in range(many)]
                return [dv] + found + [None] * (3 - many)

            chips = [z == zc for zc in range(nz) if len(pn.srcs[zc]) == many]
            pl.when(functools.reduce(jnp.logical_or, chips))(lambda: plane_sums(parts, 0, 32))
        plane_start(p, 4, 32)

    def gain_copy(blk, zz):
        i = pn.s_gain + blk * nz
        return rcopy(gsend.at[blk, zz], grecv.at[blk, z], i + zz, i + z, chip(zz, q))

    def plane_coefficients(blk, total):
        def run(zc):
            dv_sum = total[:, 0]
            for i in range(len(pn.srcs[zc])):
                g = total[:, 4 * (i + 1)]
                gsend[blk, :, i, :] = g
                p_sc = pk[:, 48 + base(blk, i), :]
                pk[:, 32 + base(blk, i), :] = p_sc * dv_sum / count
                pk[:, 40 + base(blk, i), :] = p_sc * g / count
            for zz in range(nz):
                prow[zz] = pk[zz].T
                if zz != zc:
                    gain_copy(blk, zz).start()
            grecv[blk, zc] = gsend[blk, zc]

        at_chip(run)

    def plane_dr(blk):
        def run(zc):
            def body(row, zz, r):
                dv = dvx[blk, pl.ds(row, C), :].astype(F32)
                for i in range(len(pn.srcs[zc])):
                    n = base(blk, i)
                    v = pr[i, blk, pl.ds(row, C), :].astype(F32)
                    v = plane_col(zz, r, 48 + n) * dv - (
                        plane_col(zz, r, 32 + n) + plane_col(zz, r, 40 + n) * v
                    )
                    drp[i, blk, pl.ds(row, C), :] = (v * valid).astype(BF16)

            plane_rows(body)

        at_chip(run)

    def unit_copy(blk, u):
        i = pn.s_d1[blk]
        target = d1recv.at[blk, b, u // nb]
        return rcopy(d1send.at[u], target, i + u, i + b * pn.nu + u, {"batch": u % nb})

    def unit_grads(blk):
        def run(zc):
            for i, s in enumerate(pn.srcs[zc]):
                at, width = pn.pieces[s]
                grad = dot_last(drp[i, blk], src[at : at + width, :])
                first = (at - pn.lo[zc]) // LANES
                for n in range(width // LANES):
                    d1send[first + n] = grad[:, n * LANES : (n + 1) * LANES].astype(BF16)

        at_chip(run)

    def unit_send(blk):
        def run(zc):
            for u in range(pn.width[zc] // LANES):

                @pl.when(b != u % nb)
                def _():
                    unit_copy(blk, u).start()

        at_chip(run)

    def unit_drain(blk):
        def run(zc):
            for u in range(pn.width[zc] // LANES):

                @pl.when(b != u % nb)
                def _():
                    unit_copy(blk, u).wait_send()

        at_chip(run)

    def unit_blocks(blk, zc, u):
        col = pn.lo[zc] + u * LANES
        return list(range(col // pn.share(blk), (col + LANES - 1) // pn.share(blk) + 1))

    def unit_number(zc, u):
        return [n for n, (a, e, _) in enumerate(pn.units) if (a, e) == (zc, u)][0]

    def result_copies(blk, zc, u, act_far, act_own):
        k = u // nb
        number = unit_number(zc, u)
        for zz in range(nz):
            for jj, j in enumerate(unit_blocks(blk, zc, u)):
                source = d2send.at[blk, k, zz * C : (zz + 1) * C]
                cp = rcopy(
                    source,
                    d2recv.at[blk, number],
                    pn.s_d2[blk] + (k * nz + zz) * 2 + jj,
                    pn.s_d2[blk] + number,
                    {"batch": j, "ch": zz * 2 + q},
                )
                if zz == zc and j == u % nb:
                    if act_own is not None:
                        act_own(number, k, zz)
                else:
                    act_far(cp)

    def unit_finish(blk):
        def run(zc):
            for u in range(pn.width[zc] // LANES):

                @pl.when(b == u % nb)
                def _():
                    total = d1send[u].astype(F32)
                    for d in range(1, nb):
                        bb = lax.rem(b + d, nb)
                        v = d1recv.at[blk, bb, u // nb]
                        i = pn.s_d1[blk] + bb * pn.nu + u
                        rcopy(v, v, i, i, {"ch": sib}).wait_recv()
                        total = total + d1recv[blk, bb, u // nb].astype(F32)
                    d2send[blk, u // nb] = total.astype(BF16)

                    def keep(number, k, zz):
                        d2recv[blk, number] = d2send[blk, k, zz * C : (zz + 1) * C, :]

                    result_copies(blk, zc, u, lambda cp: cp.start(), keep)

        at_chip(run)

    def result_drain(blk):
        def run(zc):
            for u in range(pn.width[zc] // LANES):

                @pl.when(b == u % nb)
                def _():
                    result_copies(blk, zc, u, lambda cp: cp.wait_send(), None)

        at_chip(run)

    def result_finish(blk, out):
        share = pn.share(blk)
        for j in range(nb):

            @pl.when(b == j)
            def _():
                for number, (zc, u, ub) in enumerate(pn.units):
                    col = pn.lo[zc] + u * LANES
                    lo_c, hi_c = max(col, j * share), min(col + LANES, (j + 1) * share)
                    if lo_c >= hi_c:
                        continue
                    v = d2recv.at[blk, number]
                    i = pn.s_d2[blk] + number
                    arrived = rcopy(v, v, i, i, {"ch": sib})
                    if ub == j:

                        @pl.when(z != zc)
                        def _():
                            arrived.wait_recv()

                    else:
                        arrived.wait_recv()
                    out[:, lo_c - j * share : hi_c - j * share] = d2recv[blk, number][
                        :, lo_c - col : hi_c - col
                    ].astype(F32)

    sum_start(4, 4)
    dv_copies(1, lambda cp: cp.start())
    total = sum_finish(4)
    slice_start(3)
    upper_q = total[0:1]
    upper_rsd = jnp.concatenate([u3[1], u8[1], mid[1]], axis=0)
    upper_sc = jnp.concatenate([u3[2], u8[2], mid[2]], axis=0)
    upper_g = total[1:4] * upper_rsd
    usg_ref[1:12, :] = jnp.broadcast_to(upper_q[:, 0:C], (11, C))
    ugg_ref[1:2, :] = upper_g[0:1, 0:C]
    ugg_ref[10:12, :] = upper_g[1:3, 0:C]
    columns(4, [upper_sc * upper_q / count, upper_sc * upper_rsd * upper_g / count])

    def grad_rows(gradient, values, sc_col, av_col, a_col, b_col):
        return ((sc_col * gradient - (a_col + b_col * (values - av_col))) * valid_rb).astype(BF16)

    own_lanes = pl.ds(mult(b * T, LANES), T)

    def upper_grad(r, values, n):
        return grad_rows(
            hold[2, r, :],
            values,
            kcol[3, r, n : n + 1],
            kcol[3, r, 3 + n : 4 + n],
            kcol[4, r, n : n + 1],
            kcol[4, r, 3 + n : 4 + n],
        )

    def upper_dy(r):
        dyg[3, r, own_lanes] = upper_grad(r, ys[3, r, :], 0)

    blocks(upper_dy)
    gx1.drain()
    for _, cp in slice_copies(1):
        cp.wait_send()
    shift_all(3)
    sc0 = Scatter(0)
    sc0.compute(w3, 0)
    sc0.send()
    dy_start(3)
    sc0.send_dist(2)
    slice_arrive(0)
    slice_arrive(1)
    slice_arrive(2)

    def upper_dr(r):
        dr8[at_row(C, r), :] = upper_grad(r, resid[at_row(C, r), :], 1)
        dbuf[at_row(K * C, r), :] = upper_grad(r, rmid[r, :], 2)

    blocks(upper_dr)

    def dense_stage(n, first_col, value):
        share = pn.share(n)
        end = first_col + value.shape[1]
        for k, bb in enumerate(pn.dense_owners(n)):
            lo_c, hi_c = max(first_col, bb * share), min(end, (bb + 1) * share)
            if lo_c < hi_c:
                drs[n, k, :, lo_c - bb * share : hi_c - bb * share] = value[
                    :, lo_c - first_col : hi_c - first_col
                ].astype(BF16)

    def dense_cut(n, bb):
        first = max(HEAD - bb * pn.share(n), 0)
        return first, first // LANES * LANES

    def dense_copy(n, k, bb):
        tile = dense_cut(n, bb)[1]
        i = pn.s_dr[n]
        return rcopy(drs.at[n, k, :, tile:], drr.at[n, b, :, tile:], i + bb, i + b, {"batch": bb})

    def dense_copies(n, act):
        for k, bb in enumerate(pn.dense_owners(n)):

            @pl.when(b != bb)
            def _():
                act(dense_copy(n, k, bb))

    def dense_finish(n, out):
        share = pn.share(n)
        for k, bb in enumerate(pn.dense_owners(n)):

            @pl.when(b == bb)
            def _():
                first, tile = dense_cut(n, bb)
                total = drs[n, k, :, first:share].astype(F32)
                for d in range(1, nb):
                    other_b = lax.rem(b + d, nb)
                    v = drr.at[n, other_b, :, tile:]
                    i = pn.s_dr[n] + other_b
                    rcopy(v, v, i, i, {"ch": sib}).wait_recv()
                    total = total + drr[n, other_b, :, first:share].astype(F32)
                out[:, first:share] = total

    dense_stage(1, HEAD, dot_last(dr8[C : 2 * C, :], src[HEAD : HEAD + PRE, :]))
    dense_stage(1, HEAD + PRE, dot_last(dbuf[K * C : (K + 1) * C, :], x2[...]))
    plane_back(1, 1)
    sc0.end()
    slice_arrive(3)

    def inner_back(p, y_index):
        def body(r):
            y = ys[y_index, r, :]
            dz = value_back(y * kcol[p, r, 0:1] + kcol[p, r, 1:2], hold[0, r, :])
            hold[3, r, :] = dz
            pack_sums(r, [dz, dz * (y - kcol[p, r, 2:3])])

        blocks(body)

    def inner_dy(p, kept, y_index):
        def body(r):
            dyg[y_index, r, own_lanes] = grad_rows(
                hold[3, r, :], ys[y_index, r, :], kcol[kept, r, 0:1], kcol[kept, r, 2:3], kcol[p, r, 0:1], kcol[p, r, 1:2]
            )

        blocks(body)

    inner_back(2, 2)
    sum_start(5, 2)
    plane_total = plane_finish(1)
    plane_coefficients(1, plane_total)
    total = sum_finish(5)
    dense_copies(1, lambda cp: cp.start())
    inner_q, inner_g = total[0:1], total[1:2] * u2[1]
    usg_ref[0:1, :] = inner_q[:, 0:C]
    ugg_ref[0:1, :] = inner_g[:, 0:C]
    columns(5, [u2[2] * inner_q / count, u2[2] * u2[1] * inner_g / count])
    inner_dy(5, 2, 2)
    shift_all(2)
    sc1 = Scatter(1)
    sc1.compute(w2, 1)
    sc1.send()
    dy_start(2)
    plane_dr(1)
    sc1.send_dist(2)
    unit_grads(1)
    weight_grad(3, g23_hbm, K * C)
    sc1.end()

    def lower_back(r):
        v = hold[1, r, :]
        dv = value_back(v, hold[0, r, :])
        hold[2, r, :] = dv
        dvx[0, at_row(z * C, r), :] = dv.astype(BF16)
        pack_sums(r, [dv, dv * (ys[1, r, :] - kcol[1, r, 2:3]), dv * (resid[r, :] - kcol[1, r, 3:4])])

    blocks(lower_back)
    sum_start(6, 3)
    dv_copies(0, lambda cp: cp.start())
    total = sum_finish(6)
    unit_send(1)
    lower_q = total[0:1]
    lower_rsd = jnp.concatenate([l1[1], l8[1]], axis=0)
    lower_sc = jnp.concatenate([l1[2], l8[2]], axis=0)
    lower_g = total[1:3] * lower_rsd
    lsg_ref[1:11, :] = jnp.broadcast_to(lower_q[:, 0:C], (10, C))
    lgg_ref[1:2, :] = lower_g[0:1, 0:C]
    lgg_ref[10:11, :] = lower_g[1:2, 0:C]
    columns(6, [lower_sc * lower_q / count, lower_sc * lower_rsd * lower_g / count])

    def lower_grad(r, values, n):
        return grad_rows(
            hold[2, r, :],
            values,
            kcol[1, r, n : n + 1],
            kcol[1, r, 2 + n : 3 + n],
            kcol[6, r, n : n + 1],
            kcol[6, r, 2 + n : 3 + n],
        )

    def lower_dy(r):
        dyg[1, r, own_lanes] = lower_grad(r, ys[1, r, :], 0)

    blocks(lower_dy)
    shift_all(1)
    sc2 = Scatter(2)
    sc2.compute(w1, 0)
    sc2.send()
    dy_start(1)
    sc2.send_dist(2)

    def lower_dr(r):
        dr8[r, :] = lower_grad(r, resid[r, :], 1)

    blocks(lower_dr)
    dense_stage(0, HEAD, dot_last(dr8[0:C, :], src[HEAD : HEAD + PRE, :]))
    dense_copies(0, lambda cp: cp.start())
    plane_back(0, 2)
    weight_grad(2, g23_hbm, 0)
    unit_drain(1)
    unit_finish(1)
    sc2.end()

    inner_back(0, 0)
    sum_start(7, 2)
    plane_total = plane_finish(2)
    plane_coefficients(0, plane_total)
    plane_dr(0)
    unit_grads(0)
    total = sum_finish(7)
    unit_send(0)
    inner_q, inner_g = total[0:1], total[1:2] * rsd
    lsg_ref[0:1, :] = inner_q[:, 0:C]
    lgg_ref[0:1, :] = inner_g[:, 0:C]
    columns(7, [sc * inner_q / count, sc * rsd * inner_g / count])
    inner_dy(7, 0, 0)
    shift_all(0)
    dbuf[K * C : (K + 2) * C, :] = dr8[...]
    split = (PRE // 2 + LANES - 1) // LANES * LANES
    back_rows(w0, 2, slice(0, split), slice(0, split))
    back_rows(w0, 2, slice(split, PRE), slice(split, PRE))
    dy_start(0)

    def dp_sib(lc, n, k):
        v = dpo.at[lc : lc + n]
        i = pn.s_dp + 1 + k
        return rcopy(v, dpsib.at[lc : lc + n], i, i, {"ch": sib})

    def dp_bound(lc, n):
        return rcopy(dpo.at[lc : lc + n], dpbnd.at[0:n], pn.s_dp, pn.s_dp, below)

    def dp_compute(zc):
        for i, s in enumerate(pn.srcs[zc]):
            at, width = pn.pieces[s]
            lc = at - pn.lo[zc]
            r = rp[:, :, lc : lc + width].reshape(2 * rows_all, width)
            grad = dot_first(r, drp[i].reshape(2 * rows_all, T))
            dpo[lc : lc + width, :] = grad.astype(BF16)
        for k, (owner, row, n) in enumerate(pn.final[zc]):

            @pl.when(q != owner % 2)
            def _():
                dp_sib(row - pn.lo[zc], n, k).start()

    def dp_add(zc):
        for k, (owner, row, n) in enumerate(pn.final[zc]):
            lc = row - pn.lo[zc]

            @pl.when(q == owner % 2)
            def _():
                dp_sib(lc, n, k).wait_recv()
                total = dpo[lc : lc + n, :].astype(F32) + dpsib[lc : lc + n, :].astype(F32)
                if owner // 2 == zc:
                    at = WIDE + row - owner * E
                    big[at : at + n, :] = total * valid
                else:
                    dpo[lc : lc + n, :] = total.astype(BF16)
                    dp_bound(lc, n).start()

    def dp_drain(zc):
        for k, (owner, row, n) in enumerate(pn.final[zc]):
            lc = row - pn.lo[zc]

            @pl.when(q != owner % 2)
            def _():
                dp_sib(lc, n, k).wait_send()

            if owner // 2 != zc:

                @pl.when(q == owner % 2)
                def _():
                    dp_bound(lc, n).wait_send()

    count_late = len(pn.late)
    gx3.drain()
    for _, cp in slice_copies(3):
        cp.wait_send()

    def tail_rows(n):
        return x3.at[pn.late[n][2] - HEAD : pn.late[n][2] - HEAD + pn.step]

    def tail_sib(n):
        return rcopy(tail_rows(n), tailsib.at[n], pn.s_tail + n, pn.s_tail + n, {"ch": sib})

    def tail_hop(n, way, device):
        i = pn.s_tail + (1 + way) * count_late + n
        return rcopy(tail_rows(n), tailrecv.at[way, n], i, i, device)

    for n in range(count_late):
        there = slice(pn.late[n][2] - HEAD, pn.late[n][2] - HEAD + pn.step)

        @pl.when(q != pn.late[n][1])
        def _():
            x3[there, :] = big[there, :].astype(BF16)
            tail_sib(n).start()

    before, after = [], [True] * count_late
    for n in range(count_late):
        same = [m for m in range(n) if pn.late[m][:2] == pn.late[n][:2]]
        before.append(same[-pn.flight] if len(same) >= pn.flight else None)
        if len(same) >= pn.flight:
            after[same[-pn.flight]] = False

    def tail_give(n):
        i = pn.s_tail + 3 * count_late + n
        return rcopy(tail_rows(n), tailfin.at[given.index(n)], i, i, {"ch": sib})

    given = [n for n in range(count_late) if pn.late[n][3]]

    def chain():
        for n in range(count_late):
            zc, qc, row, moved = pn.late[n]
            there = slice(row - HEAD, row - HEAD + pn.step)

            @pl.when(q == qc)
            def _():
                tail_sib(n).wait_recv()
                big[there, :] += tailsib[n].astype(F32)
                if zc > 0:

                    @pl.when((z > 0) & (z <= zc))
                    def _():
                        tail_hop(n, 0, above).wait_recv()
                        big[there, :] += tailrecv[0, n].astype(F32)

                if zc < nz - 1:

                    @pl.when((z < nz - 1) & (z >= zc))
                    def _():
                        tail_hop(n, 1, below).wait_recv()
                        big[there, :] += tailrecv[1, n].astype(F32)

                @pl.when(z < zc)
                def _():
                    x3[there, :] = big[there, :].astype(BF16)
                    if before[n] is not None:
                        tail_hop(before[n], 0, above).wait_send()
                    tail_hop(n, 0, above).start()

                if zc < nz - 1:

                    @pl.when(z > zc)
                    def _():
                        x3[there, :] = big[there, :].astype(BF16)
                        if before[n] is not None:
                            tail_hop(before[n], 1, below).wait_send()
                        tail_hop(n, 1, below).start()

                @pl.when(z == zc)
                def _():
                    if moved:
                        x3[there, :] = big[there, :].astype(BF16)
                        tail_give(n).start()
                    else:
                        big[WIDE + row % E : WIDE + row % E + pn.step, :] = big[there, :] * valid

    place = z * 4 // nz

    def phase(i, carry):
        pl.when(i == place)(chain)

        @pl.when(i == 0)
        def _():
            at_chip(dp_compute)
            at_chip(dp_add)

        @pl.when(i == 1)
        def _():
            unit_finish(0)
            weight_grad(1, g1_hbm, 0)

        @pl.when(i == 2)
        def _():
            weight_grad(0, g0_hbm, 0)

        return carry

    lax.fori_loop(0, 4, phase, 0)
    for n in given:
        zc, qc, row, _ = pn.late[n]

        @pl.when((z == zc) & (q != qc))
        def _():
            tail_give(n).wait_recv()
            big[WIDE + row % E : WIDE + row % E + pn.step, :] = tailfin[given.index(n)].astype(F32) * valid

    for zc, qq, row, n in pn.bound:

        @pl.when((z == zc - 1) & (q == qq))
        def _():
            dp_v = dpbnd.at[0:n]
            rcopy(dp_v, dp_v, pn.s_dp, pn.s_dp, above).wait_recv()
            at = WIDE + row % E
            big[at : at + n, :] = dpbnd[0:n, :].astype(F32) * valid

    egrad_copy = pltpu.make_async_copy(big.at[WIDE : WIDE + E], egrad_hbm, osem.at[4])
    egrad_copy.start()
    result_finish(1, rug_ref)
    dense_finish(1, rug_ref)
    for blk, ref in ((0, lgg_ref), (1, ugg_ref)):
        for zc in range(nz):
            if pn.srcs[zc]:
                gain_v = grecv.at[blk, zc]

                @pl.when(z != zc)
                def _():
                    i = pn.s_gain + blk * nz + zc
                    rcopy(gain_v, gain_v, i, i, {"ch": sib}).wait_recv()

                for i, s in enumerate(pn.srcs[zc]):
                    ref[2 + s : 3 + s, :] = grecv[blk, zc, i : i + 1, 0:C]
    dense_finish(0, rlg_ref)
    result_finish(0, rlg_ref)

    out_copy().wait()
    egrad_copy.wait()
    entry_drain()
    sized(c, lambda n: own_rows(c, n).wait_send())
    for zc, qq, row, n in pn.bound:

        @pl.when((z == zc - 1) & (q == qq))
        def _():
            bound_hop(row, n).wait_send()

        @pl.when((z == zc) & (q == qq))
        def _():
            bound_sib(row, n).wait_send()

    for blk in (0, 1):
        r_hops(blk, 1, lambda cp: cp.wait_send())
        r_hops(blk, -1, lambda cp: cp.wait_send())
        r_passes(blk, lambda cp: cp.wait_send())
    for way in (1, -1):
        prm_copies(way, lambda cp: cp.wait_send())

    def q_drain(zc):
        for blk in (0, 1):
            for zz in range(nz):
                if zz != zc:
                    q_copy(blk, zz).wait_send()
                    gain_copy(blk, zz).wait_send()

    at_chip(q_drain)
    at_chip(dp_drain)
    for blk in (0, 1):
        dv_copies(blk, lambda cp: cp.wait_send())
        dense_copies(blk, lambda cp: cp.wait_send())
        result_drain(blk)
    unit_drain(0)
    gx2.drain()
    for p in range(8):
        for _, cp in sum_copies(p):
            cp.wait_send()
    for p in range(4):
        for _, cp in plane_copies(p):
            cp.wait_send()
    for j in range(4):
        slice_pass(j, lambda bb, cp: cp.wait_send())
        if j not in (1, 3):
            for _, cp in slice_copies(j):
                cp.wait_send()
        for _, cp in dy_copies(j):
            cp.wait_send()
    for n in range(count_late):
        zc, qc, _, moved = pn.late[n]

        @pl.when(q != qc)
        def _():
            tail_sib(n).wait_send()

        if moved:

            @pl.when((z == zc) & (q == qc))
            def _():
                tail_give(n).wait_send()

        if after[n]:

            @pl.when((q == qc) & (z < zc))
            def _():
                tail_hop(n, 0, above).wait_send()

        if after[n] and zc < nz - 1:

            @pl.when((q == qc) & (z > zc))
            def _():
                tail_hop(n, 1, below).wait_send()


def per_device(
    nb,
    nc,
    earlier,
    lengths,
    lower_entry,
    lower_convs,
    upper_convs,
    lower_dense,
    upper_dense,
    lower_gain,
    lower_shift,
    upper_gain,
    upper_shift,
    cotangent,
):
    _, own, frames = earlier.shape
    taps, cw, pre = lower_entry.shape
    pn = Plan(nb, nc, own, frames, taps, cw, pre)
    T, K, C, E, WIDE, nz = frames, taps, cw, own, pn.wide, pn.nz
    late = len(pn.late)
    share = ((pn.all + WIDE) // nb + LANES - 1) // LANES * LANES
    w0p, wp = up16(pn.iw0), up16(pn.iw)
    staged = 4 if (w0p != pn.iw0 or wp != pn.iw) else 1
    vmem, any_ = pl.BlockSpec(memory_space=pltpu.VMEM), pl.BlockSpec(memory_space=pl.ANY)
    smem = pl.BlockSpec(memory_space=pltpu.SMEM)
    V = pltpu.VMEM
    scratch = [
        V(((K + 2) * C, pre), BF16),
        V((K * C, WIDE), BF16),
        V(((K + 1) * C, WIDE), BF16),
        V((K * C, WIDE), BF16),
        V((2, nz * C, pn.pw), BF16),
        V((2, nz, pn.kr, C, LANES), BF16),
        V((pn.all, T), BF16),
        V((WIDE, T), BF16),
        V((WIDE, T), BF16),
        V((WIDE, T), BF16),
        V((WIDE + E, T), F32),
        V((2 * C, T), F32),
        V((C, T), F32),
        V((4, C, T), F32),
        V(((K + 2) * C, T), BF16),
        V((pn.slots, 2, nz * C, T), BF16),
        V((pn.slots, 2, nz * C, T), BF16),
        V((2 * C, T), BF16),
        V((2, nz * C, T), BF16),
        V((2, nz, C, T), BF16),
        V((2, nz * C, T), BF16),
        V((2, nz, 8, LANES), F32),
        V((2, nz, 8, LANES), F32),
        V((max(pn.pw, E), T), BF16),
        V((pn.pw, T), BF16),
        V((max([n for _, _, _, n in pn.bound] + [16]), T), BF16),
        V((pn.nu, nz * C, LANES), BF16),
        V((2, nb, pn.ku, nz * C, LANES), BF16),
        V((2, pn.ku, nz * C, LANES), BF16),
        V((2, len(pn.units), C, LANES), BF16),
        V((3, nz, C, T), BF16),
        V((3, 4, C, T), BF16),
        V((3, max(nz - 3, 1) * (2 if nz > 4 else 1), C, T), BF16),
        V((late, pn.step, T), BF16),
        V((1 + (pn.late[0][0] < nz - 1), late, pn.step, T), BF16),
        V((max(sum(x[3] for x in pn.late), 1), pn.step, T), BF16),
        V((4, C, nb * T), BF16),
        V((w0p, nb * T), BF16),
        V((3, wp, nb * T), BF16),
        V((4, nb, max(w0p, wp), T) if staged == 4 else (1, 1, 16, T), BF16),
        V((2, len(pn.dense_owners(1)), C, share), BF16),
        V((2, nb, C, share), BF16),
        V((8, nb, 40, LANES), F32),
        V((LANES, LANES), F32),
        V((LANES, LANES), F32),
        V((8, LANES, LANES), F32),
        V((4, nb, nz, 16, LANES), F32),
        V((nz, LANES, LANES), F32),
        V((nz, LANES, LANES), F32),
        V((nz, LANES, LANES), F32),
        V((4, 16, LANES), F32),
        V((nz, 4, 8, LANES), F32),
        V((4, C, T), F32),
        V((K * C, pn.iw), F32),
        pltpu.SemaphoreType.DMA((10 + 2 * nz * pn.kr,)),
        pltpu.SemaphoreType.DMA((5,)),
        pltpu.SemaphoreType.DMA((pn.sems,)),
        pltpu.SemaphoreType.DMA((pn.sems,)),
    ]
    shape = jax.ShapeDtypeStruct
    outs = pl.pallas_call(
        functools.partial(kernel, pn),
        out_shape=(
            shape((C, T), BF16),
            shape((E, T), F32),
            shape((K * C, pn.iw), F32),
            shape((K * C, pn.iw), F32),
            shape((2 * K * C, pn.iw), F32),
            shape((C, pn.all // nb), F32),
            shape((C, (pn.all + WIDE) // nb), F32),
            shape((11, C), F32),
            shape((11, C), F32),
            shape((12, C), F32),
            shape((12, C), F32),
        ),
        in_specs=[smem] + [any_] * 6 + [vmem] * 5,
        out_specs=(vmem, any_, any_, any_, any_, vmem, vmem, vmem, vmem, vmem, vmem),
        scratch_shapes=scratch,
        compiler_params=pltpu.CompilerParams(
            collective_id=0, has_side_effects=True, vmem_limit_bytes=64000 * 1024
        ),
    )(
        lengths,
        earlier.reshape(own, frames),
        lower_entry.reshape(K * C, pre),
        lower_convs.reshape(K * C, WIDE),
        upper_convs.reshape(2 * K * C, WIDE),
        lower_dense,
        upper_dense,
        lower_gain,
        lower_shift,
        upper_gain,
        upper_shift,
        cotangent.reshape(C, T),
    )
    final, egrad, g0, g1, g23, rlg, rug, lgg, lsg, ugg, usg = outs
    return (
        final.reshape(1, C, T),
        egrad.reshape(1, E, T),
        g0.reshape(K, C, pn.iw)[:, :, 0 : pn.iw0],
        g1.reshape(1, K, C, pn.iw),
        g23.reshape(2, K, C, pn.iw),
        rlg,
        rug,
        lgg,
        lsg,
        ugg,
        usg,
    )


def solution(mesh):
    placed = (
        P("batch", "ch", None),
        P("batch"),
        P(None, "ch", None),
        P(None, None, "ch", None),
        P(None, None, "ch", None),
        P("ch", None),
        P("ch", None),
        P(None, "ch"),
        P(None, "ch"),
        P(None, "ch"),
        P(None, "ch"),
        P("batch", "ch", None),
    )
    return jax.shard_map(
        functools.partial(per_device, mesh.shape["batch"], mesh.shape["ch"]),
        mesh=mesh,
        in_specs=placed,
        out_specs=(
            P("batch", "ch", None),
            P("batch", "ch", None),
            P(None, "ch", "batch"),
            P(None, None, "ch", "batch"),
            P(None, None, "ch", "batch"),
            P("ch", "batch"),
            P("ch", "batch"),
            P(None, "ch"),
            P(None, "ch"),
            P(None, "ch"),
            P(None, "ch"),
        ),
        check_vma=False,
    )
```

```python
import functools
import math

import jax
import jax.numpy as jnp
from jax import lax
from jax.experimental import pallas as pl
from jax.experimental.pallas import tpu as pltpu
from jax.sharding import PartitionSpec as P

EPS = 0.001
WIDTHS = (2, 2, 2, 3, 3, 4, 4, 5, 5)
MESH = pl.DeviceIdType.MESH
F32 = jnp.float32
BF16 = jnp.bfloat16
RB = 16
LANES = 128


def shifted(x, by):
    if by == 0:
        return x
    frames = x.shape[1]
    lane = lax.broadcasted_iota(jnp.int32, x.shape, 1)
    rolled = pltpu.roll(x, (-by) % frames, 1)
    keep = (lane < frames - by) if by > 0 else (lane >= -by)
    return jnp.where(keep, rolled, jnp.zeros_like(rolled))


def squash(v):
    return 0.5 * jnp.tanh(0.5 * v) + 0.5


def dot(a, b):
    return jnp.dot(a, b, preferred_element_type=F32)


def dot_first(a, b):
    return lax.dot_general(a, b, (((0,), (0,)), ((), ())), preferred_element_type=F32)


def dot_last(a, b):
    return lax.dot_general(a, b, (((1,), (1,)), ((), ())), preferred_element_type=F32)


class Plan:
    def __init__(self, nb, nc, own, frames, taps, cw, pre):
        self.nb, self.nc, self.nz = nb, nc, nc // 2
        self.own, self.frames, self.taps, self.cw, self.pre = own, frames, taps, cw, pre
        self.wide = cw * nc
        self.all = own * nc
        unit = self.all // 30
        self.pieces = []
        at = 0
        for w in WIDTHS:
            self.pieces.append((at, w * unit))
            at += w * unit
        self.head = self.all - pre
        self.full = self.head // own
        self.part = self.head % own
        step = math.gcd(own, self.head)
        self.step = max(n for n in (16, 32, 48) if step % n == 0)
        self.flight = 5
        self.late = []
        for chip in range(self.nz):
            rows = [[r for r in range(self.head, self.all, self.step) if r // own == chip * 2 + core] for core in (0, 1)]
            heavy = 0 if len(rows[0]) > len(rows[1]) else 1
            extra = (len(rows[heavy]) - len(rows[1 - heavy])) // 2
            moved = rows[heavy][len(rows[heavy]) - extra :]
            for core in (0, 1):
                keep = [r for r in rows[core] if r not in moved]
                self.late += [(chip, core, r, False) for r in keep]
                if core != heavy:
                    self.late += [(chip, core, r, True) for r in moved]
        self.iw0 = pre // nb
        self.iw = self.wide // nb
        self.group = 5
        self.sems = 0
        nz = self.nz
        self.srcs = [[] for _ in range(nz)]
        for s, (at, width) in enumerate(self.pieces[:-1]):
            self.srcs[(at + width - 1) // (2 * own)].append(s)
        if len(self.srcs[0]) > 2:
            self.srcs[1].insert(0, self.srcs[0].pop())
        self.lo, self.width = [0] * nz, [0] * nz
        self.bound, self.final = [], [[] for _ in range(nz)]
        for zc in range(nz):
            if not self.srcs[zc]:
                continue
            first, last = self.pieces[self.srcs[zc][0]], self.pieces[self.srcs[zc][-1]]
            self.lo[zc], self.width[zc] = first[0], last[0] + last[1] - first[0]
            row = first[0]
            while row < last[0] + last[1]:
                end = min((row // own + 1) * own, last[0] + last[1])
                self.final[zc].append((row // own, row, end - row))
                if row // own // 2 < zc:
                    self.bound.append((zc, row // own % 2, row, end - row))
                row = end
        self.slots = max(len(x) for x in self.srcs)
        self.pw = max(self.width)
        self.split = 4
        self.units = [(zc, u, u % nb) for zc in range(nz) for u in range(self.width[zc] // LANES)]
        self.nu = self.pw // LANES
        self.ku = (self.nu + nb - 1) // nb
        self.s_entry = self.take(2 * len(self.late))
        self.s_src = self.take(3)
        self.kr = (self.nu + self.split - 1) // self.split
        self.s_r1 = [self.take(nz * self.kr) for _ in range(2)]
        self.s_r2 = [self.take(self.split * nz * self.kr) for _ in range(2)]
        self.s_prm = self.take(nz)
        self.s_q = [self.take(4 * nz + 1) for _ in range(2)]
        self.s_plane = [self.take(nb) for _ in range(4)]
        self.s_dv = self.take(2 * nz)
        self.s_gain = self.take(2 * nz)
        self.s_d1 = [self.take(nb * self.nu) for _ in range(2)]
        self.s_d2 = [self.take(max(self.ku * nz * 2, len(self.units))) for _ in range(2)]
        self.s_x = [self.take(4 + 2 * nz) for _ in range(3)]
        self.s_sum = [self.take(nb) for _ in range(8)]
        self.s_xs = [self.take(nb) for _ in range(4)]
        self.s_xp = [self.take(nb) for _ in range(4)]
        self.s_dy = [self.take(nb) for _ in range(4)]
        self.s_rs = [self.take(4 + 4 * nz) for _ in range(3)]
        self.s_dp = self.take(1 + max(len(x) for x in self.final))
        self.s_tail = self.take(4 * len(self.late))
        self.s_dr = [self.take(nb) for _ in range(2)]

    def share(self, blk):
        return (self.all + (self.wide if blk else 0)) // self.nb

    def dense_owners(self, blk):
        return [bb for bb in range(self.nb) if (bb + 1) * self.share(blk) > self.head]

    def take(self, count):
        base = self.sems
        self.sems += count
        return base


def up16(n):
    return (n + 15) // 16 * 16


SUM_ROWS = (8, 8, 8, 8, 8, 8, 8, 8)


def kernel(
    pn,
    length_ref,
    earlier_hbm,
    w0_hbm,
    w1_hbm,
    w23_hbm,
    rl_hbm,
    ru_hbm,
    lg_ref,
    lsh_ref,
    ug_ref,
    ush_ref,
    cot_ref,
    final_ref,
    egrad_hbm,
    g0_hbm,
    g1_hbm,
    g23_hbm,
    rlg_ref,
    rug_ref,
    lgg_ref,
    lsg_ref,
    ugg_ref,
    usg_ref,
    w0,
    w1,
    w2,
    w3,
    rp,
    rown,
    src,
    x1,
    x2,
    x3,
    big,
    resid,
    rmid,
    ys,
    dbuf,
    pr,
    drp,
    dr8,
    qpart,
    qrecv,
    qcomb,
    dvx,
    gsend,
    grecv,
    dpo,
    dpsib,
    dpbnd,
    d1send,
    d1recv,
    d2send,
    d2recv,
    dxsib,
    dxrecv,
    dxcomb,
    tailsib,
    tailrecv,
    tailfin,
    dyg,
    xs0,
    xs,
    xst,
    drs,
    drr,
    sums,
    colbuf,
    rowbuf,
    kcol,
    psums,
    pcol,
    prow,
    pk,
    prm,
    prms,
    hold,
    gout,
    lsem,
    osem,
    ss,
    rs,
):
    nb, nc, nz = pn.nb, pn.nc, pn.nz
    T, K, C, E = pn.frames, pn.taps, pn.cw, pn.own
    WIDE, PRE, HEAD = pn.wide, pn.pre, pn.head
    b = lax.axis_index("batch")
    c = lax.axis_index("ch")
    z = c // 2
    q = lax.rem(c, 2)
    sib = z * 2 + 1 - q
    other = 1 - q

    def mult(v, m=16):
        return pl.multiple_of(v, m)

    def rcopy(source, target, i_send, i_recv, device):
        return pltpu.make_async_remote_copy(
            src_ref=source,
            dst_ref=target,
            send_sem=ss.at[i_send],
            recv_sem=rs.at[i_recv],
            device_id=device,
            device_id_type=MESH,
        )

    def chip(zz, qq):
        return {"ch": zz * 2 + qq}

    local_loads = []

    def load(source, target):
        cp = pltpu.make_async_copy(source, target, lsem.at[len(local_loads)])
        local_loads.append(cp)
        cp.start()
        return cp

    raw = dpo
    ld_raw = load(earlier_hbm, raw.at[0:E])
    ld_w0 = load(w0_hbm, w0.at[0 : K * C])
    ld_w0l = load(rl_hbm.at[:, HEAD : HEAD + PRE], w0.at[K * C : (K + 1) * C])
    ld_w0u = load(ru_hbm.at[:, HEAD : HEAD + PRE], w0.at[(K + 1) * C : (K + 2) * C])
    dense = (rl_hbm, ru_hbm)

    def at_chip(body):
        for zc in range(nz):
            if pn.srcs[zc]:

                @pl.when(z == zc)
                def _():
                    body(zc)

    def own_dense(zc, blk):
        w = pn.width[zc]
        source = dense[blk].at[:, pn.lo[zc] : pn.lo[zc] + w]
        return pltpu.make_async_copy(source, rp.at[blk, zc * C : (zc + 1) * C, 0:w], lsem.at[8 + blk])


    bar = pltpu.get_barrier_semaphore()
    pl.semaphore_signal(bar, inc=1, device_id={"ch": sib}, device_id_type=MESH)
    for d in range(1, nz):
        pl.semaphore_signal(bar, inc=1, device_id=chip(lax.rem(z + d, nz), q), device_id_type=MESH)
    for d in range(1, nb):
        pl.semaphore_signal(bar, inc=1, device_id={"batch": lax.rem(b + d, nb)}, device_id_type=MESH)

    rowbuf[...] = jnp.zeros_like(rowbuf)
    colbuf[...] = jnp.zeros_like(colbuf)
    pcol[...] = jnp.zeros_like(pcol)
    prow[...] = jnp.zeros_like(prow)
    prm[...] = jnp.zeros_like(prm)
    prm[0, 0:11, 0:C] = lg_ref[...]
    prm[1, 0:11, 0:C] = lsh_ref[...]
    prm[2, 0:12, 0:C] = ug_ref[...]
    prm[3, 0:12, 0:C] = ush_ref[...]
    prms[z] = prm[:, 2:10, :]
    length = length_ref[0]
    lane_row = lax.broadcasted_iota(jnp.int32, (1, T), 1)
    valid = jnp.where(lane_row < length, 1.0, 0.0).astype(F32)
    valid_rb = jnp.broadcast_to(valid, (RB, T))

    ld_raw.wait()
    valid_b = valid.astype(BF16)

    def mask_rows(i, _):
        src[pl.ds(mult(c * E + i * RB), RB), :] = raw[pl.ds(mult(i * RB), RB), :] * jnp.broadcast_to(
            valid_b, (RB, T)
        )
        return 0

    lax.fori_loop(0, E // RB, mask_rows, 0, unroll=2)
    pl.semaphore_wait(bar, 1 + (nz - 1) + (nb - 1))

    def sized(cc, body):
        @pl.when(cc < pn.full)
        def _():
            body(E)

        if pn.part:

            @pl.when(cc == pn.full)
            def _():
                body(pn.part)

    def inside(zz):
        return (zz >= 0) & (zz < nz)

    class Gather:
        def __init__(self, base, buf, rows):
            self.base, self.buf, self.rows = base, buf, rows

        def view(self, zz, qq):
            return self.buf.at[pl.ds(mult((zz * 2 + qq) * self.rows), self.rows)]

        def own_copy(self, way, dist):
            v = self.view(z, q)
            i = self.base + (0 if way > 0 else 2) + dist - 1
            return rcopy(v, v, i, self.base + 4 + z, chip(z + way * dist, q))

        def on_copy(self, way, zz):
            v = self.view(zz, q)
            return rcopy(v, v, self.base + 4 + zz, self.base + 4 + zz, chip(z + way, q))

        def sib_copy(self, zz, qq):
            i = self.base + 4 + nz + zz
            return rcopy(self.view(zz, qq), self.view(zz, qq), i, i, {"ch": sib})

        def start(self):
            for dist in (2, 1):
                for way in (1, -1):

                    @pl.when(inside(z + way * dist))
                    def _():
                        self.own_copy(way, dist).start()

            self.sib_copy(z, q).start()

        def arrive(self):
            for dist in [2, 1] + list(range(3, nz)):
                for way in (1, -1):
                    zz = z - way * dist

                    @pl.when(inside(zz))
                    def _():
                        self.on_copy(way, zz).wait_recv()
                        if dist >= 2:

                            @pl.when(inside(z + way))
                            def _():
                                self.on_copy(way, zz).start()

                        self.sib_copy(zz, q).start()

        def end(self):
            for zz in range(nz):
                self.sib_copy(zz, other).wait_recv()

        def drain(self):
            for way in (1, -1):
                for dist in (1, 2):

                    @pl.when(inside(z + way * dist))
                    def _():
                        self.own_copy(way, dist).wait_send()

                for dist in range(2, nz):

                    @pl.when(inside(z - way * dist) & inside(z + way))
                    def _():
                        self.on_copy(way, z - way * dist).wait_send()

            for zz in range(nz):
                self.sib_copy(zz, q).wait_send()

    above = chip(jnp.minimum(z + 1, nz - 1), q)
    below = chip(jnp.maximum(z - 1, 0), q)

    def own_rows(cc, n):
        v = src.at[pl.ds(mult(cc * E), n)]
        return rcopy(v, v, pn.s_src, pn.s_src, {"ch": sib})

    def bound_hop(row, n):
        v = src.at[row : row + n]
        return rcopy(v, v, pn.s_src + 1, pn.s_src + 1, above)

    def bound_sib(row, n):
        v = src.at[row : row + n]
        return rcopy(v, v, pn.s_src + 2, pn.s_src + 2, {"ch": sib})

    in_group = lax.rem(b, pn.split)

    def r_units(zc, member, body):
        for k in range(pn.kr):
            u = member + pn.split * k

            @pl.when(u < pn.width[zc] // LANES)
            def _():
                body(k, pl.ds(mult(u * LANES, LANES), LANES))

    def r_load(blk, zc, k, cols):
        first = mult(pn.lo[zc] + cols.start, LANES)
        i = 10 + (blk * nz + zc) * pn.kr + k
        return pltpu.make_async_copy(dense[blk].at[:, pl.ds(first, LANES)], rown.at[blk, zc, k], lsem.at[i])

    def r_loads(blk, act):
        for zc in range(nz):
            if pn.width[zc]:

                @pl.when(z != zc)
                def _():
                    r_units(zc, in_group, lambda k, cols: act(r_load(blk, zc, k, cols)))

    def r_hop(blk, zc, k, cols):
        target = rp.at[blk, pl.ds(mult(z * C), C), cols]
        i = pn.s_r1[blk]
        return rcopy(rown.at[blk, zc, k], target, i + zc * pn.kr + k, i + z * pn.kr + k, chip(zc, q))

    def r_hops(blk, way, act):
        for zc in range(nz):
            if pn.width[zc]:

                @pl.when((z < zc) if way > 0 else (z > zc))
                def _():
                    r_units(zc, in_group, lambda k, cols: act(r_hop(blk, zc, k, cols)))

    def r_shared(blk, zf, k, cols, member):
        v = rp.at[blk, zf * C : (zf + 1) * C, cols]
        i = pn.s_r2[blk] + k
        to = b - in_group + member
        return rcopy(v, v, i + (member * nz + zf) * pn.kr, i + (in_group * nz + zf) * pn.kr, {"batch": to})

    def r_passes(blk, act):
        def run(zc):
            for zf in range(nz):
                if zf != zc:

                    def unit(k, cols):
                        for d in range(1, pn.split):
                            act(r_shared(blk, zf, k, cols, lax.rem(in_group + d, pn.split)))

                    r_units(zc, in_group, unit)

        at_chip(run)

    def r_arrive(blk):
        def run(zc):
            for zf in range(nz):
                if zf != zc:

                    def unit(k, cols):
                        v = rp.at[blk, zf * C : (zf + 1) * C, cols]
                        i = pn.s_r1[blk] + zf * pn.kr + k
                        rcopy(v, v, i, i, {"ch": sib}).wait_recv()
                        for d in range(1, pn.split):
                            r_shared(blk, zf, k, cols, lax.rem(in_group + d, pn.split)).start()

                    r_units(zc, in_group, unit)

        at_chip(run)

    def r_finish(blk):
        def run(zc):
            own_dense(zc, blk).wait()
            for d in range(1, pn.split):
                member = lax.rem(in_group + d, pn.split)
                for zf in range(nz):
                    if zf != zc:

                        def unit(k, cols):
                            v = rp.at[blk, zf * C : (zf + 1) * C, cols]
                            i = pn.s_r2[blk] + (member * nz + zf) * pn.kr + k
                            rcopy(v, v, i, i, {"ch": sib}).wait_recv()

                        r_units(zc, member, unit)

        at_chip(run)

    for blk in (0, 1):
        r_loads(blk, lambda cp: cp.start())

    def start_own_dense(zc):
        own_dense(zc, 0).start()
        own_dense(zc, 1).start()

    at_chip(start_own_dense)
    ld_w1 = load(w1_hbm, w1)
    ld_w2 = load(w23_hbm.at[0 : K * C], w2.at[0 : K * C])
    ld_w2m = load(ru_hbm.at[:, HEAD + PRE : HEAD + PRE + WIDE], w2.at[K * C : (K + 1) * C])
    ld_w3 = load(w23_hbm.at[K * C : 2 * K * C], w3)

    def others(body):
        for d in range(1, nz):
            body(lax.rem(z + d, nz))

    def prm_copy(zz):
        return rcopy(prms.at[z], prms.at[z], pn.s_prm + zz, pn.s_prm + z, chip(zz, q))

    def prm_copies(way, act):
        for zz in range(nz):

            @pl.when((z < zz) if way > 0 else (z > zz))
            def _():
                act(prm_copy(zz))

    def prm_arrive(zz):
        rcopy(prms.at[zz], prms.at[zz], pn.s_prm + zz, pn.s_prm + zz, {"ch": sib}).wait_recv()

    sized(c, lambda n: own_rows(c, n).start())
    for zc, qq, row, n in pn.bound:

        @pl.when((z == zc - 1) & (q == qq))
        def _():
            bound_hop(row, n).start()

    def entry_rows(n):
        return src.at[pn.late[n][2] : pn.late[n][2] + pn.step]

    def entry_hop(n, device):
        v = entry_rows(n)
        return rcopy(v, v, pn.s_entry + n, pn.s_entry + n, device)

    def entry_sib(n):
        i = pn.s_entry + len(pn.late) + n
        return rcopy(entry_rows(n), entry_rows(n), i, i, {"ch": sib})

    order = [n for n in range(len(pn.late))]
    def entry_up(n):
        return rcopy(entry_rows(n), entry_rows(n), pn.s_tail + n, pn.s_entry + n, above)

    for n in order:
        zc, qc, _, moved = pn.late[n]
        if moved:

            @pl.when((q != qc) & (z == zc))
            def _():
                entry_sib(n).start()

    for zc, qc in sorted({x[:2] for x in pn.late}):
        mine = [n for n in order if pn.late[n][:2] == (zc, qc)]

        @pl.when((q == qc) & (z == zc))
        def _():
            for at, n in enumerate(mine):
                if at >= pn.flight:
                    if zc > 0:
                        entry_hop(mine[at - pn.flight], below).wait_send()
                    if zc < nz - 1:
                        entry_up(mine[at - pn.flight]).wait_send()
                if pn.late[n][3]:
                    entry_sib(n).wait_recv()
                else:
                    entry_sib(n).start()
                if zc > 0:
                    entry_hop(n, below).start()
                if zc < nz - 1:
                    entry_up(n).start()
            for n in mine[-pn.flight :]:
                if zc > 0:
                    entry_hop(n, below).wait_send()
                if zc < nz - 1:
                    entry_up(n).wait_send()

    for blk in (0, 1):
        r_loads(blk, lambda cp: cp.wait())
        r_hops(blk, 1, lambda cp: cp.start())
    prm_copies(1, lambda cp: cp.start())
    for n in order:
        zc, qc, _, moved = pn.late[n]

        @pl.when((q == qc) & (z < zc))
        def _():
            entry_hop(n, below).wait_recv()

            @pl.when(z > 0)
            def _():
                entry_hop(n, below).start()

            entry_sib(n).start()

        if zc < nz - 1:

            @pl.when((q == qc) & (z > zc))
            def _():
                entry_hop(n, above).wait_recv()

                @pl.when(z < nz - 1)
                def _():
                    entry_hop(n, above).start()

                entry_sib(n).start()

    for n in order:

        zc, qc, _, moved = pn.late[n]

        @pl.when((q != qc) & (z != zc) if moved else q != qc)
        def _():
            entry_sib(n).wait_recv()

    def entry_drain():
        for n in order:
            zc, qc, _, moved = pn.late[n]

            @pl.when(((q == qc) & (z != zc)) | ((q != qc) & (z == zc)) if moved else q == qc)
            def _():
                entry_sib(n).wait_send()

            @pl.when((q == qc) & (z < zc) & (z > 0))
            def _():
                entry_hop(n, below).wait_send()

            if zc < nz - 1:

                @pl.when((q == qc) & (z > zc) & (z < nz - 1))
                def _():
                    entry_hop(n, above).wait_send()

    def sum_copies(p):
        rows = SUM_ROWS[p]
        for d in range(1, nb):
            bb = lax.rem(b + d, nb)
            v = sums.at[p, b, 0:rows]
            yield bb, rcopy(v, v, pn.s_sum[p] + bb, pn.s_sum[p] + b, {"batch": bb})


    def tree(parts):
        tiles = range(0, T, LANES)
        parts = [v if v is None else functools.reduce(jnp.add, [v[:, i : i + LANES] for i in tiles]) for v in parts]
        lane_of = lax.broadcasted_iota(jnp.int32, (parts[0].shape[0], LANES), 1)
        size = 1
        while size < len(parts):
            size *= 2
        parts = parts + [None] * (size - len(parts))
        width = LANES
        while len(parts) > 1:
            width //= 2
            low = (lane_of // width) % 2 == 0
            fold = []
            for x, y in zip(parts[: len(parts) // 2], parts[len(parts) // 2 :]):
                y = x if y is None else y
                if x is None:
                    fold.append(None)
                elif width * 2 == LANES:
                    fold.append(jnp.where(low, x, y) + pltpu.roll(jnp.where(low, y, x), width, 1))
                else:
                    fold.append(
                        jnp.where(low, x + pltpu.roll(x, LANES - width, 1), y + pltpu.roll(y, width, 1))
                    )
            parts = fold
        total = parts[0]
        while width > 1:
            width //= 2
            total = total + pltpu.roll(total, LANES - width, 1)
        return total

    def pack_sums(r, parts):
        colbuf[r, :] = tree(parts)

    def sum_start(p, count, constant=None):
        size = 1
        while size < count:
            size *= 2
        rowbuf[...] = colbuf[...].T
        sums[p, b, 0:count, :] = rowbuf[pl.ds(0, count, stride=LANES // size), :]
        if constant is not None:
            sums[p, b, count : count + 1, :] = constant
        for _, cp in sum_copies(p):
            cp.start()

    def sum_finish(p):
        rows = SUM_ROWS[p]
        for bb, _ in sum_copies(p):
            v = sums.at[p, bb, 0:rows]
            rcopy(v, v, pn.s_sum[p] + bb, pn.s_sum[p] + bb, {"batch": bb}).wait_recv()
        total = sums[p, 0, 0:rows, :]
        for bb in range(1, nb):
            total = total + sums[p, bb, 0:rows, :]
        return total

    def columns(p, parts):
        at = 0
        for part in parts:
            rowbuf[at : at + part.shape[0], :] = part
            at += part.shape[0]
        kcol[p] = rowbuf[...].T

    def norm_rows(first, second, count, gain, shift):
        average = first / count
        scaling = lax.rsqrt(second / count - average * average + EPS)
        scale = scaling * gain
        return average, scaling, scale, shift - average * scale

    def blocks(body):
        for i in range(0, C, RB):
            body(pl.ds(i, RB))

    def rolled(body):
        def step(i, carry):
            body(pl.ds(mult(i * RB), RB))
            return carry

        lax.fori_loop(0, C // RB, step, 0)

    def at_row(base, r):
        if isinstance(base, int) and isinstance(r.start, int):
            return pl.ds(base + r.start, RB)
        return pl.ds(mult(base + r.start), RB)

    def conv(w, x, y_index, more=None):
        if more is not None:
            more[...] = dot(w[K * C : K * C + more.shape[0], :], x)
        for i in range(0, C, RB):
            taps = jnp.concatenate([w[k * C + i : k * C + i + RB, :] for k in range(K)], axis=0)
            rows = dot(taps, x)
            total = None
            for k in range(K):
                v = shifted(rows[k * RB : (k + 1) * RB], k - K // 2)
                total = v if total is None else total + v
            ys[y_index, i : i + RB, :] = total

    def conv_sums(y_index):
        def body(r):
            y = ys[y_index, r, :] * valid_rb
            pack_sums(r, [y, y * y])

        blocks(body)

    def slices(j):
        if j == 0:
            return src, HEAD, pn.iw0, xs0
        return (None, x1, x2, x3)[j], 0, pn.iw, xs.at[j - 1]

    def half_rows(j, core):
        iw = slices(j)[2]
        if iw % 32:
            return 0, up16(iw)
        return mult(core * (iw // 2)), iw // 2

    def slice_half(j, core, bb):
        first, many = half_rows(j, core)
        return slices(j)[3].at[pl.ds(first, many), pl.ds(mult(bb * T, LANES), T)]

    def slice_pass(j, act):
        if slices(j)[2] % 32 == 0:
            for d in range(1, nb):
                bb = lax.rem(b + d, nb)
                i = pn.s_xp[j] + bb
                v = slice_half(j, q, bb)
                act(bb, rcopy(v, v, i, i, {"ch": sib}))

    def slice_arrive(j):
        def take(bb, cp):
            v = slice_half(j, q, bb)
            rcopy(v, v, pn.s_xs[j] + bb, pn.s_xs[j] + bb, {"batch": bb}).wait_recv()
            cp.start()

        slice_pass(j, take)

    def slice_copies(j):
        x, base, iw, target = slices(j)
        rows = up16(iw)
        for d in range(1, nb):
            bb = lax.rem(b + d, nb)
            if rows == iw:
                first, many = half_rows(j, q)
                source = x.at[pl.ds(mult(base + bb * iw + first), many)]
            else:
                source = xst.at[j, bb, 0:rows]
            there = slice_half(j, q, b)
            yield bb, rcopy(source, there, pn.s_xs[j] + bb, pn.s_xs[j] + b, {"batch": bb})

    def slice_start(j):
        x, base, iw, target = slices(j)
        rows = up16(iw)
        here = pl.ds(mult(b * T, LANES), T)
        if rows == iw:
            target[:, here] = x[pl.ds(mult(base + b * iw), iw), :]
        else:
            for bb in range(nb):
                xst[j, bb, 0:rows, :] = jnp.zeros((rows, T), BF16)
                xst[j, bb, 0:iw, :] = x[base + bb * iw : base + (bb + 1) * iw, :]
            target[:, here] = xst[j, b, 0:rows, :]
        for _, cp in slice_copies(j):
            cp.start()

    def slice_finish(j):
        for bb, _ in slice_copies(j):
            if slices(j)[2] % 32 == 0:
                v, i = slice_half(j, other, bb), pn.s_xp[j] + bb
            else:
                v, i = slice_half(j, q, bb), pn.s_xs[j] + bb
            rcopy(v, v, i, i, {"ch": sib}).wait_recv()

    def dy_copies(j):
        v = dyg.at[j, :, pl.ds(mult(b * T, LANES), T)]
        for d in range(1, nb):
            bb = lax.rem(b + d, nb)
            yield bb, rcopy(v, v, pn.s_dy[j] + bb, pn.s_dy[j] + b, {"batch": bb})

    def dy_start(j):
        for _, cp in dy_copies(j):
            cp.start()

    def dy_finish(j):
        for bb, _ in dy_copies(j):
            v = dyg.at[j, :, pl.ds(mult(bb * T, LANES), T)]
            rcopy(v, v, pn.s_dy[j] + bb, pn.s_dy[j] + bb, {"batch": bb}).wait_recv()

    out_copies = []

    def out_copy():
        out, first, k = out_copies[-1]
        return pltpu.make_async_copy(gout, out.at[first : first + K * C], osem.at[k])

    def weight_grad(j, out, first, groups=range(K // pn.group)):
        _, _, iw, target = slices(j)
        rows = pn.group * C
        for g in groups:
            if g == 0:
                if out_copies:
                    out_copy().wait()
                slice_finish(j)
                dy_finish(j)

            grad = None
            for u in range(nb):
                here = slice(u * T, (u + 1) * T)
                dy = dyg[j, :, here]
                taps = [shifted(dy, K // 2 - g * pn.group - i) for i in range(pn.group)]
                v = dot_last(jnp.concatenate(taps, axis=0), target[:, here])
                grad = v if grad is None else grad + v
            gout[g * rows : (g + 1) * rows, 0:iw] = grad[:, 0:iw]
            if g == K // pn.group - 1:
                out_copies.append((out, first, len(out_copies)))
                out_copy().start()

    half = WIDE // 2
    hz = nz // 2
    upper_half = z // hz

    def shift_all(j):
        dy = dyg[j, :, pl.ds(mult(b * T, LANES), T)]
        for k in range(K):
            dbuf[k * C : (k + 1) * C, :] = shifted(dy, K // 2 - k)

    def back_rows(w, extra, lanes, to):
        rows = (K + extra) * C
        big[to, :] = dot_first(w[0:rows, lanes], dbuf[0:rows, :])

    class Scatter:
        def __init__(self, n):
            self.base, self.part, self.sibs, self.recv = pn.s_rs[n], x1, dxsib.at[n], dxrecv.at[n]
            self.combs = dxcomb.at[n]

        def rows(self, zz, qq):
            return pl.ds(mult((zz * 2 + qq) * C), C)

        def to_sib(self, zz):
            return rcopy(
                self.part.at[self.rows(zz, other)],
                self.sibs.at[zz],
                self.base + 4 + zz,
                self.base + 4 + zz,
                {"ch": sib},
            )

        def slot(self, way, dist):
            return (0 if way > 0 else 2) + dist - 1

        def comb(self, way, dist):
            first = 0 if way > 0 or nz <= 4 else nz - 3
            return self.combs.at[first + dist - 2], self.base + 4 + nz + (0 if way > 0 else nz) + dist

        def out(self, way, dist):
            zz = z + way * dist
            source = self.part.at[self.rows(zz, q)]
            i_send = self.base + 4 + 3 * nz + zz
            if dist <= 2:
                at = self.slot(way, dist)
                return rcopy(source, self.recv.at[at], i_send, self.base + at, chip(zz, q))
            target, i = self.comb(way, dist - 1)
            return rcopy(source, target, i_send, i, chip(z + way, q))

        def compute(self, w, extra):
            for far in (1, 0):
                m = upper_half + far - 2 * upper_half * far
                at = pl.ds(mult(m * half, LANES), half)
                back_rows(w, extra, at, at)
                for i in range(hz):
                    zz = m * hz + i
                    r = self.rows(zz, other)
                    self.part[r, :] = big[r, :].astype(BF16)
                    self.to_sib(zz).start()

        def fold(self, zz):
            self.to_sib(zz).wait_recv()
            return big[self.rows(zz, q), :] + self.sibs[zz].astype(F32)

        def send_dist(self, dist):
            for way in (1, -1):
                zz = z + way * dist

                @pl.when(inside(zz))
                def _():
                    total = self.fold(zz)
                    if dist >= 2:
                        big[self.rows(zz, q), :] = total

                        @pl.when(inside(z - way))
                        def _():
                            v, i = self.comb(way, dist)
                            rcopy(v, v, i, i, {"ch": sib}).wait_recv()
                            big[self.rows(zz, q), :] += v[...].astype(F32)

                        total = big[self.rows(zz, q), :]
                    self.part[self.rows(zz, q), :] = total.astype(BF16)
                    self.out(way, dist).start()

        def send(self):
            for dist in list(range(nz - 1, 2, -1)) + [1]:
                self.send_dist(dist)
            hold[0] = self.fold(z)

        def end(self):
            for dist in (1, 2):
                for way in (1, -1):

                    @pl.when(inside(z - way * dist))
                    def _():
                        at = self.slot(way, dist)
                        v = self.recv.at[at]
                        rcopy(v, v, self.base + at, self.base + at, {"ch": sib}).wait_recv()
                        hold[0] += v[...].astype(F32)

            self.drain()

        def drain(self):
            for d in range(nz):
                self.to_sib(lax.rem(z + d, nz)).wait_send()
            for way in (1, -1):
                for dist in range(1, nz):

                    @pl.when(inside(z + way * dist))
                    def _():
                        self.out(way, dist).wait_send()

    rows_all = nz * C

    def plane_rows(body, straight=False):
        if straight:
            for zz in range(nz):
                body(zz * C, zz, pl.ds(0, C))
            return

        def step(zz, carry):
            body(mult(zz * C), zz, pl.ds(0, C))
            return carry

        lax.fori_loop(0, nz, step, 0)


    def plane_sums(body, slot, step):
        def run(row, zz, r):
            total = tree(body(row))
            if slot > 0:
                lane_mod = lax.broadcasted_iota(jnp.int32, total.shape, 1) % step
                total = jnp.where(lane_mod == slot, pltpu.roll(total, slot, 1), pcol[zz, r, :])
            pcol[zz, r, :] = total

        plane_rows(run, True)

    def at_slot(i, body):
        chips = [zc for zc in range(nz) if len(pn.srcs[zc]) > i]
        pl.when(functools.reduce(jnp.logical_or, [z == zc for zc in chips]))(body)

    def plane_copies(p):
        v = psums.at[p, b]
        for d in range(1, nb):
            bb = lax.rem(b + d, nb)
            yield bb, rcopy(v, v, pn.s_plane[p] + bb, pn.s_plane[p] + b, {"batch": bb})

    def plane_start(p, groups, step):
        for zz in range(nz):
            prow[zz] = pcol[zz].T
            for n in range(groups):
                psums[p, b, zz, 4 * n : 4 * n + 4, :] = prow[zz, step * n : step * n + 4, :]
        for _, cp in plane_copies(p):
            cp.start()

    def plane_finish(p):
        for bb, _ in plane_copies(p):
            v = psums.at[p, bb]
            rcopy(v, v, pn.s_plane[p] + bb, pn.s_plane[p] + bb, {"batch": bb}).wait_recv()
        total = psums[p, 0]
        for bb in range(1, nb):
            total = total + psums[p, bb]
        return total

    def project(zc, s, blk):
        at, width = pn.pieces[s]
        place = at - pn.lo[zc]
        big[0:rows_all, :] = dot(rp[blk, :, place : place + width], src[at : at + width, :])

    def project_slot(i, blk):
        def run(zc):
            if len(pn.srcs[zc]) > i:
                project(zc, pn.srcs[zc][i], blk)

        at_chip(run)

    def plane_first(blk):
        for i in range(pn.slots):
            project_slot(i, blk)

            def parts(row):
                v = big[pl.ds(row, C), :]
                return [v, v * v]

            at_slot(i, lambda: plane_sums(parts, i, 64))

    def base(blk, i):
        return blk * 4 + i

    def plane_norms(zc, total, blk):
        shift_sum = None
        for i, s in enumerate(pn.srcs[zc]):
            gain, shift = prms[:, 2 * blk, s, :], prms[:, 2 * blk + 1, s, :]
            p_av, p_rsd, p_sc, _ = norm_rows(total[:, i], total[:, 4 + i], count, gain, shift)
            pk[:, base(blk, i), :] = p_rsd
            pk[:, 8 + base(blk, i), :] = p_av
            pk[:, 16 + base(blk, i), :] = gain
            pk[:, 48 + base(blk, i), :] = p_sc
            shift_sum = shift if shift_sum is None else shift_sum + shift
        pk[:, 24 + blk, :] = shift_sum
        for zz in range(nz):
            prow[zz] = pk[zz].T

    def plane_col(zz, r, n):
        return prow[zz, r, n : n + 1]

    def plane_values(blk):
        for i in range(pn.slots):
            project_slot(i, blk)

            def scale(row, zz, r):
                v = big[pl.ds(row, C), :]
                v = (v - plane_col(zz, r, 8 + base(blk, i))) * plane_col(zz, r, base(blk, i))
                pr[i, blk, pl.ds(row, C), :] = v.astype(BF16)
                v = v * plane_col(zz, r, 16 + base(blk, i))
                if i == 0:
                    v = v + plane_col(zz, r, 24 + blk)
                else:
                    v = v + qpart[blk, pl.ds(row, C), :].astype(F32)
                qpart[blk, pl.ds(row, C), :] = v.astype(BF16)

            at_slot(i, lambda: plane_rows(scale))

    def q_comb(blk, way, dist):
        first = 0 if way > 0 or nz <= 4 else nz - 3
        return qcomb.at[blk, first + dist - 2], pn.s_q[blk] + 2 * nz + (0 if way > 0 else nz) + dist

    def q_copy(blk, zc, zz):
        way, dist = (1, zz - zc) if zz > zc else (-1, zc - zz)
        source = qpart.at[blk, zz * C : (zz + 1) * C]
        i_send = pn.s_q[blk] + nz + zz
        if dist <= 2:
            return rcopy(source, qrecv.at[blk, zc], i_send, pn.s_q[blk] + zc, chip(zz, q))
        target, i = q_comb(blk, way, dist - 1)
        return rcopy(source, target, i_send, i, chip(zc + way, q))

    def q_sends(blk, zc, late):
        for zz in sorted(range(nz), key=lambda zz: -abs(zz - zc)):
            way, dist = (1, zz - zc) if zz > zc else (-1, zc - zz)
            after_other = dist >= 2 and 0 <= zc - way < nz and bool(pn.srcs[zc - way])
            if dist == 0 or after_other != late:
                continue
            if late:
                v, i = q_comb(blk, way, dist)
                rcopy(v, v, i, i, {"ch": sib}).wait_recv()
                rows = slice(zz * C, (zz + 1) * C)
                qpart[blk, rows, :] = (qpart[blk, rows, :].astype(F32) + v[...].astype(F32)).astype(BF16)
            q_copy(blk, zc, zz).start()

    def q_send(blk):
        def send(zc):
            q_sends(blk, zc, False)
            qrecv[blk, zc] = qpart[blk, zc * C : (zc + 1) * C, :]

        at_chip(send)

    def q_late(blk):
        at_chip(lambda zc: q_sends(blk, zc, True))

    def q_finish(blk):
        for zc in range(nz):
            if pn.srcs[zc]:

                @pl.when((z != zc) & (z <= zc + 2) & (z >= zc - 2))
                def _():
                    v = qrecv.at[blk, zc]
                    i = pn.s_q[blk] + zc
                    rcopy(v, v, i, i, {"ch": sib}).wait_recv()

    for zc in range(nz):
        if pn.srcs[zc]:

            @pl.when((z > zc + 2) | (z < zc - 2))
            def _():
                for blk in (0, 1):
                    qrecv[blk, zc] = jnp.zeros((C, T), BF16)

    def q_sum(blk, r, v):
        for zc in range(nz):
            if pn.srcs[zc]:
                v = v + qrecv[blk, zc, r, :].astype(F32)
        return v

    @pl.when(z == nz - 1)
    def _():
        r_hops(0, -1, lambda cp: cp.start())

    ld_w0.wait()
    ld_w0l.wait()
    ld_w0u.wait()
    conv(w0, src[HEAD : HEAD + PRE, :], 0, resid)
    conv_sums(0)
    sum_start(0, 2, jnp.broadcast_to(length.astype(F32), (1, LANES)))

    @pl.when(z < nz - 1)
    def _():
        r_hops(0, -1, lambda cp: cp.start())

    prm_copies(-1, lambda cp: cp.start())
    for zc, qq, row, n in pn.bound:

        @pl.when((z == zc) & (q == qq))
        def _():
            bound_hop(row, n).wait_recv()
            bound_sib(row, n).start()

    total = sum_finish(0)
    count = jnp.broadcast_to(total[2:3, 0:1], (1, LANES))
    av, rsd, sc, off = norm_rows(total[0:1], total[1:2], count, prm[0, 0:1], prm[1, 0:1])
    columns(0, [sc, off, av, rsd])

    def activate(p, y_index, out):
        def body(r):
            v = ys[y_index, r, :] * kcol[p, r, 0:1] + kcol[p, r, 1:2]
            out[at_row(c * C, r), :] = (v * squash(v) * valid_rb).astype(BF16)

        blocks(body)

    activate(0, 0, x1)
    gx1 = Gather(pn.s_x[0], x1, C)
    gx1.start()
    r_arrive(0)
    for zc, qq, row, n in pn.bound:

        @pl.when((z == zc) & (q != qq))
        def _():
            bound_sib(row, n).wait_recv()

    sized(sib, lambda n: own_rows(sib, n).wait_recv())
    gx1.arrive()
    r_finish(0)
    plane_first(0)
    plane_start(0, 2, 64)
    gx1.end()
    ld_w1.wait()
    conv(w1, x1[...], 1)

    def first_sums(r):
        y = ys[1, r, :] * valid_rb
        lo, up = resid[r, :], resid[at_row(C, r), :]
        pack_sums(r, [y, y * y, lo, lo * lo, up, up * up])

    blocks(first_sums)
    sum_start(1, 6)
    r_hops(1, -1, lambda cp: cp.start())
    others(prm_arrive)
    plane_total = plane_finish(0)
    at_chip(lambda zc: plane_norms(zc, plane_total, 0))
    plane_values(0)
    q_send(0)
    total = sum_finish(1)
    r_arrive(1)
    slice_start(0)
    q_late(0)
    l1 = norm_rows(total[0:1], total[1:2], count, prm[0, 1:2], prm[1, 1:2])
    l8 = norm_rows(total[2:3], total[3:4], count, prm[0, 10:11], prm[1, 10:11])
    u8 = norm_rows(total[4:5], total[5:6], count, prm[2, 10:11], prm[3, 10:11])
    columns(1, [l1[2], l8[2], l1[0], l8[0], l1[3] + l8[3]])
    q_finish(0)

    def lower_out(r):
        v = ys[1, r, :] * kcol[1, r, 0:1] + kcol[1, r, 4:5] + resid[r, :] * kcol[1, r, 1:2]
        v = q_sum(0, r, v)
        hold[1, r, :] = v
        x2[at_row(c * C, r), :] = (v * squash(v) * valid_rb).astype(BF16)

    blocks(lower_out)
    gx2 = Gather(pn.s_x[1], x2, C)
    gx2.start()
    gx2.arrive()
    r_finish(1)
    plane_first(1)
    plane_start(3, 2, 64)
    gx2.end()
    ld_w2.wait()
    ld_w2m.wait()
    conv(w2, x2[...], 2, rmid)

    def mid_sums(r):
        y = ys[2, r, :] * valid_rb
        v = rmid[r, :]
        pack_sums(r, [y, y * y, v, v * v])

    blocks(mid_sums)
    sum_start(2, 4)
    total = sum_finish(2)
    u2 = norm_rows(total[0:1], total[1:2], count, prm[2, 0:1], prm[3, 0:1])
    mid = norm_rows(total[2:3], total[3:4], count, prm[2, 11:12], prm[3, 11:12])
    columns(2, [u2[2], u2[3], u2[0], u2[1]])
    activate(2, 2, x3)
    gx3 = Gather(pn.s_x[2], x3, C)
    gx3.start()
    plane_total = plane_finish(3)
    at_chip(lambda zc: plane_norms(zc, plane_total, 1))
    plane_values(1)
    slice_start(2)
    slice_start(1)
    gx3.arrive()
    q_send(1)
    q_late(1)
    gx3.end()
    ld_w3.wait()
    conv(w3, x3[...], 3)
    conv_sums(3)
    sum_start(3, 2)
    q_finish(1)
    total = sum_finish(3)
    u3 = norm_rows(total[0:1], total[1:2], count, prm[2, 1:2], prm[3, 1:2])
    columns(3, [u3[2], u8[2], mid[2], u3[0], u8[0], mid[0], u3[3] + u8[3] + mid[3]])

    def value_back(v, gradient):
        s = squash(v)
        return gradient * valid_rb * s * (1.0 + v * (1.0 - s))

    def upper_out(r):
        up = resid[at_row(C, r), :]
        v = ys[3, r, :] * kcol[3, r, 0:1] + kcol[3, r, 6:7] + up * kcol[3, r, 1:2] + rmid[r, :] * kcol[3, r, 2:3]
        v = q_sum(1, r, v)
        final_ref[r, :] = (v * squash(v) * valid_rb).astype(BF16)
        dv = value_back(v, cot_ref[r, :].astype(F32))
        hold[2, r, :] = dv
        dvx[1, at_row(z * C, r), :] = dv.astype(BF16)
        parts = [dv]
        for n, x in enumerate((ys[3, r, :], up, rmid[r, :])):
            parts.append(dv * (x - kcol[3, r, 3 + n : 4 + n]))
        pack_sums(r, parts)

    blocks(upper_out)

    def dv_copy(blk, zz):
        v = dvx.at[blk, pl.ds(mult(z * C), C)]
        return rcopy(v, v, pn.s_dv + blk * nz + zz, pn.s_dv + blk * nz + z, chip(zz, q))

    def dv_copies(blk, act):
        for zz in range(nz):
            if pn.srcs[zz]:

                @pl.when(z != zz)
                def _():
                    act(dv_copy(blk, zz))

    def plane_back(blk, p):
        def wait(zc):
            for zf in range(nz):
                if zf != zc:
                    v = dvx.at[blk, zf * C : (zf + 1) * C]
                    i = pn.s_dv + blk * nz + zf
                    rcopy(v, v, i, i, {"ch": sib}).wait_recv()

        at_chip(wait)
        counts = sorted({len(x) for x in pn.srcs} - {0})
        for many in counts:

            def parts(row):
                dv = dvx[blk, pl.ds(row, C), :].astype(F32)
                found = [dv * pr[i, blk, pl.ds(row, C), :].astype(F32) for i in range(many)]
                return [dv] + found + [None] * (3 - many)

            chips = [z == zc for zc in range(nz) if len(pn.srcs[zc]) == many]
            pl.when(functools.reduce(jnp.logical_or, chips))(lambda: plane_sums(parts, 0, 32))
        plane_start(p, 4, 32)

    def gain_copy(blk, zz):
        i = pn.s_gain + blk * nz
        return rcopy(gsend.at[blk, zz], grecv.at[blk, z], i + zz, i + z, chip(zz, q))

    def plane_coefficients(blk, total):
        def run(zc):
            dv_sum = total[:, 0]
            for i in range(len(pn.srcs[zc])):
                g = total[:, 4 * (i + 1)]
                gsend[blk, :, i, :] = g
                p_sc = pk[:, 48 + base(blk, i), :]
                pk[:, 32 + base(blk, i), :] = p_sc * dv_sum / count
                pk[:, 40 + base(blk, i), :] = p_sc * g / count
            for zz in range(nz):
                prow[zz] = pk[zz].T
                if zz != zc:
                    gain_copy(blk, zz).start()
            grecv[blk, zc] = gsend[blk, zc]

        at_chip(run)

    def plane_dr(blk):
        def run(zc):
            def body(row, zz, r):
                dv = dvx[blk, pl.ds(row, C), :].astype(F32)
                for i in range(len(pn.srcs[zc])):
                    n = base(blk, i)
                    v = pr[i, blk, pl.ds(row, C), :].astype(F32)
                    v = plane_col(zz, r, 48 + n) * dv - (
                        plane_col(zz, r, 32 + n) + plane_col(zz, r, 40 + n) * v
                    )
                    drp[i, blk, pl.ds(row, C), :] = (v * valid).astype(BF16)

            plane_rows(body)

        at_chip(run)

    def unit_copy(blk, u):
        i = pn.s_d1[blk]
        target = d1recv.at[blk, b, u // nb]
        return rcopy(d1send.at[u], target, i + u, i + b * pn.nu + u, {"batch": u % nb})

    def unit_grads(blk):
        def run(zc):
            for i, s in enumerate(pn.srcs[zc]):
                at, width = pn.pieces[s]
                grad = dot_last(drp[i, blk], src[at : at + width, :])
                first = (at - pn.lo[zc]) // LANES
                for n in range(width // LANES):
                    d1send[first + n] = grad[:, n * LANES : (n + 1) * LANES].astype(BF16)

        at_chip(run)

    def unit_send(blk):
        def run(zc):
            for u in range(pn.width[zc] // LANES):

                @pl.when(b != u % nb)
                def _():
                    unit_copy(blk, u).start()

        at_chip(run)

    def unit_drain(blk):
        def run(zc):
            for u in range(pn.width[zc] // LANES):

                @pl.when(b != u % nb)
                def _():
                    unit_copy(blk, u).wait_send()

        at_chip(run)

    def unit_blocks(blk, zc, u):
        col = pn.lo[zc] + u * LANES
        return list(range(col // pn.share(blk), (col + LANES - 1) // pn.share(blk) + 1))

    def unit_number(zc, u):
        return [n for n, (a, e, _) in enumerate(pn.units) if (a, e) == (zc, u)][0]

    def result_copies(blk, zc, u, act_far, act_own):
        k = u // nb
        number = unit_number(zc, u)
        for zz in range(nz):
            for jj, j in enumerate(unit_blocks(blk, zc, u)):
                source = d2send.at[blk, k, zz * C : (zz + 1) * C]
                cp = rcopy(
                    source,
                    d2recv.at[blk, number],
                    pn.s_d2[blk] + (k * nz + zz) * 2 + jj,
                    pn.s_d2[blk] + number,
                    {"batch": j, "ch": zz * 2 + q},
                )
                if zz == zc and j == u % nb:
                    if act_own is not None:
                        act_own(number, k, zz)
                else:
                    act_far(cp)

    def unit_finish(blk):
        def run(zc):
            for u in range(pn.width[zc] // LANES):

                @pl.when(b == u % nb)
                def _():
                    total = d1send[u].astype(F32)
                    for d in range(1, nb):
                        bb = lax.rem(b + d, nb)
                        v = d1recv.at[blk, bb, u // nb]
                        i = pn.s_d1[blk] + bb * pn.nu + u
                        rcopy(v, v, i, i, {"ch": sib}).wait_recv()
                        total = total + d1recv[blk, bb, u // nb].astype(F32)
                    d2send[blk, u // nb] = total.astype(BF16)

                    def keep(number, k, zz):
                        d2recv[blk, number] = d2send[blk, k, zz * C : (zz + 1) * C, :]

                    result_copies(blk, zc, u, lambda cp: cp.start(), keep)

        at_chip(run)

    def result_drain(blk):
        def run(zc):
            for u in range(pn.width[zc] // LANES):

                @pl.when(b == u % nb)
                def _():
                    result_copies(blk, zc, u, lambda cp: cp.wait_send(), None)

        at_chip(run)

    def result_finish(blk, out):
        share = pn.share(blk)
        for j in range(nb):

            @pl.when(b == j)
            def _():
                for number, (zc, u, ub) in enumerate(pn.units):
                    col = pn.lo[zc] + u * LANES
                    lo_c, hi_c = max(col, j * share), min(col + LANES, (j + 1) * share)
                    if lo_c >= hi_c:
                        continue
                    v = d2recv.at[blk, number]
                    i = pn.s_d2[blk] + number
                    arrived = rcopy(v, v, i, i, {"ch": sib})
                    if ub == j:

                        @pl.when(z != zc)
                        def _():
                            arrived.wait_recv()

                    else:
                        arrived.wait_recv()
                    out[:, lo_c - j * share : hi_c - j * share] = d2recv[blk, number][
                        :, lo_c - col : hi_c - col
                    ].astype(F32)

    sum_start(4, 4)
    dv_copies(1, lambda cp: cp.start())
    total = sum_finish(4)
    slice_start(3)
    upper_q = total[0:1]
    upper_rsd = jnp.concatenate([u3[1], u8[1], mid[1]], axis=0)
    upper_sc = jnp.concatenate([u3[2], u8[2], mid[2]], axis=0)
    upper_g = total[1:4] * upper_rsd
    usg_ref[1:12, :] = jnp.broadcast_to(upper_q[:, 0:C], (11, C))
    ugg_ref[1:2, :] = upper_g[0:1, 0:C]
    ugg_ref[10:12, :] = upper_g[1:3, 0:C]
    columns(4, [upper_sc * upper_q / count, upper_sc * upper_rsd * upper_g / count])

    def grad_rows(gradient, values, sc_col, av_col, a_col, b_col):
        return ((sc_col * gradient - (a_col + b_col * (values - av_col))) * valid_rb).astype(BF16)

    own_lanes = pl.ds(mult(b * T, LANES), T)

    def upper_grad(r, values, n):
        return grad_rows(
            hold[2, r, :],
            values,
            kcol[3, r, n : n + 1],
            kcol[3, r, 3 + n : 4 + n],
            kcol[4, r, n : n + 1],
            kcol[4, r, 3 + n : 4 + n],
        )

    def upper_dy(r):
        dyg[3, r, own_lanes] = upper_grad(r, ys[3, r, :], 0)

    blocks(upper_dy)
    gx1.drain()
    for _, cp in slice_copies(1):
        cp.wait_send()
    shift_all(3)
    sc0 = Scatter(0)
    sc0.compute(w3, 0)
    sc0.send()
    dy_start(3)
    sc0.send_dist(2)
    slice_arrive(0)
    slice_arrive(1)
    slice_arrive(2)

    def upper_dr(r):
        dr8[at_row(C, r), :] = upper_grad(r, resid[at_row(C, r), :], 1)
        dbuf[at_row(K * C, r), :] = upper_grad(r, rmid[r, :], 2)

    blocks(upper_dr)

    def dense_stage(n, first_col, value):
        share = pn.share(n)
        end = first_col + value.shape[1]
        for k, bb in enumerate(pn.dense_owners(n)):
            lo_c, hi_c = max(first_col, bb * share), min(end, (bb + 1) * share)
            if lo_c < hi_c:
                drs[n, k, :, lo_c - bb * share : hi_c - bb * share] = value[
                    :, lo_c - first_col : hi_c - first_col
                ].astype(BF16)

    def dense_cut(n, bb):
        first = max(HEAD - bb * pn.share(n), 0)
        return first, first // LANES * LANES

    def dense_copy(n, k, bb):
        tile = dense_cut(n, bb)[1]
        i = pn.s_dr[n]
        return rcopy(drs.at[n, k, :, tile:], drr.at[n, b, :, tile:], i + bb, i + b, {"batch": bb})

    def dense_copies(n, act):
        for k, bb in enumerate(pn.dense_owners(n)):

            @pl.when(b != bb)
            def _():
                act(dense_copy(n, k, bb))

    def dense_finish(n, out):
        share = pn.share(n)
        for k, bb in enumerate(pn.dense_owners(n)):

            @pl.when(b == bb)
            def _():
                first, tile = dense_cut(n, bb)
                total = drs[n, k, :, first:share].astype(F32)
                for d in range(1, nb):
                    other_b = lax.rem(b + d, nb)
                    v = drr.at[n, other_b, :, tile:]
                    i = pn.s_dr[n] + other_b
                    rcopy(v, v, i, i, {"ch": sib}).wait_recv()
                    total = total + drr[n, other_b, :, first:share].astype(F32)
                out[:, first:share] = total

    dense_stage(1, HEAD, dot_last(dr8[C : 2 * C, :], src[HEAD : HEAD + PRE, :]))
    dense_stage(1, HEAD + PRE, dot_last(dbuf[K * C : (K + 1) * C, :], x2[...]))
    plane_back(1, 1)
    sc0.end()
    slice_arrive(3)

    def inner_back(p, y_index):
        def body(r):
            y = ys[y_index, r, :]
            dz = value_back(y * kcol[p, r, 0:1] + kcol[p, r, 1:2], hold[0, r, :])
            hold[3, r, :] = dz
            pack_sums(r, [dz, dz * (y - kcol[p, r, 2:3])])

        blocks(body)

    def inner_dy(p, kept, y_index):
        def body(r):
            dyg[y_index, r, own_lanes] = grad_rows(
                hold[3, r, :], ys[y_index, r, :], kcol[kept, r, 0:1], kcol[kept, r, 2:3], kcol[p, r, 0:1], kcol[p, r, 1:2]
            )

        blocks(body)

    inner_back(2, 2)
    sum_start(5, 2)
    plane_total = plane_finish(1)
    plane_coefficients(1, plane_total)
    total = sum_finish(5)
    dense_copies(1, lambda cp: cp.start())
    inner_q, inner_g = total[0:1], total[1:2] * u2[1]
    usg_ref[0:1, :] = inner_q[:, 0:C]
    ugg_ref[0:1, :] = inner_g[:, 0:C]
    columns(5, [u2[2] * inner_q / count, u2[2] * u2[1] * inner_g / count])
    inner_dy(5, 2, 2)
    shift_all(2)
    sc1 = Scatter(1)
    sc1.compute(w2, 1)
    sc1.send()
    dy_start(2)
    plane_dr(1)
    sc1.send_dist(2)
    unit_grads(1)
    weight_grad(3, g23_hbm, K * C)
    sc1.end()

    def lower_back(r):
        v = hold[1, r, :]
        dv = value_back(v, hold[0, r, :])
        hold[2, r, :] = dv
        dvx[0, at_row(z * C, r), :] = dv.astype(BF16)
        pack_sums(r, [dv, dv * (ys[1, r, :] - kcol[1, r, 2:3]), dv * (resid[r, :] - kcol[1, r, 3:4])])

    blocks(lower_back)
    sum_start(6, 3)
    dv_copies(0, lambda cp: cp.start())
    total = sum_finish(6)
    unit_send(1)
    lower_q = total[0:1]
    lower_rsd = jnp.concatenate([l1[1], l8[1]], axis=0)
    lower_sc = jnp.concatenate([l1[2], l8[2]], axis=0)
    lower_g = total[1:3] * lower_rsd
    lsg_ref[1:11, :] = jnp.broadcast_to(lower_q[:, 0:C], (10, C))
    lgg_ref[1:2, :] = lower_g[0:1, 0:C]
    lgg_ref[10:11, :] = lower_g[1:2, 0:C]
    columns(6, [lower_sc * lower_q / count, lower_sc * lower_rsd * lower_g / count])

    def lower_grad(r, values, n):
        return grad_rows(
            hold[2, r, :],
            values,
            kcol[1, r, n : n + 1],
            kcol[1, r, 2 + n : 3 + n],
            kcol[6, r, n : n + 1],
            kcol[6, r, 2 + n : 3 + n],
        )

    def lower_dy(r):
        dyg[1, r, own_lanes] = lower_grad(r, ys[1, r, :], 0)

    blocks(lower_dy)
    shift_all(1)
    sc2 = Scatter(2)
    sc2.compute(w1, 0)
    sc2.send()
    dy_start(1)
    sc2.send_dist(2)

    def lower_dr(r):
        dr8[r, :] = lower_grad(r, resid[r, :], 1)

    blocks(lower_dr)
    dense_stage(0, HEAD, dot_last(dr8[0:C, :], src[HEAD : HEAD + PRE, :]))
    dense_copies(0, lambda cp: cp.start())
    plane_back(0, 2)
    weight_grad(2, g23_hbm, 0)
    unit_drain(1)
    unit_finish(1)
    sc2.end()

    inner_back(0, 0)
    sum_start(7, 2)
    plane_total = plane_finish(2)
    plane_coefficients(0, plane_total)
    plane_dr(0)
    unit_grads(0)
    total = sum_finish(7)
    unit_send(0)
    inner_q, inner_g = total[0:1], total[1:2] * rsd
    lsg_ref[0:1, :] = inner_q[:, 0:C]
    lgg_ref[0:1, :] = inner_g[:, 0:C]
    columns(7, [sc * inner_q / count, sc * rsd * inner_g / count])
    inner_dy(7, 0, 0)
    shift_all(0)
    dbuf[K * C : (K + 2) * C, :] = dr8[...]
    count_late = len(pn.late)
    gx3.drain()
    for _, cp in slice_copies(3):
        cp.wait_send()

    def tail_rows(n):
        return x3.at[pn.late[n][2] - HEAD : pn.late[n][2] - HEAD + pn.step]

    def tail_sib(n):
        return rcopy(tail_rows(n), tailsib.at[n], pn.s_tail + n, pn.s_tail + n, {"ch": sib})

    def tail_partials(first, last):
        for n in range(count_late):
            at = pn.late[n][2] - HEAD
            there = slice(at, at + pn.step)
            if first < at + pn.step <= last:

                @pl.when(q != pn.late[n][1])
                def _():
                    x3[there, :] = big[there, :].astype(BF16)
                    tail_sib(n).start()

    split = (PRE // 2 + LANES - 1) // LANES * LANES
    back_rows(w0, 2, slice(0, split), slice(0, split))
    tail_partials(0, split)
    back_rows(w0, 2, slice(split, PRE), slice(split, PRE))
    tail_partials(split, PRE)
    dy_start(0)

    def dp_sib(lc, n, k):
        v = dpo.at[lc : lc + n]
        i = pn.s_dp + 1 + k
        return rcopy(v, dpsib.at[lc : lc + n], i, i, {"ch": sib})

    def dp_bound(lc, n):
        return rcopy(dpo.at[lc : lc + n], dpbnd.at[0:n], pn.s_dp, pn.s_dp, below)

    def dp_compute(zc):
        for i, s in enumerate(pn.srcs[zc]):
            at, width = pn.pieces[s]
            lc = at - pn.lo[zc]
            r = rp[:, :, lc : lc + width].reshape(2 * rows_all, width)
            grad = dot_first(r, drp[i].reshape(2 * rows_all, T))
            dpo[lc : lc + width, :] = grad.astype(BF16)
        for k, (owner, row, n) in enumerate(pn.final[zc]):

            @pl.when(q != owner % 2)
            def _():
                dp_sib(row - pn.lo[zc], n, k).start()

    def dp_add(zc):
        for k, (owner, row, n) in enumerate(pn.final[zc]):
            lc = row - pn.lo[zc]

            @pl.when(q == owner % 2)
            def _():
                dp_sib(lc, n, k).wait_recv()
                total = dpo[lc : lc + n, :].astype(F32) + dpsib[lc : lc + n, :].astype(F32)
                if owner // 2 == zc:
                    at = WIDE + row - owner * E
                    big[at : at + n, :] = total * valid
                else:
                    dpo[lc : lc + n, :] = total.astype(BF16)
                    dp_bound(lc, n).start()

    def dp_drain(zc):
        for k, (owner, row, n) in enumerate(pn.final[zc]):
            lc = row - pn.lo[zc]

            @pl.when(q != owner % 2)
            def _():
                dp_sib(lc, n, k).wait_send()

            if owner // 2 != zc:

                @pl.when(q == owner % 2)
                def _():
                    dp_bound(lc, n).wait_send()

    def tail_hop(n, way, device):
        i = pn.s_tail + (1 + way) * count_late + n
        return rcopy(tail_rows(n), tailrecv.at[way, n], i, i, device)

    before, after = [], [True] * count_late
    for n in range(count_late):
        same = [m for m in range(n) if pn.late[m][:2] == pn.late[n][:2]]
        before.append(same[-pn.flight] if len(same) >= pn.flight else None)
        if len(same) >= pn.flight:
            after[same[-pn.flight]] = False

    def tail_give(n):
        i = pn.s_tail + 3 * count_late + n
        return rcopy(tail_rows(n), tailfin.at[given.index(n)], i, i, {"ch": sib})

    given = [n for n in range(count_late) if pn.late[n][3]]

    def chain():
        for n in range(count_late):
            zc, qc, row, moved = pn.late[n]
            there = slice(row - HEAD, row - HEAD + pn.step)

            @pl.when(q == qc)
            def _():
                tail_sib(n).wait_recv()
                big[there, :] += tailsib[n].astype(F32)
                if zc > 0:

                    @pl.when((z > 0) & (z <= zc))
                    def _():
                        tail_hop(n, 0, above).wait_recv()
                        big[there, :] += tailrecv[0, n].astype(F32)

                if zc < nz - 1:

                    @pl.when((z < nz - 1) & (z >= zc))
                    def _():
                        tail_hop(n, 1, below).wait_recv()
                        big[there, :] += tailrecv[1, n].astype(F32)

                @pl.when(z < zc)
                def _():
                    x3[there, :] = big[there, :].astype(BF16)
                    if before[n] is not None:
                        tail_hop(before[n], 0, above).wait_send()
                    tail_hop(n, 0, above).start()

                if zc < nz - 1:

                    @pl.when(z > zc)
                    def _():
                        x3[there, :] = big[there, :].astype(BF16)
                        if before[n] is not None:
                            tail_hop(before[n], 1, below).wait_send()
                        tail_hop(n, 1, below).start()

                @pl.when(z == zc)
                def _():
                    if moved:
                        x3[there, :] = big[there, :].astype(BF16)
                        tail_give(n).start()
                    else:
                        big[WIDE + row % E : WIDE + row % E + pn.step, :] = big[there, :] * valid

    place = z * 4 // nz

    def phase(i, carry):
        pl.when(i == place)(chain)

        @pl.when(i == 0)
        def _():
            at_chip(dp_compute)
            at_chip(dp_add)

        @pl.when(i == 1)
        def _():
            unit_finish(0)
            weight_grad(1, g1_hbm, 0)

        @pl.when(i == 2)
        def _():
            weight_grad(0, g0_hbm, 0)

        return carry

    lax.fori_loop(0, 4, phase, 0)
    for n in given:
        zc, qc, row, _ = pn.late[n]

        @pl.when((z == zc) & (q != qc))
        def _():
            tail_give(n).wait_recv()
            big[WIDE + row % E : WIDE + row % E + pn.step, :] = tailfin[given.index(n)].astype(F32) * valid

    for zc, qq, row, n in pn.bound:

        @pl.when((z == zc - 1) & (q == qq))
        def _():
            dp_v = dpbnd.at[0:n]
            rcopy(dp_v, dp_v, pn.s_dp, pn.s_dp, above).wait_recv()
            at = WIDE + row % E
            big[at : at + n, :] = dpbnd[0:n, :].astype(F32) * valid

    egrad_copy = pltpu.make_async_copy(big.at[WIDE : WIDE + E], egrad_hbm, osem.at[4])
    egrad_copy.start()
    result_finish(1, rug_ref)
    dense_finish(1, rug_ref)
    for blk, ref in ((0, lgg_ref), (1, ugg_ref)):
        for zc in range(nz):
            if pn.srcs[zc]:
                gain_v = grecv.at[blk, zc]

                @pl.when(z != zc)
                def _():
                    i = pn.s_gain + blk * nz + zc
                    rcopy(gain_v, gain_v, i, i, {"ch": sib}).wait_recv()

                for i, s in enumerate(pn.srcs[zc]):
                    ref[2 + s : 3 + s, :] = grecv[blk, zc, i : i + 1, 0:C]
    dense_finish(0, rlg_ref)
    result_finish(0, rlg_ref)

    out_copy().wait()
    egrad_copy.wait()
    entry_drain()
    sized(c, lambda n: own_rows(c, n).wait_send())
    for zc, qq, row, n in pn.bound:

        @pl.when((z == zc - 1) & (q == qq))
        def _():
            bound_hop(row, n).wait_send()

        @pl.when((z == zc) & (q == qq))
        def _():
            bound_sib(row, n).wait_send()

    for blk in (0, 1):
        r_hops(blk, 1, lambda cp: cp.wait_send())
        r_hops(blk, -1, lambda cp: cp.wait_send())
        r_passes(blk, lambda cp: cp.wait_send())
    for way in (1, -1):
        prm_copies(way, lambda cp: cp.wait_send())

    def q_drain(zc):
        for blk in (0, 1):
            for zz in range(nz):
                if zz != zc:
                    q_copy(blk, zc, zz).wait_send()
                    gain_copy(blk, zz).wait_send()

    at_chip(q_drain)
    at_chip(dp_drain)
    for blk in (0, 1):
        dv_copies(blk, lambda cp: cp.wait_send())
        dense_copies(blk, lambda cp: cp.wait_send())
        result_drain(blk)
    unit_drain(0)
    gx2.drain()
    for p in range(8):
        for _, cp in sum_copies(p):
            cp.wait_send()
    for p in range(4):
        for _, cp in plane_copies(p):
            cp.wait_send()
    for j in range(4):
        slice_pass(j, lambda bb, cp: cp.wait_send())
        if j not in (1, 3):
            for _, cp in slice_copies(j):
                cp.wait_send()
        for _, cp in dy_copies(j):
            cp.wait_send()
    for n in range(count_late):
        zc, qc, _, moved = pn.late[n]

        @pl.when(q != qc)
        def _():
            tail_sib(n).wait_send()

        if moved:

            @pl.when((z == zc) & (q == qc))
            def _():
                tail_give(n).wait_send()

        if after[n]:

            @pl.when((q == qc) & (z < zc))
            def _():
                tail_hop(n, 0, above).wait_send()

        if after[n] and zc < nz - 1:

            @pl.when((q == qc) & (z > zc))
            def _():
                tail_hop(n, 1, below).wait_send()


def per_device(
    nb,
    nc,
    earlier,
    lengths,
    lower_entry,
    lower_convs,
    upper_convs,
    lower_dense,
    upper_dense,
    lower_gain,
    lower_shift,
    upper_gain,
    upper_shift,
    cotangent,
):
    _, own, frames = earlier.shape
    taps, cw, pre = lower_entry.shape
    pn = Plan(nb, nc, own, frames, taps, cw, pre)
    T, K, C, E, WIDE, nz = frames, taps, cw, own, pn.wide, pn.nz
    late = len(pn.late)
    share = ((pn.all + WIDE) // nb + LANES - 1) // LANES * LANES
    w0p, wp = up16(pn.iw0), up16(pn.iw)
    staged = 4 if (w0p != pn.iw0 or wp != pn.iw) else 1
    vmem, any_ = pl.BlockSpec(memory_space=pltpu.VMEM), pl.BlockSpec(memory_space=pl.ANY)
    smem = pl.BlockSpec(memory_space=pltpu.SMEM)
    V = pltpu.VMEM
    scratch = [
        V(((K + 2) * C, pre), BF16),
        V((K * C, WIDE), BF16),
        V(((K + 1) * C, WIDE), BF16),
        V((K * C, WIDE), BF16),
        V((2, nz * C, pn.pw), BF16),
        V((2, nz, pn.kr, C, LANES), BF16),
        V((pn.all, T), BF16),
        V((WIDE, T), BF16),
        V((WIDE, T), BF16),
        V((WIDE, T), BF16),
        V((WIDE + E, T), F32),
        V((2 * C, T), F32),
        V((C, T), F32),
        V((4, C, T), F32),
        V(((K + 2) * C, T), BF16),
        V((pn.slots, 2, nz * C, T), BF16),
        V((pn.slots, 2, nz * C, T), BF16),
        V((2 * C, T), BF16),
        V((2, nz * C, T), BF16),
        V((2, nz, C, T), BF16),
        V((2, max(nz - 3, 1) * (2 if nz > 4 else 1), C, T), BF16),
        V((2, nz * C, T), BF16),
        V((2, nz, 8, LANES), F32),
        V((2, nz, 8, LANES), F32),
        V((max(pn.pw, E), T), BF16),
        V((pn.pw, T), BF16),
        V((max([n for _, _, _, n in pn.bound] + [16]), T), BF16),
        V((pn.nu, nz * C, LANES), BF16),
        V((2, nb, pn.ku, nz * C, LANES), BF16),
        V((2, pn.ku, nz * C, LANES), BF16),
        V((2, len(pn.units), C, LANES), BF16),
        V((3, nz, C, T), BF16),
        V((3, 4, C, T), BF16),
        V((3, max(nz - 3, 1) * (2 if nz > 4 else 1), C, T), BF16),
        V((late, pn.step, T), BF16),
        V((1 + (pn.late[0][0] < nz - 1), late, pn.step, T), BF16),
        V((max(sum(x[3] for x in pn.late), 1), pn.step, T), BF16),
        V((4, C, nb * T), BF16),
        V((w0p, nb * T), BF16),
        V((3, wp, nb * T), BF16),
        V((4, nb, max(w0p, wp), T) if staged == 4 else (1, 1, 16, T), BF16),
        V((2, len(pn.dense_owners(1)), C, share), BF16),
        V((2, nb, C, share), BF16),
        V((8, nb, 8, LANES), F32),
        V((LANES, LANES), F32),
        V((LANES, LANES), F32),
        V((8, LANES, LANES), F32),
        V((4, nb, nz, 16, LANES), F32),
        V((nz, LANES, LANES), F32),
        V((nz, LANES, LANES), F32),
        V((nz, LANES, LANES), F32),
        V((4, 16, LANES), F32),
        V((nz, 4, 8, LANES), F32),
        V((4, C, T), F32),
        V((K * C, pn.iw), F32),
        pltpu.SemaphoreType.DMA((10 + 2 * nz * pn.kr,)),
        pltpu.SemaphoreType.DMA((5,)),
        pltpu.SemaphoreType.DMA((pn.sems,)),
        pltpu.SemaphoreType.DMA((pn.sems,)),
    ]
    shape = jax.ShapeDtypeStruct
    outs = pl.pallas_call(
        functools.partial(kernel, pn),
        out_shape=(
            shape((C, T), BF16),
            shape((E, T), F32),
            shape((K * C, pn.iw), F32),
            shape((K * C, pn.iw), F32),
            shape((2 * K * C, pn.iw), F32),
            shape((C, pn.all // nb), F32),
            shape((C, (pn.all + WIDE) // nb), F32),
            shape((11, C), F32),
            shape((11, C), F32),
            shape((12, C), F32),
            shape((12, C), F32),
        ),
        in_specs=[smem] + [any_] * 6 + [vmem] * 5,
        out_specs=(vmem, any_, any_, any_, any_, vmem, vmem, vmem, vmem, vmem, vmem),
        scratch_shapes=scratch,
        compiler_params=pltpu.CompilerParams(
            collective_id=0, has_side_effects=True, vmem_limit_bytes=64000 * 1024
        ),
    )(
        lengths,
        earlier.reshape(own, frames),
        lower_entry.reshape(K * C, pre),
        lower_convs.reshape(K * C, WIDE),
        upper_convs.reshape(2 * K * C, WIDE),
        lower_dense,
        upper_dense,
        lower_gain,
        lower_shift,
        upper_gain,
        upper_shift,
        cotangent.reshape(C, T),
    )
    final, egrad, g0, g1, g23, rlg, rug, lgg, lsg, ugg, usg = outs
    return (
        final.reshape(1, C, T),
        egrad.reshape(1, E, T),
        g0.reshape(K, C, pn.iw)[:, :, 0 : pn.iw0],
        g1.reshape(1, K, C, pn.iw),
        g23.reshape(2, K, C, pn.iw),
        rlg,
        rug,
        lgg,
        lsg,
        ugg,
        usg,
    )


def solution(mesh):
    placed = (
        P("batch", "ch", None),
        P("batch"),
        P(None, "ch", None),
        P(None, None, "ch", None),
        P(None, None, "ch", None),
        P("ch", None),
        P("ch", None),
        P(None, "ch"),
        P(None, "ch"),
        P(None, "ch"),
        P(None, "ch"),
        P("batch", "ch", None),
    )
    return jax.shard_map(
        functools.partial(per_device, mesh.shape["batch"], mesh.shape["ch"]),
        mesh=mesh,
        in_specs=placed,
        out_specs=(
            P("batch", "ch", None),
            P("batch", "ch", None),
            P(None, "ch", "batch"),
            P(None, None, "ch", "batch"),
            P(None, None, "ch", "batch"),
            P("ch", "batch"),
            P("ch", "batch"),
            P(None, "ch"),
            P(None, "ch"),
            P(None, "ch"),
            P(None, "ch"),
        ),
        check_vma=False,
    )
```
